32 devices in a mesh: dp: 4 (over z), fsdp: 8 (over y, x, core).
Axes of the slice: x: 2, y: 2, z: 4, core: 2. Of those that a mesh axis runs over, the one named last changes fastest.
Arguments:
- activations: bfloat16 [16384, 1024], P(('dp', 'fsdp')), may hold values from -6 to 6
- time_features: bfloat16 [64, 256], P(('dp', 'fsdp')), may hold values from -6 to 6
- lengths: int32 [32, 2], P(('dp', 'fsdp')), may hold values from 32 to 480, as said below
- attn_gain: bfloat16 [1024], P('fsdp'), may hold values from 0.099609375 to 1.8984375
- attn_shift: bfloat16 [1024], P('fsdp'), may hold values from -3 to 3
- qkv_weight: bfloat16 [1024, 3072], P('fsdp'), may hold values from -0.1875 to 0.1875
- qkv_bias: bfloat16 [3072], P('fsdp'), may hold values from -3 to 3
- out_weight: bfloat16 [1024, 1024], P('fsdp'), may hold values from -1.5 to 1.5
- out_bias: bfloat16 [1024], P('fsdp'), may hold values from -3 to 3
- mlp_gain: bfloat16 [1024], P('fsdp'), may hold values from 0.099609375 to 1.8984375
- mlp_shift: bfloat16 [1024], P('fsdp'), may hold values from -3 to 3
- up_weight: bfloat16 [1024, 4096], P('fsdp'), may hold values from -0.1875 to 0.1875
- up_bias: bfloat16 [4096], P('fsdp'), may hold values from -3 to 3
- down_weight: bfloat16 [4096, 1024], P('fsdp'), may hold values from -0.09375 to 0.09375
- down_bias: bfloat16 [1024], P('fsdp'), may hold values from -3 to 3
- time_weight: bfloat16 [256, 1024], P('fsdp'), may hold values from -0.375 to 0.375
- time_bias: bfloat16 [1024], P('fsdp'), may hold values from -3 to 3
- cotangent: bfloat16 [16384, 1024], P(('dp', 'fsdp')), may hold values from -12 to 12
Outputs:
- output: bfloat16 [16384, 1024], P(('dp', 'fsdp'))
- input_grad: bfloat16 [16384, 1024], P(('dp', 'fsdp'))
- attn_gain_grad: float32 [1024], P('fsdp')
- attn_shift_grad: float32 [1024], P('fsdp')
- qkv_weight_grad: float32 [1024, 3072], P('fsdp')
- qk_bias_grad: float32 [2048], P('fsdp')
- value_bias_grad: float32 [1024], P('fsdp')
- out_weight_grad: float32 [1024, 1024], P('fsdp')
- out_bias_grad: float32 [1024], P('fsdp')
- mlp_gain_grad: float32 [1024], P('fsdp')
- mlp_shift_grad: float32 [1024], P('fsdp')
- up_weight_grad: float32 [1024, 4096], P('fsdp')
- up_bias_grad: float32 [4096], P('fsdp')
- down_weight_grad: float32 [4096, 1024], P('fsdp')
- down_bias_grad: float32 [1024], P('fsdp')
- time_weight_grad: float32 [256, 1024], P('fsdp')
- time_bias_grad: float32 [1024], P('fsdp')
The draws below stay inside these ranges and needn't reach their ends.
Inputs may be any that keep to these rules, and one draw needn't show every extreme that they name: Each row holds the lengths of one device's sequences, packed in order from its first slot; the slots after them are padding. A row adds up to 256 or more and to 512 or less; some device's row adds up to 512.
All inputs are finite; a program needn't handle non-finite values.
Results may differ from the reference program's by a relative error of at most 0.017.
Values may be sent and summed in bfloat16 or wider, within the bound.
No kernel may reach another device: no remote copies, remote signals or barrier semaphores. Data moves between devices by JAX's collectives and lax.ppermute only.
A program may use at most 192 MiB of HBM per device.

```python
import jax
import jax.numpy as jnp
from jax import lax

D = 1024
H = 16
FF = 4096
TE = 256
TOK_DEV = 512
SEQ_DEV = 2
MIN_LEN = 32
TOKENS = 16384
SEQS = 64
N_DP = 4
N_FSDP = 8


def draw_lengths(key, part):
    key = jax.random.fold_in(key, 7)
    total_key, full_key, share_key = jax.random.split(key, 3)
    device_count = N_DP * N_FSDP
    totals = jax.random.randint(total_key, (device_count,), TOK_DEV // 2, TOK_DEV + 1)
    shares = jax.random.randint(share_key, (device_count, SEQ_DEV), 1, 17)
    spare_tokens = totals - SEQ_DEV * MIN_LEN
    extra_tokens = spare_tokens[:, None] * shares // jnp.sum(shares, axis=1, keepdims=True)
    base_rows = MIN_LEN + extra_tokens
    remainder = totals - jnp.sum(base_rows, axis=1)
    last_slot = (jnp.arange(SEQ_DEV) == SEQ_DEV - 1).astype(jnp.int32)
    length_rows = base_rows + remainder[:, None] * last_slot[None, :]
    full_row = jnp.where(jnp.arange(SEQ_DEV) == 0, TOK_DEV - (SEQ_DEV - 1) * MIN_LEN, MIN_LEN)
    full_device = jax.random.randint(full_key, (), 0, device_count)
    length_rows = jnp.where((jnp.arange(device_count) == full_device)[:, None], full_row[None, :], length_rows)
    return length_rows.astype(jnp.int32)


def strengthened(array, own_key, source, target, blocks, factor):
    def block_of(dim):
        return (jnp.arange(array.shape[dim]) // (array.shape[dim] // blocks)).reshape((-1,) + (1,) * (array.ndim - 1 - dim))

    one_side = jax.random.permutation(own_key, blocks)[block_of(target)]
    far = (block_of(target) + blocks // 2) % blocks
    return jnp.where((block_of(source) == one_side) | (block_of(source) == far), factor * array, array)


def level_of(own_key, extent, pieces, least, top_value):
    gain = 1.0
    for axis_at, blocks in pieces:
        steps = jax.random.uniform(jax.random.fold_in(jax.random.fold_in(own_key, 6), axis_at), (blocks,), jnp.float32, least / len(pieces), top_value / len(pieces))
        gain = gain * jnp.repeat(jnp.exp(steps), extent[axis_at] // blocks).reshape((-1,) + (1,) * (len(extent) - 1 - axis_at))
    return gain


def gaussian(stream_key, shape, width, reach, pieces=(), held_as=jnp.bfloat16):
    entries = jax.random.normal(stream_key, shape, jnp.float32) * width
    if len(pieces) > 0:
        entries = level_of(stream_key, shape, pieces, -0.22, 0.18) * entries
    return jnp.clip(entries, min=-reach, max=reach).astype(held_as)


def bell_draw_with(key, shape, spread, bound, shards, heavy, kind=jnp.bfloat16):
    values = spread * jax.random.normal(key, shape, jnp.float32)
    if shards:
        values = values * level_of(key, shape, shards, -0.22, 0.18)
    return jnp.clip(strengthened(values, jax.random.fold_in(key, 3), *heavy), -bound, bound).astype(kind)


def setup_inputs(seed: int = 0) -> dict:
    seeds = jax.random.split(jax.random.key(seed), 19)
    activations = gaussian(seeds[0], (TOKENS, D), 1.0, 6.0, ((0, 32),))
    time_features = gaussian(seeds[1], (SEQS, TE), 1.0, 6.0, ((0, 32),))
    lengths = draw_lengths(jax.random.fold_in(seeds[18], 71), 0)
    attn_gain = jnp.clip(1.0 + 0.18 * jax.random.normal(seeds[3], (D,), jnp.float32), 0.099609375, 1.8984375).astype(jnp.bfloat16)
    attn_shift = gaussian(seeds[4], (D,), 0.5, 3.0, ((0, 8),))
    qkv_weight = gaussian(seeds[5], (D, 3 * D), D ** -0.5, 0.1875, ((0, 8),))
    qkv_bias = gaussian(seeds[6], (3 * D,), 0.5, 3.0, ((0, 8),))
    out_weight = gaussian(seeds[7], (D, D), (max(D // 64, 16)) ** -0.5, 1.5, ((0, 8),))
    out_bias = gaussian(seeds[8], (D,), 0.5, 3.0, ((0, 8),))
    mlp_gain = jnp.clip(1.0 + 0.18 * jax.random.normal(seeds[9], (D,), jnp.float32), 0.099609375, 1.8984375).astype(jnp.bfloat16)
    mlp_shift = gaussian(seeds[10], (D,), 0.5, 3.0, ((0, 8),))
    up_weight = gaussian(seeds[11], (D, FF), D ** -0.5, 0.1875, ((0, 8),))
    up_bias = gaussian(seeds[12], (FF,), 0.5, 3.0, ((0, 8),))
    down_weight = gaussian(seeds[13], (FF, D), FF ** -0.5, 0.09375, ((0, 8),))
    down_bias = gaussian(seeds[14], (D,), 0.5, 3.0, ((0, 8),))
    time_weight = gaussian(seeds[15], (TE, D), TE ** -0.5, 0.375, ((0, 8),))
    time_bias = gaussian(seeds[16], (D,), 0.5, 3.0, ((0, 8),))
    cotangent = bell_draw_with(seeds[17], (TOKENS, D), 1.0, 12.0, ((0, 32),), (0, 1, 32, 2.75))
    return dict(activations=activations, time_features=time_features, lengths=lengths, attn_gain=attn_gain, attn_shift=attn_shift, qkv_weight=qkv_weight, qkv_bias=qkv_bias, out_weight=out_weight, out_bias=out_bias, mlp_gain=mlp_gain, mlp_shift=mlp_shift, up_weight=up_weight, up_bias=up_bias, down_weight=down_weight, down_bias=down_bias, time_weight=time_weight, time_bias=time_bias, cotangent=cotangent)


@jax.custom_vjp
def low(v):
    return lax.optimization_barrier(v.astype(jnp.bfloat16)).astype(jnp.float32)

@jax.custom_vjp
def low_back(v):
    return v

def low_keep(v):
    return (low(v), None)

def low_pass(kept, grad):
    return (grad,)

def back_keep(v):
    return (v, None)

def back_low(kept, grad):
    return (low(grad),)
low.defvjp(low_keep, low_pass)
low_back.defvjp(back_keep, back_low)

def segment_info(lengths_row, token_count):
    ends_at = jnp.cumsum(lengths_row)
    starts_at = ends_at - lengths_row
    indices = jnp.arange(token_count, dtype=jnp.int32)
    segment = lax.optimization_barrier(jnp.sum((indices[:, None] >= ends_at[None, :]).astype(jnp.int32), axis=1))
    members = segment[:, None] == jnp.arange(lengths_row.shape[0], dtype=jnp.int32)[None, :]
    offset = lax.optimization_barrier(jnp.sum(members.astype(jnp.int32) * starts_at[None, :], axis=1))
    position = (indices - offset).astype(jnp.float32)
    return (segment, members.astype(jnp.float32), position, segment < lengths_row.shape[0])

def rotary_tables(position, head_size):
    half_size = head_size // 2
    frequency = 10000.0 ** (-2.0 * jnp.arange(half_size, dtype=jnp.float32) / head_size)
    angles = position[:, None] * frequency[None, :]
    return (jnp.cos(angles)[:, None, :], jnp.sin(angles)[:, None, :])

def rotate(vectors, cosine_table, sine_table):
    half_size = vectors.shape[-1] // 2
    first_half = vectors[..., :half_size]
    second_half = vectors[..., half_size:]
    return jnp.concatenate([first_half * cosine_table - second_half * sine_table, second_half * cosine_table + first_half * sine_table], axis=-1)

def layer_norm(vectors, gain_vector, shift_vector):
    center = vectors - lax.optimization_barrier(jnp.mean(vectors, axis=-1, keepdims=True))
    variance = lax.optimization_barrier(jnp.mean(center * center, axis=-1, keepdims=True))
    return center * lax.rsqrt(variance + 1e-05) * gain_vector + shift_vector

def block_layer(weights_all, inputs_block, time_block, lengths_row):
    attn_gain, attn_shift, qkv_weight, qkv_bias, out_weight, out_bias, mlp_gain, mlp_shift, up_weight, up_bias, down_weight, down_bias, time_weight, time_bias = weights_all
    highest = lax.Precision.HIGHEST
    token_count = inputs_block.shape[0]
    model_width = inputs_block.shape[1]
    head_size = model_width // H
    segment, members, position, valid_rows = segment_info(lengths_row, token_count)
    time_rows = jnp.dot(time_block, time_weight, precision=highest) + time_bias
    resid_zero = inputs_block + jnp.dot(members, time_rows, precision=highest)
    attn_in = low(layer_norm(resid_zero, attn_gain, attn_shift))
    qkv_rows = low_back(jnp.dot(attn_in, qkv_weight, precision=highest) + qkv_bias)
    qkv_rows = qkv_rows.reshape(token_count, 3, H, head_size)
    cosine_table, sine_table = rotary_tables(position, head_size)
    queries = low(rotate(qkv_rows[:, 0], cosine_table, sine_table))
    key_rows = low(rotate(qkv_rows[:, 1], cosine_table, sine_table))
    values = low(qkv_rows[:, 2])
    same_segment = segment[:, None] == segment[None, :]
    scores = low_back(jnp.einsum('qhd,khd->hqk', queries, key_rows, precision=highest) * head_size ** (-0.5))
    scores = jnp.where(same_segment[None], scores, -1e+30)
    highest_score = lax.optimization_barrier(jnp.max(scores, axis=-1, keepdims=True))
    exponent = jnp.exp(scores - highest_score)
    soft = low(exponent / lax.optimization_barrier(jnp.sum(exponent, axis=-1, keepdims=True)))
    attended = jnp.einsum('hqk,khd->qhd', soft, values, precision=highest).reshape(token_count, model_width)
    attended = low(low_back(attended))
    attn_branch = low_back(jnp.dot(attended, out_weight, precision=highest) + out_bias)
    resid_one = resid_zero + attn_branch
    mlp_in = low(layer_norm(resid_one, mlp_gain, mlp_shift))
    pre_act = low_back(jnp.dot(mlp_in, up_weight, precision=highest) + up_bias)
    activated = low(jax.nn.gelu(pre_act, approximate=False))
    mlp_branch = low_back(jnp.dot(activated, down_weight, precision=highest) + down_bias)
    return jnp.where(valid_rows[:, None], resid_one + mlp_branch, 0.0)

def reference(activations, time_features, lengths, attn_gain, attn_shift, qkv_weight, qkv_bias, out_weight, out_bias, mlp_gain, mlp_shift, up_weight, up_bias, down_weight, down_bias, time_weight, time_bias, cotangent):
    device_count = N_DP * N_FSDP
    weights_all = (attn_gain.astype(jnp.float32), attn_shift.astype(jnp.float32), qkv_weight.astype(jnp.float32), qkv_bias.astype(jnp.float32), out_weight.astype(jnp.float32), out_bias.astype(jnp.float32), mlp_gain.astype(jnp.float32), mlp_shift.astype(jnp.float32), up_weight.astype(jnp.float32), up_bias.astype(jnp.float32), down_weight.astype(jnp.float32), down_bias.astype(jnp.float32), time_weight.astype(jnp.float32), time_bias.astype(jnp.float32))
    input_blocks = activations.astype(jnp.float32).reshape(device_count, TOK_DEV, D)
    time_blocks = time_features.astype(jnp.float32).reshape(device_count, SEQ_DEV, TE)
    cot_blocks = cotangent.astype(jnp.float32).reshape(device_count, TOK_DEV, D)
    checked_layer = jax.checkpoint(block_layer)

    def forward(inputs_all, params_all):

        def one_block(block_args):
            return checked_layer(params_all, block_args[0], block_args[1], block_args[2])
        return lax.map(one_block, (inputs_all, time_blocks, lengths))
    outputs, pullback = jax.vjp(forward, input_blocks, weights_all)
    input_grad, grads = pullback(cot_blocks)
    return (outputs.reshape(TOKENS, D).astype(jnp.bfloat16), input_grad.reshape(TOKENS, D).astype(jnp.bfloat16), grads[0], grads[1], grads[2], grads[3][:2 * D], grads[3][2 * D:], grads[4], grads[5], grads[6], grads[7], grads[8], grads[9], grads[10], grads[11], grads[12], grads[13])
```

```python
from functools import partial

import jax
import jax.numpy as jnp
from jax import lax
from jax.experimental import pallas as pl
from jax.experimental.pallas import tpu as pltpu
from jax.sharding import PartitionSpec as P

H = 16
GROUP = 4
BLOCKS = 8
PIECES = 10
CHIPS = 4
CHIP_AT = BLOCKS
ENDS_AT = BLOCKS + CHIPS
FAR = -1e30
NO_COST = pl.CostEstimate(flops=0, bytes_accessed=0, transcendentals=0)
F32 = jnp.float32
BF16 = jnp.bfloat16


def rows_by_cols(a, b):
    return lax.dot_general(a, b, (((1,), (0,)), ((), ())), preferred_element_type=F32)


def rows_by_rows(a, b):
    return lax.dot_general(a, b, (((1,), (1,)), ((), ())), preferred_element_type=F32)


def cols_by_cols(a, b):
    return lax.dot_general(a, b, (((0,), (0,)), ((), ())), preferred_element_type=F32)


def call(kernel, scalars, inputs, in_specs, out_shapes, out_specs, grid, scratch=(), aliases=None, after=()):
    count = len(inputs)

    def body(s_ref, *refs):
        kernel(s_ref, *refs[:count], *refs[count + len(after) :])

    return pl.pallas_call(
        body,
        name=getattr(kernel, "func", kernel).__name__,
        grid_spec=pltpu.PrefetchScalarGridSpec(
            num_scalar_prefetch=1,
            grid=grid,
            in_specs=list(in_specs) + [pl.BlockSpec(memory_space=pl.ANY)] * len(after),
            out_specs=out_specs,
            scratch_shapes=list(scratch),
        ),
        out_shape=out_shapes,
        input_output_aliases=aliases or {},
        compiler_params=pltpu.CompilerParams(
            dimension_semantics=("arbitrary",) * len(grid), vmem_limit_bytes=56 * 2**20
        ),
        cost_estimate=NO_COST,
    )(scalars, *inputs, *after)


def next_round(arrays, others):
    def kernel(*refs):
        pass

    anywhere = pl.BlockSpec(memory_space=pl.ANY)
    return pl.pallas_call(
        kernel,
        out_shape=[jax.ShapeDtypeStruct(x.shape, x.dtype) for x in arrays],
        in_specs=[anywhere] * (len(arrays) + len(others)),
        out_specs=[anywhere] * len(arrays),
        input_output_aliases={i: i for i in range(len(arrays))},
        cost_estimate=NO_COST,
    )(*arrays, *others)


def copy_after(x, *others):
    def kernel(x_ref, *refs):
        refs[-1][...] = x_ref[...]

    block = pl.BlockSpec((x.shape[0] // 2, x.shape[1]), lambda i: (i, 0))
    return pl.pallas_call(
        kernel,
        grid=(2,),
        out_shape=jax.ShapeDtypeStruct(x.shape, x.dtype),
        in_specs=[block] + [pl.BlockSpec(memory_space=pl.ANY)] * len(others),
        out_specs=block,
        cost_estimate=NO_COST,
    )(x, *others)


def whole(shape):
    zeros = (0,) * len(shape)
    return pl.BlockSpec(shape, lambda *_: zeros)


def normalize(x):
    center = x - jnp.mean(x, axis=-1, keepdims=True)
    variance = jnp.mean(center * center, axis=-1, keepdims=True)
    inverse = lax.rsqrt(variance + 1e-05)
    return center * inverse, inverse


def normalize_back(grad, normal, inverse, gain):
    scaled = grad * gain
    return inverse * (
        scaled
        - jnp.mean(scaled, axis=-1, keepdims=True)
        - normal * jnp.mean(scaled * normal, axis=-1, keepdims=True)
    )


def row_ids(count, first=0):
    return lax.broadcasted_iota(jnp.int32, (count, 1), 0) + first


def members_of(s_ref, ids, slots):
    out = []
    start = 0
    for slot in range(slots):
        end = s_ref[ENDS_AT + slot]
        out.append((ids >= start) & (ids < end))
        start = end
    return out


def segment_of(s_ref, ids, slots):
    segment = jnp.zeros(ids.shape, jnp.int32)
    for slot in range(slots):
        segment = segment + (ids >= s_ref[ENDS_AT + slot]).astype(jnp.int32)
    return segment


def resid_zero_of(s_ref, act, time_rows, first, slots):
    x = act.astype(F32)
    for slot, inside in enumerate(members_of(s_ref, row_ids(act.shape[0], first), slots)):
        x = x + jnp.where(inside, time_rows[slot : slot + 1, :], 0.0)
    return x


def pieces_of(blocks, half):
    return list(blocks[:6]) + [blocks[6][:half], blocks[6][half:], blocks[7][:half], blocks[7][half:]]


def piece_specs(rows, columns, at):
    sizes = [rows] * 6 + [rows // 2] * 4
    return [pl.BlockSpec((size, columns), lambda *a: (0, at(*a))) for size in sizes]


def rows_of(refs, at=slice(None)):
    return jnp.concatenate([ref[:, at] for ref in refs], axis=0)


def pack_kernel(s_ref, qkv_ref, out_ref, time_ref, *refs):
    vectors, pack_ref = refs[:-1], refs[-1]
    rows, columns = qkv_ref.shape
    pack_ref[0:rows, 0:columns] = qkv_ref[...]
    pack_ref[0:rows, columns:] = out_ref[...]
    depth = pack_ref.shape[0] - rows
    width = out_ref.shape[1]
    pack_ref[rows:, 0:width] = time_ref[0:depth, :]
    pack_ref[rows:, width : 2 * width] = time_ref[depth:, :]
    line = jnp.concatenate([v[...] for v in vectors], axis=1).astype(F32)
    line = jnp.concatenate([line, jnp.zeros((1, pack_ref.shape[1] - 2 * width - line.shape[1]), F32)], axis=1)
    lines = jnp.where(row_ids(depth) == 0, line, 0.0).astype(BF16)
    pack_ref[rows:, 2 * width :] = lines


def norm_one_kernel(slots, s_ref, act_ref, feat_ref, *refs):
    extras = refs[:BLOCKS]
    out_ref, time_ref, lines_ref, qkv_b_ref, up_b_ref = refs[BLOCKS:]
    depth = extras[0].shape[0]
    width = act_ref.shape[1]
    small = width // BLOCKS
    time_rows = jnp.zeros((slots, width), F32)
    for j in range(BLOCKS):
        block = s_ref[j]
        for half in range(2):
            at = pl.multiple_of((block * 2 + half) * 128, 128)
            part = feat_ref[:, pl.ds(at, 128)]
            time_rows = time_rows + rows_by_cols(part[:, 0:depth], extras[j][:, half * width : (half + 1) * width])
        line = extras[j][:, 2 * width :].astype(F32)[0:1]
        at = pl.ds(pl.multiple_of(block * small, 128), small)
        for v in range(7):
            lines_ref[v : v + 1, at] = line[:, v * small : (v + 1) * small]
        first = 7 * small
        for ref in (qkv_b_ref, up_b_ref):
            size = ref.shape[1] // BLOCKS
            ref[0:1, pl.ds(pl.multiple_of(block * size, 128), size)] = line[:, first : first + size]
            first += size
    lines_ref[7:8, :] = jnp.zeros((1, width), F32)
    time_rows = time_rows + lines_ref[6:7, :]
    time_ref[...] = time_rows
    x = resid_zero_of(s_ref, act_ref[...], time_rows, 0, slots)
    normal, _ = normalize(x)
    out_ref[...] = (normal * lines_ref[0:1, :] + lines_ref[1:2, :]).astype(BF16)


def by_block(s_ref, x_ref, out_ref, back=False):
    width = x_ref.shape[1] // BLOCKS
    for j in range(BLOCKS):
        at = pl.ds(pl.multiple_of(s_ref[j] * width, 128), width)
        if back:
            out_ref[:, at] = x_ref[:, j * width : (j + 1) * width]
        else:
            out_ref[:, j * width : (j + 1) * width] = x_ref[:, at]


def turn(x, cosine, sine):
    lanes = lax.broadcasted_iota(jnp.int32, x.shape, 1)
    width = x.shape[1]
    swapped = jnp.where(lanes % 64 < 32, pltpu.roll(x, width - 32, 1), pltpu.roll(x, 32, 1))
    return x * cosine + swapped * sine


def lane_ids(width):
    return lax.broadcasted_iota(jnp.int32, (1, width), 1)


def head_lanes(h, width):
    lanes = lane_ids(width)
    return (lanes >= h * 64) & (lanes < (h + 1) * 64)


def spare_head(h):
    return 1 if h == 0 else 0


def mask_lanes(s_ref, tokens, width, slots, query_ref, key_ref):
    segment = segment_of(s_ref, row_ids(tokens), slots)
    for p in range(2):
        at = lane_ids(width) - 64 * p
        inside = (at >= 0) & (at <= slots)
        more = (at > slots) & (at <= slots + 3)
        query_ref[p] = jnp.where(inside & (at != segment), FAR, 0.0).astype(BF16)
        key_ref[p] = jnp.where((inside & (at == segment)) | more, 1.0, 0.0).astype(BF16)


def attention_kernel(slots, s_ref, x_ref, bq_ref, bk_ref, bv_ref, cos_ref, sin_ref, *refs):
    wq, wk, wv = refs[:PIECES], refs[PIECES : 2 * PIECES], refs[2 * PIECES : 3 * PIECES]
    q_ref, k_ref, v_ref, att_ref, lse_ref, rel_ref, qm_ref, km_ref = refs[3 * PIECES :]
    tokens, width = q_ref.shape

    @pl.when(pl.program_id(0) == 0)
    def _():
        by_block(s_ref, x_ref, rel_ref)
        mask_lanes(s_ref, tokens, width, slots, qm_ref, km_ref)

    x = rel_ref[...]
    cosine, sine = cos_ref[...], sin_ref[...]
    q = turn(rows_by_cols(x, rows_of(wq)) + bq_ref[...], cosine, sine).astype(BF16)
    k = turn(rows_by_cols(x, rows_of(wk)) + bk_ref[...], cosine, sine).astype(BF16)
    v = (rows_by_cols(x, rows_of(wv)) + bv_ref[...]).astype(BF16)
    q = q * jnp.asarray(0.125, BF16)
    q_ref[...] = q
    k_ref[...] = k
    v_ref[...] = v
    masked_keys = [jnp.where(head_lanes(p, width), km_ref[p], k) for p in range(2)]
    total = jnp.zeros((tokens, width), F32)
    lse = jnp.zeros((tokens, 128), F32)
    for h in range(GROUP):
        p = spare_head(h)
        mine = head_lanes(h, width)
        scores = rows_by_rows(jnp.where(mine, q, qm_ref[p]), masked_keys[p])
        top = jnp.max(scores, axis=1, keepdims=True)
        e = jnp.exp(scores - top)
        denominator = jnp.sum(e, axis=1, keepdims=True)
        part = rows_by_cols(e.astype(BF16), v) * (1.0 / denominator)
        total = jnp.where(mine, part, total)
        lse = jnp.where(lane_ids(128) == h, top + jnp.log(denominator), lse)
    att_ref[...] = total.astype(BF16)
    lse_ref[0] = lse


def out_kernel(slots, s_ref, att_ref, act_ref, time_ref, bias_ref, gain_ref, shift_ref, *refs):
    w, (res_ref, mlp_ref, rel_ref) = refs[:PIECES], refs[PIECES:]
    by_block(s_ref, att_ref, rel_ref)
    x = resid_zero_of(s_ref, act_ref[...], time_ref[...], 0, slots)
    x = x + rows_by_cols(rel_ref[...], rows_of(w)) + bias_ref[...]
    res_ref[...] = x
    normal, _ = normalize(x)
    mlp_ref[...] = (normal * gain_ref[...] + shift_ref[...]).astype(BF16)


def up_kernel(s_ref, x_ref, bias_ref, *refs):
    w, (act_ref, slope_ref, rel_ref) = refs[:PIECES], refs[PIECES:]

    @pl.when(pl.program_id(0) == 0)
    def _():
        by_block(s_ref, x_ref, rel_ref)

    pre = rows_by_cols(rel_ref[...], rows_of(w)) + bias_ref[...]
    cdf = 0.5 + 0.5 * lax.erf(pre * 0.7071067811865476)
    density = 0.3989422804014327 * jnp.exp(-0.5 * pre * pre)
    act_ref[...] = (pre * cdf).astype(BF16)
    slope_ref[...] = (cdf + pre * density).astype(BF16)


def down_copies(refs, held_ref, sems):
    rows = held_ref.shape[1]
    at, out = 0, []
    for n, ref in enumerate(refs):
        size = ref.shape[0]
        block, first = at // rows, at % rows
        out.append((block // 2, pltpu.make_async_copy(ref, held_ref.at[block, pl.ds(first, size)], sems.at[n])))
        at += size
    return out


def fetch_down(step, copies):
    @pl.when(step == 0)
    def _():
        for _, copy in copies:
            copy.start()

    for chip in range(CHIPS):

        @pl.when(step == chip)
        def _():
            for owner, copy in copies:
                if owner == chip:
                    copy.wait()


def halves_of(s_ref, width):
    core = s_ref[0] % 2
    return [pl.ds(pl.multiple_of(at * width, 128), width) for at in (core, 1 - core)]


def down_kernel(slots, s_ref, a_ref, res_ref, bias_ref, *refs):
    w, (out_ref, acc_ref, held_ref, sems) = refs[:PIECES], refs[PIECES:]
    c = pl.program_id(0)
    fetch_down(c, down_copies(w, held_ref, sems))

    @pl.when(c == 0)
    def _():
        acc_ref[...] = res_ref[...] + bias_ref[...]

    for n, at in enumerate(halves_of(s_ref, held_ref.shape[1])):
        acc_ref[...] += rows_by_cols(a_ref[:, at], held_ref[2 * c + n])

    @pl.when(c == pl.num_programs(0) - 1)
    def _():
        valid = row_ids(out_ref.shape[0]) < s_ref[ENDS_AT + slots - 1]
        out_ref[...] = jnp.where(valid, acc_ref[...], 0.0).astype(BF16)


def branch_kernel(slots, s_ref, cot_ref, branch_ref, bias_ref):
    valid = row_ids(cot_ref.shape[0]) < s_ref[ENDS_AT + slots - 1]
    branch = jnp.where(valid, cot_ref[...].astype(F32), 0.0)
    branch_ref[...] = branch.astype(BF16)
    bias_ref[...] = jnp.sum(branch, axis=0, keepdims=True)


def mlp_back_kernel(s_ref, branch_ref, slope_ref, res_ref, gain_ref, *refs):
    down, up = refs[:PIECES], refs[PIECES : 2 * PIECES]
    pre_ref, bias_ref, dres_ref, datt_ref, sums_ref, acc_ref, grad_ref, held_ref, sems = refs[2 * PIECES :]
    c = pl.program_id(0)
    fetch_down(c, down_copies(down, held_ref, sems))

    @pl.when(c == 0)
    def _():
        acc_ref[...] = jnp.zeros_like(acc_ref)

    branch = branch_ref[...]
    for n, at in enumerate(halves_of(s_ref, held_ref.shape[1])):
        d_pre = (rows_by_rows(branch, held_ref[2 * c + n]) * slope_ref[:, at].astype(F32)).astype(BF16)
        pre_ref[:, at] = d_pre
        bias_ref[:, at] = jnp.sum(d_pre.astype(F32), axis=0, keepdims=True)
        acc_ref[...] += rows_by_rows(d_pre, rows_of(up, at))

    @pl.when(c == pl.num_programs(0) - 1)
    def _():
        by_block(s_ref, acc_ref, grad_ref, back=True)
        grad = grad_ref[...]
        normal, inverse = normalize(res_ref[...])
        d_res = branch.astype(F32) + normalize_back(grad, normal, inverse, gain_ref[...])
        dres_ref[...] = d_res
        d_att = d_res.astype(BF16)
        datt_ref[...] = d_att
        sums_ref[0:1, :] = jnp.sum(grad * normal, axis=0, keepdims=True)
        sums_ref[1:2, :] = jnp.sum(grad, axis=0, keepdims=True)
        sums_ref[2:3, :] = jnp.sum(d_att.astype(F32), axis=0, keepdims=True)
        sums_ref[3:8, :] = jnp.zeros((5, sums_ref.shape[1]), F32)


def three_lanes(x, p, slots):
    first = x.astype(BF16)
    rest = x - first.astype(F32)
    second = rest.astype(BF16)
    third = (rest - second.astype(F32)).astype(BF16)
    at = lane_ids(64 * GROUP) - 64 * p - slots - 1
    spread = jnp.where(at == 0, first, jnp.where(at == 1, second, third))
    return jnp.where((at >= 0) & (at < 3), spread, jnp.zeros((), BF16))


def attention_back_kernel(slots, s_ref, d_ref, q_ref, k_ref, v_ref, lse_ref, cos_ref, sin_ref, *refs):
    w, (out_ref, sums_ref, qm_ref, km_ref, dq_ref, dk_ref, dv_ref, heads_ref) = refs[:PIECES], refs[PIECES:]
    tokens, width = q_ref.shape
    step = pl.program_id(0)

    @pl.when(pl.program_id(0) == 0)
    def _():
        mask_lanes(s_ref, tokens, width, slots, qm_ref, km_ref)

    for chip, pieces in enumerate((w[0:2], w[2:4], w[4:6], w[6:10])):

        @pl.when(step == chip)
        def _():
            both = rows_by_rows(d_ref[...], rows_of(pieces)).astype(BF16)
            for n, at in enumerate(halves_of(s_ref, width // 2)):
                heads_ref[:, at] = both[:, n * (width // 2) : (n + 1) * (width // 2)]

    d_heads = heads_ref[...]
    q, k, v = q_ref[...], k_ref[...], v_ref[...]
    for h in range(GROUP):
        p = spare_head(h)
        mine, spare = head_lanes(h, width), head_lanes(p, width)
        queries = jnp.where(spare, qm_ref[p] + three_lanes(-lse_ref[0, :, h : h + 1], p, slots), q)
        soft = jnp.exp(rows_by_rows(jnp.where(mine, k, km_ref[p]), queries))
        product = soft * rows_by_rows(jnp.where(mine, v, jnp.zeros((), BF16)), d_heads)
        row_terms = jnp.sum(product, axis=0, keepdims=True)
        d_scores = (product - soft * row_terms).astype(BF16)
        d_v = rows_by_cols(soft.astype(BF16), d_heads)
        d_k = rows_by_cols(d_scores, q)
        d_q = cols_by_cols(d_scores, k)
        if h == 0:
            dq_ref[...], dk_ref[...], dv_ref[...] = d_q, d_k, d_v
        else:
            dq_ref[...] = jnp.where(mine, d_q, dq_ref[...])
            dk_ref[...] = jnp.where(mine, d_k, dk_ref[...])
            dv_ref[...] = jnp.where(mine, d_v, dv_ref[...])
    cosine, sine = cos_ref[...], sin_ref[...]
    sums_ref[...] = jnp.zeros_like(sums_ref)
    parts = (turn(dq_ref[...] * 0.125, cosine, -sine), turn(dk_ref[...], cosine, -sine), dv_ref[...])
    for i, part in enumerate(parts):
        part = part.astype(BF16)
        out_ref[i] = part
        sums_ref[i : i + 1, :] = jnp.sum(part.astype(F32), axis=0, keepdims=True)


def d_input_kernel(slots, s_ref, d_ref, act_ref, time_ref, gain_ref, dres_ref, *refs):
    w, (out_ref, sums_ref, acc_ref, grad_ref) = refs[:PIECES], refs[PIECES:]
    j = pl.program_id(0)

    @pl.when(j == 0)
    def _():
        acc_ref[...] = jnp.zeros_like(acc_ref)

    acc_ref[...] += rows_by_rows(d_ref[0], rows_of(w))

    @pl.when(j == pl.num_programs(0) - 1)
    def _():
        by_block(s_ref, acc_ref, grad_ref, back=True)
        grad = grad_ref[...]
        normal, inverse = normalize(resid_zero_of(s_ref, act_ref[...], time_ref[...], 0, slots))
        d_in = dres_ref[...] + normalize_back(grad, normal, inverse, gain_ref[...])
        out_ref[...] = d_in.astype(BF16)
        sums_ref[...] = jnp.zeros_like(sums_ref)
        sums_ref[0:1, :] = jnp.sum(grad * normal, axis=0, keepdims=True)
        sums_ref[1:2, :] = jnp.sum(grad, axis=0, keepdims=True)
        for slot, inside in enumerate(members_of(s_ref, row_ids(act_ref.shape[0]), slots)):
            sums_ref[2 + slot : 3 + slot, :] = jnp.sum(jnp.where(inside, d_in, 0.0), axis=0, keepdims=True)


def grad_kernel(steps, sources, s_ref, *refs):
    per = 5 * sources
    outs = refs[per * len(steps) :]
    i = pl.program_id(0)
    first = 0
    for n, (count, lead) in enumerate(steps):
        mine = refs[per * n : per * (n + 1)]

        @pl.when((i >= first) & (i < first + count))
        def _():
            product = None
            for source in range(sources):
                *a_refs, b_ref = mine[5 * source : 5 * source + 5]
                a = jnp.concatenate([ref[...] for ref in a_refs], axis=1)
                part = cols_by_cols(a, b_ref[0] if lead else b_ref[...])
                product = part if product is None else product + part
            rows = product.shape[0] // 4
            for j, out in enumerate(outs):
                out[...] = product[j * rows : (j + 1) * rows].astype(BF16)

        first += count


def weight_grad(scalars, odd, pairs, tile, after=()):
    tokens, width = pairs[0][0].shape[0], pairs[0][0].shape[1] // BLOCKS
    sources = len(pairs[0]) // 2
    specs, inputs, steps = [], [], []
    first = 0
    for pair in pairs:
        lead = pair[1].ndim == 3
        per = pair[1].shape[-1] // tile
        count = per * (pair[1].shape[0] if lead else 1)

        def local(i, first=first, count=count):
            return jnp.clip(i - first, 0, count - 1)

        for a, b in zip(pair[::2], pair[1::2]):
            for j in range(4):
                specs.append(pl.BlockSpec((tokens, width), lambda i, s, j=j: (0, s[2 * j + odd])))
                inputs.append(a)
            if lead:
                specs.append(
                    pl.BlockSpec((1, tokens, tile), lambda i, s, at=local, per=per: (at(i) // per, 0, at(i) % per))
                )
            else:
                specs.append(pl.BlockSpec((tokens, tile), lambda i, s, at=local: (0, at(i))))
            inputs.append(b)
        steps.append((count, lead))
        first += count
    return call(
        partial(grad_kernel, tuple(steps), sources), scalars, inputs, specs,
        [jax.ShapeDtypeStruct((width, first * tile), BF16)] * 4,
        [pl.BlockSpec((width, tile), lambda i, s: (0, i))] * 4, (first,), after=after,
    )


def pack_grads_kernel(slots, s_ref, one_ref, qkv_ref, two_ref, up_ref, down_ref, time_ref, odd_ref, even_ref):
    rows = time_ref.shape[0] // BLOCKS
    d_time = one_ref[2 : 2 + slots, :]
    one, two = d_time.shape[1] // BLOCKS, 2 * d_time.shape[1] // BLOCKS
    ff = up_ref.shape[1] // BLOCKS
    odd_ref[...] = jnp.zeros_like(odd_ref)
    even_ref[...] = jnp.zeros_like(even_ref)
    for j in range(BLOCKS):
        block = s_ref[j]
        out = odd_ref if j % 2 else even_ref
        features = time_ref[pl.ds(pl.multiple_of(block * rows, 8), rows), :]
        out[j // 2, 0:rows, :] = sum(features[:, s : s + 1] * d_time[s : s + 1, :] for s in range(slots)).astype(BF16)
        at = pl.ds(pl.multiple_of(block * one, 128), one)
        sources = (one_ref[0:1, at], one_ref[1:2, at], two_ref[2:3, at], two_ref[0:1, at], two_ref[1:2, at],
                   down_ref[0:1, at], qkv_ref[2:3, at])
        line = jnp.concatenate(sources, axis=1)
        out[j // 2, rows : rows + 1, 0 : line.shape[1]] = line.astype(BF16)
        wide = pl.ds(pl.multiple_of((block % 4) * two, 128), two)
        pair = jnp.where(block < 4, qkv_ref[0:1, wide], qkv_ref[1:2, wide])
        hidden = up_ref[0:1, pl.ds(pl.multiple_of(block * ff, 128), ff)]
        out[j // 2, rows + 1 : rows + 2, 0 : two + ff] = jnp.concatenate([pair, hidden], axis=1).astype(BF16)
        bias = jnp.sum(one_ref[2 : 2 + slots, at], axis=0, keepdims=True)
        out[j // 2, rows + 2 : rows + 3, 0:one] = bias.astype(BF16)


def per_device(
    n_dp, n_fsdp, activations, time_features, lengths, attn_gain, attn_shift, qkv_weight, qkv_bias, out_weight, out_bias,
    mlp_gain, mlp_shift, up_weight, up_bias, down_weight, down_bias, time_weight, time_bias, cotangent,
):
    tokens, width = activations.shape
    slots = lengths.shape[1]
    hidden = down_weight.shape[0] * n_fsdp
    small = n_fsdp == BLOCKS
    me = lax.axis_index("fsdp")
    blocks = jnp.arange(BLOCKS, dtype=jnp.int32)
    chips = jnp.arange(CHIPS, dtype=jnp.int32)
    if small:
        blocks, chips = blocks ^ me, chips ^ (me // 2)
    upto = jnp.arange(slots)[:, None] >= jnp.arange(slots)[None, :]
    ends = jnp.sum(jnp.where(upto, lengths, 0), axis=1)
    scalars = jnp.concatenate([blocks, chips, ends]).astype(jnp.int32)

    def swap(x, bit):
        return lax.ppermute(x, "fsdp", [(i, i ^ bit) for i in range(n_fsdp)])

    def add(*parts):
        total = parts[0].astype(F32)
        for part in parts[1:]:
            total = total + part.astype(F32)
        return total.astype(BF16)

    def gather_rows(w):
        return lax.all_gather(w, "fsdp", axis=0, tiled=True).reshape(BLOCKS, -1, w.shape[1])

    rows = whole((tokens, width))
    line = whole((1, width))
    vectors = [attn_gain, attn_shift, out_bias, mlp_gain, mlp_shift, down_bias, time_bias, qkv_bias, up_bias]
    per = width // BLOCKS
    qkv_columns = qkv_weight.shape[1]
    columns = qkv_columns + width
    depth = 16
    if small:
        half = per // 2
        vectors = [v.reshape(1, -1) for v in vectors]
        sources = [qkv_weight, out_weight, time_weight] + vectors
        pack = call(
            pack_kernel, scalars, sources, [whole(x.shape) for x in sources],
            jax.ShapeDtypeStruct((per + depth, columns), BF16), whole((per + depth, columns)), (1,),
        )
        first_x, first_y, first_core = swap(pack, 2), swap(pack, 4), swap(pack, 1)
        up_own, down_own = copy_after(up_weight, pack), copy_after(down_weight, pack)
    else:
        gathered = [lax.all_gather(v, "fsdp", axis=0, tiled=True).reshape(BLOCKS, -1) for v in vectors]
        matrices = jnp.concatenate([gather_rows(qkv_weight), gather_rows(out_weight)], axis=2)
        times = lax.all_gather(time_weight, "fsdp", axis=0, tiled=True).reshape(BLOCKS, 2, depth, width)
        lines = jnp.concatenate(gathered, axis=1)
        lines = jnp.pad(lines, ((0, 0), (0, columns - 2 * width - lines.shape[1])))[:, None]
        lines = jnp.pad(lines, ((0, 0), (0, depth - 1), (0, 0)))
        extra = jnp.concatenate([times[:, 0], times[:, 1], lines], axis=2)
        first = pieces_of(jnp.concatenate([matrices, extra], axis=1), per // 2)
        up_rel = pieces_of(gather_rows(up_weight), per // 2)
        down_rel = pieces_of(gather_rows(down_weight), hidden // BLOCKS // 2)

    ids = jnp.arange(tokens, dtype=jnp.int32)[:, None]
    starts = ends - lengths[0]
    inside = (ids >= starts[None, :]) & (ids < ends[None, :])
    position = (ids[:, 0] - jnp.sum(jnp.where(inside, starts[None, :], 0), axis=1)).astype(F32)
    frequency = 10000.0 ** (-2.0 * jnp.arange(32, dtype=F32) / 64)
    angles = position[:, None] * frequency[None, :]
    cosine, sine = jnp.cos(angles), jnp.sin(angles)
    lanes = 64 * GROUP
    cos_table = jnp.tile(cosine, (1, 2 * GROUP))
    sin_table = jnp.tile(jnp.concatenate([-sine, sine], axis=1), (1, GROUP))

    d_branch, down_bias_sum = call(
        partial(branch_kernel, slots), scalars, [cotangent], [rows],
        [jax.ShapeDtypeStruct((tokens, width), BF16), jax.ShapeDtypeStruct((1, width), F32)], [rows, line], (1,),
    )
    if small:
        first_x, first_y = next_round(
            [first_x, first_y], [first_core, d_branch, up_own, down_own, cos_table, sin_table]
        )
        first_a, first_b = swap(first_y[:half], 2), swap(first_x[half:], 4)
        core_x, core_y, branch_core = swap(first_x, 1), swap(first_y, 1), swap(d_branch, 1)
        first_a, first_b, up_own = next_round([first_a, first_b, up_own], [core_x, core_y, branch_core])
        up_x, up_y = swap(up_own, 2), swap(up_own, 4)
        first = [pack, first_core, first_x, core_x, first_y, core_y, first_a, first_b, swap(first_a, 1), swap(first_b, 1)]
    spread = time_features.reshape(slots, 2 * BLOCKS, -1)
    spread = jnp.pad(spread, ((0, 0), (0, 0), (0, 128 - spread.shape[2]))).reshape(slots, -1)
    extra_specs = [pl.BlockSpec((depth, columns), lambda i, s: (per // depth, 0))] * 6
    extra_specs += [pl.BlockSpec((depth, columns), lambda i, s: (per // 2 // depth, 0))] * 2
    attn_in, time_rows, lines, qkv_b, up_b = call(
        partial(norm_one_kernel, slots), scalars, [activations, spread] + first[:6] + [first[7], first[9]],
        [rows, whole(spread.shape)] + extra_specs,
        [jax.ShapeDtypeStruct((tokens, width), BF16), jax.ShapeDtypeStruct((slots, width), F32),
         jax.ShapeDtypeStruct((8, width), F32), jax.ShapeDtypeStruct((1, qkv_columns), F32),
         jax.ShapeDtypeStruct((1, hidden), F32)],
        [rows, whole((slots, width)), whole((8, width)), whole((1, qkv_columns)), whole((1, hidden))], (1,),
        after=(d_branch,),
    )
    gain_one, shift_one, out_b, gain_two, shift_two, down_b = [lines[i : i + 1] for i in range(6)]
    groups = H // GROUP
    col = pl.BlockSpec((tokens, lanes), lambda g, s: (0, g))
    table = whole((tokens, lanes))
    mask_rooms = [pltpu.VMEM((2, tokens, lanes), BF16)] * 2
    qkv_specs = []
    for o in range(3):
        qkv_specs += piece_specs(per, lanes, lambda g, s, o=o: o * groups + g)
    queries, keys, values, attended, lse = call(
        partial(attention_kernel, slots), scalars,
        [attn_in, qkv_b, qkv_b, qkv_b, cos_table, sin_table] + first * 3,
        [rows] + [pl.BlockSpec((1, lanes), lambda g, s, o=o: (0, o * groups + g)) for o in range(3)]
        + [table, table] + qkv_specs,
        [jax.ShapeDtypeStruct((tokens, width), BF16)] * 4 + [jax.ShapeDtypeStruct((groups, tokens, 128), F32)],
        [col, col, col, col, pl.BlockSpec((1, tokens, 128), lambda g, s: (g, 0, 0))],
        (groups,), [pltpu.VMEM((tokens, width), BF16)] + mask_rooms)
    if small:
        up_x, up_y, up_own = next_round([up_x, up_y, up_own], [attended])
        up_low, up_high = swap(up_y[:half], 2), swap(up_x[half:], 4)
        up_core, core_x, core_y = swap(up_own, 1), swap(up_x, 1), swap(up_y, 1)
        wait = (up_x,)
    else:
        wait = ()
    out_specs = piece_specs(per, width, lambda *a: qkv_columns // width)
    resid_one, mlp_in = call(
        partial(out_kernel, slots), scalars,
        [attended, activations, time_rows, out_b, gain_two, shift_two] + first,
        [rows, rows, whole((slots, width)), line, line, line] + out_specs,
        [jax.ShapeDtypeStruct((tokens, width), F32), jax.ShapeDtypeStruct((tokens, width), BF16)],
        [rows, rows], (1,), [pltpu.VMEM((tokens, width), BF16)], after=wait,
    )
    if small:
        up_low, up_high, down_own = next_round([up_low, up_high, down_own], [core_x, core_y, up_core, mlp_in])
        up_rel = [up_own, up_core, up_x, core_x, up_y, core_y, up_low, up_high, swap(up_low, 1), swap(up_high, 1)]
        down_x, down_y, down_core = swap(down_own, 2), swap(down_own, 4), swap(down_own, 1)
    tile = hidden // CHIPS
    wide = pl.BlockSpec((tokens, tile), lambda i, s: (0, i))
    activated, slope = call(
        up_kernel, scalars, [mlp_in, up_b] + up_rel,
        [rows, pl.BlockSpec((1, tile), lambda i, s: (0, i))] + piece_specs(per, tile, lambda i, s: i),
        [jax.ShapeDtypeStruct((tokens, hidden), BF16)] * 2, [wide, wide], (CHIPS,),
        [pltpu.VMEM((tokens, width), BF16)])

    def sum_line(x):
        if n_dp != 4:
            return lax.psum(x, "dp").astype(F32)
        pair = add(x, line_in(x))
        total = add(pair, line_middle(pair))
        return line_end(total, line_out(total))

    def line_in(x):
        return lax.ppermute(x, "dp", [(0, 1), (3, 2)])

    def line_middle(x):
        return lax.ppermute(x, "dp", [(1, 2), (2, 1)])

    def line_out(x):
        return lax.ppermute(x, "dp", [(1, 0), (2, 3)])

    def line_end(total, back):
        z = lax.axis_index("dp")
        return jnp.where((z == 0) | (z == 3), back, total).astype(F32)

    def rows_of_all(pairs, tile):
        blocks = [weight_grad(scalars, odd, pairs, tile) for odd in range(2)]
        both = jnp.stack([x for pair in zip(*blocks) for x in pair]).reshape(-1, blocks[0][0].shape[1])
        return sum_line(lax.psum_scatter(both, "fsdp", scatter_dimension=0, tiled=True))

    if small:
        down_x, down_y, activated = next_round([down_x, down_y, activated], [down_core])
        half = down_own.shape[0] // 2
        down_low, down_high = swap(down_y[:half], 2), swap(down_x[half:], 4)
        core_x, core_y, activated_core = swap(down_x, 1), swap(down_y, 1), swap(activated, 1)
        down_parts = weight_grad(scalars, 0, [(activated, d_branch, activated_core, branch_core)], 512)
        down_low, down_high, to_x, to_y = next_round([down_low, down_high, *down_parts[1:3]], [core_x, core_y])
        down_rel = [down_own, down_core, down_x, core_x, down_y, core_y, down_low, down_high, swap(down_low, 1), swap(down_high, 1)]
        came = [swap(to_x, 2), swap(to_y, 4)]
        mlp_in_core = swap(mlp_in, 1)
    else:
        down_grad = rows_of_all([(activated, d_branch)], 512)

    chip_wide = pl.BlockSpec((tokens, tile), lambda i, s: (0, s[CHIP_AT + i]))
    down_rooms = [pltpu.VMEM((BLOCKS, hidden // BLOCKS, width), BF16), pltpu.SemaphoreType.DMA((PIECES,))]
    d_pre, up_bias_sum, d_resid_one, d_attn, sums_two = call(
        mlp_back_kernel, scalars, [d_branch, slope, resid_one, gain_two] + down_rel + up_rel,
        [rows, chip_wide, rows, line] + [pl.BlockSpec(memory_space=pl.ANY)] * PIECES
        + piece_specs(per, tile, lambda i, s: s[CHIP_AT + i]),
        [jax.ShapeDtypeStruct((tokens, hidden), BF16),
         jax.ShapeDtypeStruct((1, hidden), F32), jax.ShapeDtypeStruct((tokens, width), F32),
         jax.ShapeDtypeStruct((tokens, width), BF16), jax.ShapeDtypeStruct((8, width), F32)],
        [chip_wide, pl.BlockSpec((1, tile), lambda i, s: (0, s[CHIP_AT + i])), rows, rows, whole((8, width))],
        (CHIPS,), [pltpu.VMEM((tokens, width), F32)] * 2 + down_rooms,
    )
    wait = (d_attn,)
    output = call(
        partial(down_kernel, slots), scalars, [activated, resid_one, down_b] + down_rel,
        [chip_wide, rows, line] + [pl.BlockSpec(memory_space=pl.ANY)] * PIECES,
        jax.ShapeDtypeStruct((tokens, width), BF16), rows, (CHIPS,), [pltpu.VMEM((tokens, width), F32)] + down_rooms,
        after=wait)
    if small:
        d_pre, d_attn, to_both = next_round([d_pre, d_attn, down_parts[3]], [*came, mlp_in_core, output])
        d_pre_core, d_attn_core, attended_core = swap(d_pre, 1), swap(d_attn, 1), swap(attended, 1)
        came.append(swap(to_both, 6))
        up_parts = weight_grad(
            scalars, 0, [(mlp_in, d_pre, mlp_in_core, d_pre_core), (attended, d_attn, attended_core, d_attn_core)], width
        )
        to_x, to_y, *came = next_round([*up_parts[1:3], *came], [])
        down_sum = add(down_parts[0], *came)
        came = [swap(to_x, 2), swap(to_y, 4)]
        down_line = line_in(down_sum)
        wait = (to_x,)
    else:
        up_out_grad = rows_of_all([(mlp_in, d_pre), (attended, d_attn)], width)
        up_grad, out_grad = up_out_grad[:, :hidden], up_out_grad[:, hidden:]
        wait = ()
    chip_col = pl.BlockSpec((tokens, lanes), lambda g, s: (0, s[CHIP_AT + g]))
    d_qkv, sums_qkv = call(
        partial(attention_back_kernel, slots), scalars,
        [d_attn, queries, keys, values, lse, cos_table, sin_table] + first,
        [rows, chip_col, chip_col, chip_col,
         pl.BlockSpec((1, tokens, 128), lambda g, s: (s[CHIP_AT + g], 0, 0)), table, table] + out_specs,
        [jax.ShapeDtypeStruct((3, tokens, width), BF16), jax.ShapeDtypeStruct((8, width), F32)],
        [pl.BlockSpec((3, tokens, lanes), lambda g, s: (0, 0, s[CHIP_AT + g])),
         pl.BlockSpec((8, lanes), lambda g, s: (0, s[CHIP_AT + g]))],
        (groups,), mask_rooms + [pltpu.VMEM((tokens, lanes), F32)] * 3 + [pltpu.VMEM((tokens, lanes), BF16)],
        after=wait,
    )
    if small:
        d_qkv, to_both, down_line, *came = next_round([d_qkv, up_parts[3], down_line, *came], [])
        down_sum = add(down_sum, down_line)
        d_qkv_core, attn_in_core = swap(d_qkv, 1), swap(attn_in, 1)
        came.append(swap(to_both, 6))
        down_line = line_middle(down_sum)
        qkv_parts = weight_grad(scalars, 0, [(attn_in, d_qkv, attn_in_core, d_qkv_core)], width)
        wait = (qkv_parts[0],)
    else:
        qkv_grad = rows_of_all([(attn_in, d_qkv)], width)
        wait = ()
    input_grad, sums_one = call(
        partial(d_input_kernel, slots), scalars,
        [d_qkv, activations, time_rows, gain_one, d_resid_one] + first,
        [pl.BlockSpec((1, tokens, width), lambda i, s: (i, 0, 0)), rows, whole((slots, width)), line, rows]
        + piece_specs(per, width, lambda i, s: i),
        [jax.ShapeDtypeStruct((tokens, width), BF16), jax.ShapeDtypeStruct((8, width), F32)],
        [rows, whole((8, width))], (3,), [pltpu.VMEM((tokens, width), F32)] * 2, after=wait,
    )
    if small:
        time_cols = time_features.astype(F32).T
        depth = 48
        v_odd, v_even = call(
            partial(pack_grads_kernel, slots), scalars,
            [sums_one, sums_qkv, sums_two, up_bias_sum, down_bias_sum, time_cols],
            [whole((8, width)), whole((8, width)), whole((8, width)), whole((1, hidden)), line, whole(time_cols.shape)],
            [jax.ShapeDtypeStruct((4, depth, width), BF16)] * 2, [whole((4, depth, width))] * 2, (1,),
        )
        to_x, to_y, v_odd, down_line, *came = next_round([*qkv_parts[1:3], v_odd, down_line, *came], [])
        up_sum = add(up_parts[0], *came)
        came = [swap(to_x, 2), swap(to_y, 4)]
        cut = up_sum.shape[1] // 2
        up_sums = [up_sum[:, :cut], up_sum[:, cut:]]
        up_line = line_in(up_sums[0])
        down_sum = add(down_sum, down_line)
        down_line = line_out(down_sum)
        v_came = swap(v_odd, 1)
        to_both, up_line, down_line, v_came, *came = next_round([qkv_parts[3], up_line, down_line, v_came, *came], [])
        came.append(swap(to_both, 6))
        down_grad = line_end(down_sum, down_line)
        up_sums[0] = add(up_sums[0], up_line)
        up_line, up_line_two = line_middle(up_sums[0]), line_in(up_sums[1])
        part = add(v_even, v_came).reshape(2, 2, depth, width)
        v_came = swap(part[:, 1], 2)
        up_line, up_line_two, v_came, *came = next_round([up_line, up_line_two, v_came, *came], [])
        qkv_sum = add(qkv_parts[0], *came)
        qkv_line = line_in(qkv_sum)
        up_sums = [add(up_sums[0], up_line), add(up_sums[1], up_line_two)]
        up_line, up_line_two = line_out(up_sums[0]), line_middle(up_sums[1])
        part = add(part[:, 0], v_came)
        v_came = swap(part[1], 4)
        up_line, up_line_two, v_came, qkv_line = next_round([up_line, up_line_two, v_came, qkv_line], [])
        up_one = line_end(up_sums[0], up_line)
        up_sums[1] = add(up_sums[1], up_line_two)
        up_line_two = line_out(up_sums[1])
        qkv_sum = add(qkv_sum, qkv_line)
        qkv_line = line_middle(qkv_sum)
        part = add(part[0], v_came)
        v_came = line_in(part)
        up_line_two, qkv_line, v_came = next_round([up_line_two, qkv_line, v_came], [])
        up_two = line_end(up_sums[1], up_line_two)
        qkv_sum = add(qkv_sum, qkv_line)
        qkv_line = line_out(qkv_sum)
        part = add(part, v_came)
        v_came = line_middle(part)
        qkv_line, v_came = next_round([qkv_line, v_came], [])
        qkv_grad = line_end(qkv_sum, qkv_line)
        part = add(part, v_came)
        share = line_end(part, line_out(part))
        up_out_grad = jnp.concatenate([up_one, up_two], axis=1)
        up_grad, out_grad = up_out_grad[:, :hidden], up_out_grad[:, hidden:]
        time_rows_here = time_weight.shape[0]
        time_grad = share[:time_rows_here]
        one, two, ff = width // BLOCKS, 2 * width // BLOCKS, hidden // BLOCKS
        row = share[time_rows_here]
        (gain_one_grad, shift_one_grad, out_bias_grad, gain_two_grad, shift_two_grad, down_bias_grad,
         value_bias_grad) = [row[i * one : (i + 1) * one] for i in range(7)]
        row = share[time_rows_here + 1]
        qk_bias_grad, up_bias_grad = row[:two], row[two : two + ff]
        time_bias_grad = share[time_rows_here + 2, :one]
    else:
        d_time = sums_one[2 : 2 + slots]
        time_grad = lax.dot_general(
            time_features.astype(F32), d_time, (((0,), (0,)), ((), ())), precision=lax.Precision.HIGHEST
        )
        vector_sums = (
            sums_one[0], sums_one[1], sums_qkv[:2].reshape(-1), sums_qkv[2], sums_two[2], sums_two[0], sums_two[1],
            up_bias_sum[0], down_bias_sum[0], jnp.sum(d_time, axis=0),
        )
        shares = jnp.concatenate(
            [time_grad.reshape(n_fsdp, -1)] + [v.reshape(n_fsdp, -1) for v in vector_sums], axis=1
        )
        sizes = [time_weight.size] + [v.size // n_fsdp for v in vector_sums]
        shares = jnp.pad(shares, ((0, 0), (0, -shares.shape[1] % 4096))).reshape(n_fsdp, -1, 128)
        share = sum_line(lax.psum_scatter(shares.astype(BF16), "fsdp", scatter_dimension=0, tiled=False)).reshape(-1)
        got = []
        at = 0
        for size in sizes:
            got.append(share[at : at + size])
            at += size
        (time_grad, gain_one_grad, shift_one_grad, qk_bias_grad, value_bias_grad, out_bias_grad, gain_two_grad,
         shift_two_grad, up_bias_grad, down_bias_grad, time_bias_grad) = got
    return (
        output, input_grad, gain_one_grad, shift_one_grad, qkv_grad, qk_bias_grad, value_bias_grad, out_grad, out_bias_grad,
        gain_two_grad, shift_two_grad, up_grad, up_bias_grad, down_grad, down_bias_grad,
        time_grad.reshape(time_weight.shape), time_bias_grad,
    )


def solution(mesh):
    tokens = P(("dp", "fsdp"), None)
    vector = P("fsdp")
    matrix = P("fsdp", None)
    in_specs = (
        tokens, tokens, tokens, vector, vector, matrix, vector, matrix, vector, vector, vector, matrix, vector, matrix,
        vector, matrix, vector, tokens,
    )
    out_specs = (
        tokens, tokens, vector, vector, matrix, vector, vector, matrix, vector, vector, vector, matrix, vector, matrix,
        vector, matrix, vector,
    )
    body = partial(per_device, mesh.shape["dp"], mesh.shape["fsdp"])
    return jax.shard_map(body, mesh=mesh, in_specs=in_specs, out_specs=out_specs, check_vma=False)
```

```python
from functools import partial

import jax
import jax.numpy as jnp
from jax import lax
from jax.experimental import pallas as pl
from jax.experimental.pallas import tpu as pltpu
from jax.sharding import PartitionSpec as P

H = 16
GROUP = 4
BLOCKS = 8
CHIPS = 4
CHIP_AT = BLOCKS
PARITY_AT = CHIP_AT + CHIPS
ENDS_AT = PARITY_AT + 1
FAR = -1e30
NO_COST = pl.CostEstimate(flops=0, bytes_accessed=0, transcendentals=0)
F32 = jnp.float32
BF16 = jnp.bfloat16


def rows_by_cols(a, b):
    return lax.dot_general(a, b, (((1,), (0,)), ((), ())), preferred_element_type=F32)


def rows_by_rows(a, b):
    return lax.dot_general(a, b, (((1,), (1,)), ((), ())), preferred_element_type=F32)


def cols_by_cols(a, b):
    return lax.dot_general(a, b, (((0,), (0,)), ((), ())), preferred_element_type=F32)


def call(kernel, scalars, inputs, in_specs, out_shapes, out_specs, grid, scratch=(), aliases=None, after=()):
    count = len(inputs)

    def body(s_ref, *refs):
        kernel(s_ref, *refs[:count], *refs[count + len(after) :])

    return pl.pallas_call(
        body,
        name=getattr(kernel, "func", kernel).__name__,
        grid_spec=pltpu.PrefetchScalarGridSpec(
            num_scalar_prefetch=1,
            grid=grid,
            in_specs=list(in_specs) + [pl.BlockSpec(memory_space=pl.ANY)] * len(after),
            out_specs=out_specs,
            scratch_shapes=list(scratch),
        ),
        out_shape=out_shapes,
        input_output_aliases=aliases or {},
        compiler_params=pltpu.CompilerParams(
            dimension_semantics=("arbitrary",) * len(grid), vmem_limit_bytes=64 * 2**20
        ),
        cost_estimate=NO_COST,
    )(scalars, *inputs, *after)


def round_kernel(counts, s_ref, *refs):
    outs = refs[-len(counts) :] if counts else ()
    at = 0
    for count, out in zip(counts, outs):
        total = refs[at][...].astype(F32)
        for ref in refs[at + 1 : at + count]:
            total = total + ref[...].astype(F32)
        out[...] = total.astype(BF16)
        at += count


def next_round(scalars, passed, others=(), sums=()):
    anywhere = pl.BlockSpec(memory_space=pl.ANY)
    steps = 4
    specs, inputs, counts, shapes, out_specs = [], [], [], [], []
    for parts, rows, columns in sums:
        size = rows // steps
        for array, row, column in parts:
            even, odd = row if isinstance(row, tuple) else (row, row)

            def at(i, s, even=even // size, odd=odd // size, column=column // columns):
                return (i + even + s[PARITY_AT] * (odd - even), column)

            specs.append(pl.BlockSpec((size, columns), at))
            inputs.append(array)
        counts.append(len(parts))
        shapes.append(jax.ShapeDtypeStruct((rows, columns), BF16))
        out_specs.append(pl.BlockSpec((size, columns), lambda i, s: (i, 0)))
    first = len(inputs)

    def kernel(s_ref, *refs):
        given = first + len(passed) + len(others)
        round_kernel(counts, s_ref, *refs[:first], *refs[given + len(passed) :])

    out = pl.pallas_call(
        kernel,
        name="next_round",
        grid_spec=pltpu.PrefetchScalarGridSpec(
            num_scalar_prefetch=1,
            grid=(steps if sums else 1,),
            in_specs=specs + [anywhere] * (len(passed) + len(others)),
            out_specs=[anywhere] * len(passed) + out_specs,
        ),
        out_shape=[jax.ShapeDtypeStruct(x.shape, x.dtype) for x in passed] + shapes,
        input_output_aliases={1 + first + i: i for i in range(len(passed))},
        compiler_params=pltpu.CompilerParams(dimension_semantics=("arbitrary",), vmem_limit_bytes=64 * 2**20),
        cost_estimate=NO_COST,
    )(scalars, *inputs, *passed, *others)
    return list(out)


def copy_after(x, *others):
    def kernel(x_ref, *refs):
        refs[-1][...] = x_ref[...]

    block = pl.BlockSpec((x.shape[0] // 2, x.shape[1]), lambda i: (i, 0))
    return pl.pallas_call(
        kernel,
        grid=(2,),
        out_shape=jax.ShapeDtypeStruct(x.shape, x.dtype),
        in_specs=[block] + [pl.BlockSpec(memory_space=pl.ANY)] * len(others),
        out_specs=block,
        cost_estimate=NO_COST,
    )(x, *others)


def whole(shape):
    zeros = (0,) * len(shape)
    return pl.BlockSpec(shape, lambda *_: zeros)


def normalize(x):
    center = x - jnp.mean(x, axis=-1, keepdims=True)
    variance = jnp.mean(center * center, axis=-1, keepdims=True)
    inverse = lax.rsqrt(variance + 1e-05)
    return center * inverse, inverse


def normalize_back(grad, normal, inverse, gain):
    scaled = grad * gain
    return inverse * (
        scaled
        - jnp.mean(scaled, axis=-1, keepdims=True)
        - normal * jnp.mean(scaled * normal, axis=-1, keepdims=True)
    )


def row_ids(count, first=0):
    return lax.broadcasted_iota(jnp.int32, (count, 1), 0) + first


def members_of(s_ref, ids, slots):
    out = []
    start = 0
    for slot in range(slots):
        end = s_ref[ENDS_AT + slot]
        out.append((ids >= start) & (ids < end))
        start = end
    return out


def segment_of(s_ref, ids, slots):
    segment = jnp.zeros(ids.shape, jnp.int32)
    for slot in range(slots):
        segment = segment + (ids >= s_ref[ENDS_AT + slot]).astype(jnp.int32)
    return segment


def resid_zero_of(s_ref, act, time_rows, first, slots):
    x = act.astype(F32)
    for slot, inside in enumerate(members_of(s_ref, row_ids(act.shape[0], first), slots)):
        x = x + jnp.where(inside, time_rows[slot : slot + 1, :], 0.0)
    return x


def piece_specs(rows, columns, at):
    return [pl.BlockSpec((rows, columns), lambda *a: (0, at(*a)))] * BLOCKS


def rows_of(refs, at=slice(None)):
    return jnp.concatenate([ref[:, at] for ref in refs], axis=0)


def pack_kernel(s_ref, qkv_ref, out_ref, time_ref, *refs):
    vectors, pack_ref = refs[:-1], refs[-1]
    rows, columns = qkv_ref.shape
    pack_ref[0:rows, 0:columns] = qkv_ref[...]
    pack_ref[0:rows, columns:] = out_ref[...]
    depth = pack_ref.shape[0] - rows
    width = out_ref.shape[1]
    pack_ref[rows:, 0:width] = time_ref[0:depth, :]
    pack_ref[rows:, width : 2 * width] = time_ref[depth:, :]
    line = jnp.concatenate([v[...].astype(F32).reshape(1, -1) for v in vectors], axis=1)
    line = jnp.concatenate([line, jnp.zeros((1, pack_ref.shape[1] - 2 * width - line.shape[1]), F32)], axis=1)
    lines = jnp.where(row_ids(depth) == 0, line, 0.0).astype(BF16)
    pack_ref[rows:, 2 * width :] = lines


def norm_one_kernel(slots, s_ref, act_ref, feat_ref, *refs):
    extras = refs[:BLOCKS]
    out_ref, time_ref, lines_ref, qkv_b_ref, up_b_ref = refs[BLOCKS:]
    depth = extras[0].shape[0]
    width = act_ref.shape[1]
    small = width // BLOCKS
    time_rows = jnp.zeros((slots, width), F32)
    for j in range(BLOCKS):
        block = s_ref[j]
        for half in range(2):
            at = pl.multiple_of((block * 2 + half) * 128, 128)
            part = feat_ref[:, pl.ds(at, 128)]
            time_rows = time_rows + rows_by_cols(part[:, 0:depth], extras[j][:, half * width : (half + 1) * width])
        line = extras[j][:, 2 * width :].astype(F32)[0:1]
        at = pl.ds(pl.multiple_of(block * small, 128), small)
        for v in range(7):
            lines_ref[v : v + 1, at] = line[:, v * small : (v + 1) * small]
        first = 7 * small
        for ref in (qkv_b_ref, up_b_ref):
            size = ref.shape[1] // BLOCKS
            ref[0:1, pl.ds(pl.multiple_of(block * size, 128), size)] = line[:, first : first + size]
            first += size
    lines_ref[7:8, :] = jnp.zeros((1, width), F32)
    time_rows = time_rows + lines_ref[6:7, :]
    time_ref[...] = time_rows
    x = resid_zero_of(s_ref, act_ref[...], time_rows, 0, slots)
    normal, _ = normalize(x)
    out_ref[...] = (normal * lines_ref[0:1, :] + lines_ref[1:2, :]).astype(BF16)


def by_block(s_ref, x_ref, out_ref, back=False):
    width = x_ref.shape[1] // BLOCKS
    for j in range(BLOCKS):
        at = pl.ds(pl.multiple_of(s_ref[j] * width, 128), width)
        if back:
            out_ref[:, at] = x_ref[:, j * width : (j + 1) * width]
        else:
            out_ref[:, j * width : (j + 1) * width] = x_ref[:, at]


def turn(x, cosine, sine):
    lanes = lax.broadcasted_iota(jnp.int32, x.shape, 1)
    width = x.shape[1]
    swapped = jnp.where(lanes % 64 < 32, pltpu.roll(x, width - 32, 1), pltpu.roll(x, 32, 1))
    return x * cosine + swapped * sine


def lane_ids(width):
    return lax.broadcasted_iota(jnp.int32, (1, width), 1)


def head_lanes(h, width):
    lanes = lane_ids(width)
    return (lanes >= h * 64) & (lanes < (h + 1) * 64)


def spare_head(h):
    return 1 if h == 0 else 0


def mask_lanes(s_ref, tokens, width, slots, query_ref, key_ref):
    segment = segment_of(s_ref, row_ids(tokens), slots)
    for p in range(2):
        at = lane_ids(width) - 64 * p
        inside = (at >= 0) & (at <= slots)
        more = (at > slots) & (at <= slots + 3)
        query_ref[p] = jnp.where(inside & (at != segment), FAR, 0.0).astype(BF16)
        key_ref[p] = jnp.where((inside & (at == segment)) | more, 1.0, 0.0).astype(BF16)


def attention_kernel(slots, s_ref, x_ref, bq_ref, bk_ref, bv_ref, cos_ref, sin_ref, *refs):
    wq, wk, wv = refs[:BLOCKS], refs[BLOCKS : 2 * BLOCKS], refs[2 * BLOCKS : 3 * BLOCKS]
    q_ref, k_ref, v_ref, att_ref, lse_ref, rel_ref, qm_ref, km_ref = refs[3 * BLOCKS :]
    tokens, width = q_ref.shape

    @pl.when(pl.program_id(0) == 0)
    def _():
        by_block(s_ref, x_ref, rel_ref)
        mask_lanes(s_ref, tokens, width, slots, qm_ref, km_ref)

    x = rel_ref[...]
    cosine, sine = cos_ref[...], sin_ref[...]
    q = turn(rows_by_cols(x, rows_of(wq)) + bq_ref[...], cosine, sine).astype(BF16)
    k = turn(rows_by_cols(x, rows_of(wk)) + bk_ref[...], cosine, sine).astype(BF16)
    v = (rows_by_cols(x, rows_of(wv)) + bv_ref[...]).astype(BF16)
    q = q * jnp.asarray(0.125, BF16)
    q_ref[...] = q
    k_ref[...] = k
    v_ref[...] = v
    masked_keys = [jnp.where(head_lanes(p, width), km_ref[p], k) for p in range(2)]
    total = jnp.zeros((tokens, width), F32)
    lse = jnp.zeros((tokens, 128), F32)
    for h in range(GROUP):
        p = spare_head(h)
        mine = head_lanes(h, width)
        scores = rows_by_rows(jnp.where(mine, q, qm_ref[p]), masked_keys[p])
        top = jnp.max(scores, axis=1, keepdims=True)
        e = jnp.exp(scores - top)
        denominator = jnp.sum(e, axis=1, keepdims=True)
        part = rows_by_cols(e.astype(BF16), v) * (1.0 / denominator)
        total = jnp.where(mine, part, total)
        lse = jnp.where(lane_ids(128) == h, top + jnp.log(denominator), lse)
    att_ref[...] = total.astype(BF16)
    lse_ref[0] = lse


def out_kernel(slots, s_ref, att_ref, act_ref, time_ref, bias_ref, gain_ref, shift_ref, *refs):
    w, (res_ref, mlp_ref, rel_ref) = refs[:BLOCKS], refs[BLOCKS:]
    by_block(s_ref, att_ref, rel_ref)
    x = resid_zero_of(s_ref, act_ref[...], time_ref[...], 0, slots)
    x = x + rows_by_cols(rel_ref[...], rows_of(w)) + bias_ref[...]
    res_ref[...] = x
    normal, _ = normalize(x)
    mlp_ref[...] = (normal * gain_ref[...] + shift_ref[...]).astype(BF16)


def up_kernel(s_ref, x_ref, bias_ref, *refs):
    w, (act_ref, slope_ref, rel_ref) = refs[:BLOCKS], refs[BLOCKS:]

    @pl.when(pl.program_id(0) == 0)
    def _():
        by_block(s_ref, x_ref, rel_ref)

    pre = rows_by_cols(rel_ref[...], rows_of(w)) + bias_ref[...]
    cdf = 0.5 + 0.5 * lax.erf(pre * 0.7071067811865476)
    density = 0.3989422804014327 * jnp.exp(-0.5 * pre * pre)
    act_ref[...] = (pre * cdf).astype(BF16)
    slope_ref[...] = (cdf + pre * density).astype(BF16)


def down_copies(refs, held_ref, sems):
    return [(n // 2, pltpu.make_async_copy(ref, held_ref.at[n], sems.at[n])) for n, ref in enumerate(refs)]


def fetch_down(step, copies):
    @pl.when(step == 0)
    def _():
        for _, copy in copies:
            copy.start()

    for chip in range(CHIPS):

        @pl.when(step == chip)
        def _():
            for owner, copy in copies:
                if owner == chip:
                    copy.wait()


def halves_of(s_ref, width):
    core = s_ref[0] % 2
    return [pl.ds(pl.multiple_of(at * width, 128), width) for at in (core, 1 - core)]


def down_kernel(slots, s_ref, a_ref, res_ref, bias_ref, *refs):
    w, (out_ref, acc_ref, held_ref, sems) = refs[:BLOCKS], refs[BLOCKS:]
    c = pl.program_id(0)
    fetch_down(c, down_copies(w, held_ref, sems))

    @pl.when(c == 0)
    def _():
        acc_ref[...] = res_ref[...] + bias_ref[...]

    for n, at in enumerate(halves_of(s_ref, held_ref.shape[1])):
        acc_ref[...] += rows_by_cols(a_ref[:, at], held_ref[2 * c + n])

    @pl.when(c == pl.num_programs(0) - 1)
    def _():
        valid = row_ids(out_ref.shape[0]) < s_ref[ENDS_AT + slots - 1]
        out_ref[...] = jnp.where(valid, acc_ref[...], 0.0).astype(BF16)


def branch_kernel(slots, s_ref, cot_ref, branch_ref, bias_ref):
    valid = row_ids(cot_ref.shape[0]) < s_ref[ENDS_AT + slots - 1]
    branch = jnp.where(valid, cot_ref[...].astype(F32), 0.0)
    branch_ref[...] = branch.astype(BF16)
    bias_ref[...] = jnp.sum(branch, axis=0, keepdims=True)


def mlp_back_kernel(s_ref, branch_ref, slope_ref, res_ref, gain_ref, *refs):
    down, up = refs[:BLOCKS], refs[BLOCKS : 2 * BLOCKS]
    pre_ref, bias_ref, dres_ref, datt_ref, sums_ref, acc_ref, grad_ref, held_ref, sems = refs[2 * BLOCKS :]
    c = pl.program_id(0)
    fetch_down(c, down_copies(down, held_ref, sems))

    @pl.when(c == 0)
    def _():
        acc_ref[...] = jnp.zeros_like(acc_ref)

    branch = branch_ref[...]
    for n, at in enumerate(halves_of(s_ref, held_ref.shape[1])):
        d_pre = (rows_by_rows(branch, held_ref[2 * c + n]) * slope_ref[:, at].astype(F32)).astype(BF16)
        pre_ref[:, at] = d_pre
        bias_ref[:, at] = jnp.sum(d_pre.astype(F32), axis=0, keepdims=True)
        acc_ref[...] += rows_by_rows(d_pre, rows_of(up, at))

    @pl.when(c == pl.num_programs(0) - 1)
    def _():
        by_block(s_ref, acc_ref, grad_ref, back=True)
        grad = grad_ref[...]
        normal, inverse = normalize(res_ref[...])
        d_res = branch.astype(F32) + normalize_back(grad, normal, inverse, gain_ref[...])
        dres_ref[...] = d_res
        d_att = d_res.astype(BF16)
        datt_ref[...] = d_att
        sums_ref[0:1, :] = jnp.sum(grad * normal, axis=0, keepdims=True)
        sums_ref[1:2, :] = jnp.sum(grad, axis=0, keepdims=True)
        sums_ref[2:3, :] = jnp.sum(d_att.astype(F32), axis=0, keepdims=True)
        sums_ref[3:8, :] = jnp.zeros((5, sums_ref.shape[1]), F32)


def three_lanes(x, p, slots):
    first = x.astype(BF16)
    rest = x - first.astype(F32)
    second = rest.astype(BF16)
    third = (rest - second.astype(F32)).astype(BF16)
    at = lane_ids(64 * GROUP) - 64 * p - slots - 1
    spread = jnp.where(at == 0, first, jnp.where(at == 1, second, third))
    return jnp.where((at >= 0) & (at < 3), spread, jnp.zeros((), BF16))


def attention_back_kernel(slots, s_ref, d_ref, q_ref, k_ref, v_ref, lse_ref, cos_ref, sin_ref, *refs):
    w, (out_ref, sums_ref, qm_ref, km_ref, dq_ref, dk_ref, dv_ref, heads_ref) = refs[:BLOCKS], refs[BLOCKS:]
    tokens, width = q_ref.shape
    step = pl.program_id(0)

    @pl.when(pl.program_id(0) == 0)
    def _():
        mask_lanes(s_ref, tokens, width, slots, qm_ref, km_ref)

    for chip, pieces in enumerate((w[0:2], w[2:4], w[4:6], w[6:8])):

        @pl.when(step == chip)
        def _():
            both = rows_by_rows(d_ref[...], rows_of(pieces)).astype(BF16)
            for n, at in enumerate(halves_of(s_ref, width // 2)):
                heads_ref[:, at] = both[:, n * (width // 2) : (n + 1) * (width // 2)]

    d_heads = heads_ref[...]
    q, k, v = q_ref[...], k_ref[...], v_ref[...]
    for h in range(GROUP):
        p = spare_head(h)
        mine, spare = head_lanes(h, width), head_lanes(p, width)
        queries = jnp.where(spare, qm_ref[p] + three_lanes(-lse_ref[0, :, h : h + 1], p, slots), q)
        soft = jnp.exp(rows_by_rows(jnp.where(mine, k, km_ref[p]), queries))
        product = soft * rows_by_rows(jnp.where(mine, v, jnp.zeros((), BF16)), d_heads)
        row_terms = jnp.sum(product, axis=0, keepdims=True)
        d_scores = (product - soft * row_terms).astype(BF16)
        d_v = rows_by_cols(soft.astype(BF16), d_heads)
        d_k = rows_by_cols(d_scores, q)
        d_q = cols_by_cols(d_scores, k)
        if h == 0:
            dq_ref[...], dk_ref[...], dv_ref[...] = d_q, d_k, d_v
        else:
            dq_ref[...] = jnp.where(mine, d_q, dq_ref[...])
            dk_ref[...] = jnp.where(mine, d_k, dk_ref[...])
            dv_ref[...] = jnp.where(mine, d_v, dv_ref[...])
    cosine, sine = cos_ref[...], sin_ref[...]
    sums_ref[...] = jnp.zeros_like(sums_ref)
    parts = (turn(dq_ref[...] * 0.125, cosine, -sine), turn(dk_ref[...], cosine, -sine), dv_ref[...])
    for i, part in enumerate(parts):
        part = part.astype(BF16)
        out_ref[i] = part
        sums_ref[i : i + 1, :] = jnp.sum(part.astype(F32), axis=0, keepdims=True)


def d_input_kernel(slots, s_ref, d_ref, act_ref, time_ref, gain_ref, dres_ref, *refs):
    w, (out_ref, sums_ref, acc_ref, grad_ref) = refs[:BLOCKS], refs[BLOCKS:]
    j = pl.program_id(0)

    @pl.when(j == 0)
    def _():
        acc_ref[...] = jnp.zeros_like(acc_ref)

    acc_ref[...] += rows_by_rows(d_ref[0], rows_of(w))

    @pl.when(j == pl.num_programs(0) - 1)
    def _():
        by_block(s_ref, acc_ref, grad_ref, back=True)
        grad = grad_ref[...]
        normal, inverse = normalize(resid_zero_of(s_ref, act_ref[...], time_ref[...], 0, slots))
        d_in = dres_ref[...] + normalize_back(grad, normal, inverse, gain_ref[...])
        out_ref[...] = d_in.astype(BF16)
        sums_ref[...] = jnp.zeros_like(sums_ref)
        sums_ref[0:1, :] = jnp.sum(grad * normal, axis=0, keepdims=True)
        sums_ref[1:2, :] = jnp.sum(grad, axis=0, keepdims=True)
        for slot, inside in enumerate(members_of(s_ref, row_ids(act_ref.shape[0]), slots)):
            sums_ref[2 + slot : 3 + slot, :] = jnp.sum(jnp.where(inside, d_in, 0.0), axis=0, keepdims=True)


def grad_kernel(steps, sources, groups, s_ref, *refs):
    per = 5 * sources
    outs = refs[per * len(steps) :]
    i = pl.program_id(0)
    first = 0
    for n, (count, lead) in enumerate(steps):
        mine = refs[per * n : per * (n + 1)]

        @pl.when((i >= first) & (i < first + count))
        def _():
            product = None
            for source in range(sources):
                *a_refs, b_ref = mine[5 * source : 5 * source + 5]
                a = jnp.concatenate([ref[...] for ref in a_refs], axis=1)
                part = cols_by_cols(a, b_ref[0] if lead else b_ref[...])
                product = part if product is None else product + part
            rows = product.shape[0] // 4
            for out, group in zip(outs, groups):
                out[...] = product[group[0] * rows : (group[-1] + 1) * rows].astype(BF16)

        first += count


def weight_grad(scalars, odd, pairs, tile, after=(), groups=((0,), (1,), (2, 3))):
    tokens, width = pairs[0][0].shape[0], pairs[0][0].shape[1] // BLOCKS
    sources = len(pairs[0]) // 2
    specs, inputs, steps = [], [], []
    first = 0
    for pair in pairs:
        lead = pair[1].ndim == 3
        per = pair[1].shape[-1] // tile
        count = per * (pair[1].shape[0] if lead else 1)

        def local(i, first=first, count=count):
            return jnp.clip(i - first, 0, count - 1)

        for a, b in zip(pair[::2], pair[1::2]):
            for j in range(4):
                specs.append(pl.BlockSpec((tokens, width), lambda i, s, j=j: (0, s[2 * j + odd])))
                inputs.append(a)
            if lead:
                specs.append(
                    pl.BlockSpec((1, tokens, tile), lambda i, s, at=local, per=per: (at(i) // per, 0, at(i) % per))
                )
            else:
                specs.append(pl.BlockSpec((tokens, tile), lambda i, s, at=local: (0, at(i))))
            inputs.append(b)
        steps.append((count, lead))
        first += count
    sizes = [len(group) * width for group in groups]
    out = call(
        partial(grad_kernel, tuple(steps), sources, groups), scalars, inputs, specs,
        [jax.ShapeDtypeStruct((rows, first * tile), BF16) for rows in sizes],
        [pl.BlockSpec((rows, tile), lambda i, s: (0, i)) for rows in sizes], (first,), after=after,
    )
    return list(out)


def pack_grads_kernel(slots, s_ref, one_ref, qkv_ref, two_ref, up_ref, down_ref, time_ref, odd_ref, even_ref):
    rows = time_ref.shape[0] // BLOCKS
    d_time = one_ref[2 : 2 + slots, :]
    one, two = d_time.shape[1] // BLOCKS, 2 * d_time.shape[1] // BLOCKS
    ff = up_ref.shape[1] // BLOCKS
    odd_ref[...] = jnp.zeros_like(odd_ref)
    even_ref[...] = jnp.zeros_like(even_ref)
    for j in range(BLOCKS):
        block = s_ref[j]
        out, chip = (odd_ref, (0, 2, 1, 3)[j // 2]) if j % 2 else (even_ref, j // 2)
        features = time_ref[pl.ds(pl.multiple_of(block * rows, 8), rows), :]
        out[chip, 0:rows, :] = sum(features[:, s : s + 1] * d_time[s : s + 1, :] for s in range(slots)).astype(BF16)
        at = pl.ds(pl.multiple_of(block * one, 128), one)
        sources = (one_ref[0:1, at], one_ref[1:2, at], two_ref[2:3, at], two_ref[0:1, at], two_ref[1:2, at],
                   down_ref[0:1, at], qkv_ref[2:3, at])
        line = jnp.concatenate(sources, axis=1)
        out[chip, rows : rows + 1, 0 : line.shape[1]] = line.astype(BF16)
        wide = pl.ds(pl.multiple_of((block % 4) * two, 128), two)
        pair = jnp.where(block < 4, qkv_ref[0:1, wide], qkv_ref[1:2, wide])
        hidden = up_ref[0:1, pl.ds(pl.multiple_of(block * ff, 128), ff)]
        out[chip, rows + 1 : rows + 2, 0 : two + ff] = jnp.concatenate([pair, hidden], axis=1).astype(BF16)
        bias = jnp.sum(one_ref[2 : 2 + slots, at], axis=0, keepdims=True)
        out[chip, rows + 2 : rows + 3, 0:one] = bias.astype(BF16)


def per_device(
    n_dp, n_fsdp, activations, time_features, lengths, attn_gain, attn_shift, qkv_weight, qkv_bias, out_weight, out_bias,
    mlp_gain, mlp_shift, up_weight, up_bias, down_weight, down_bias, time_weight, time_bias, cotangent,
):
    tokens, width = activations.shape
    slots = lengths.shape[1]
    hidden = down_weight.shape[0] * n_fsdp
    small = n_fsdp == BLOCKS
    me = lax.axis_index("fsdp")
    blocks = jnp.arange(BLOCKS, dtype=jnp.int32)
    chips = jnp.arange(CHIPS, dtype=jnp.int32)
    if small:
        turned = jnp.where(chips % 3 > 0, 3 - chips, chips)
        chips = jnp.where(me % 2 == 0, turned, chips)
        blocks = (2 * chips[:, None] + jnp.arange(2, dtype=jnp.int32)[None, :]).reshape(-1) ^ me
        chips = chips ^ (me // 2)
    upto = jnp.arange(slots)[:, None] >= jnp.arange(slots)[None, :]
    ends = jnp.sum(jnp.where(upto, lengths, 0), axis=1)
    parity = lax.axis_index("dp") % 2
    scalars = jnp.concatenate([blocks, chips, parity[None], ends]).astype(jnp.int32)

    def swap(x, even, odd):
        return lax.ppermute(x, "fsdp", [(i, i ^ (odd if i % 2 else even)) for i in range(n_fsdp)])

    def sibling(x):
        return swap(x, 1, 1)

    def first_way(x):
        return swap(x, 4, 2)

    def second_way(x):
        return swap(x, 2, 4)

    def pieces(own, first, second, far, own_sibling, first_sibling, second_sibling, far_sibling):
        return [own, own_sibling, first, second_sibling, second, first_sibling, far, far_sibling]

    def add(*parts):
        total = parts[0].astype(F32)
        for part in parts[1:]:
            total = total + part.astype(F32)
        return total.astype(BF16)

    def gather_rows(w):
        return lax.all_gather(w, "fsdp", axis=0, tiled=True).reshape(BLOCKS, -1, w.shape[1])

    rows = whole((tokens, width))
    line = whole((1, width))
    vectors = [attn_gain, attn_shift, out_bias, mlp_gain, mlp_shift, down_bias, time_bias, qkv_bias, up_bias]
    per = width // BLOCKS
    qkv_columns = qkv_weight.shape[1]
    columns = qkv_columns + width
    depth = 16
    if small:
        sources = [qkv_weight, out_weight, time_weight] + vectors
        pack = call(
            pack_kernel, scalars, sources, [whole(x.shape) for x in sources],
            jax.ShapeDtypeStruct((per + depth, columns), BF16), whole((per + depth, columns)), (1,),
        )
        first_one, first_two, first_core = first_way(pack), second_way(pack), sibling(pack)
        up_own, down_own = copy_after(up_weight, pack), copy_after(down_weight, pack)
    else:
        gathered = [lax.all_gather(v, "fsdp", axis=0, tiled=True).reshape(BLOCKS, -1) for v in vectors]
        matrices = jnp.concatenate([gather_rows(qkv_weight), gather_rows(out_weight)], axis=2)
        times = lax.all_gather(time_weight, "fsdp", axis=0, tiled=True).reshape(BLOCKS, 2, depth, width)
        lines = jnp.concatenate(gathered, axis=1)
        lines = jnp.pad(lines, ((0, 0), (0, columns - 2 * width - lines.shape[1])))[:, None]
        lines = jnp.pad(lines, ((0, 0), (0, depth - 1), (0, 0)))
        extra = jnp.concatenate([times[:, 0], times[:, 1], lines], axis=2)
        first = list(jnp.concatenate([matrices, extra], axis=1))
        up_rel = list(gather_rows(up_weight))
        down_rel = list(gather_rows(down_weight))

    ids = jnp.arange(tokens, dtype=jnp.int32)[:, None]
    starts = ends - lengths[0]
    inside = (ids >= starts[None, :]) & (ids < ends[None, :])
    position = (ids[:, 0] - jnp.sum(jnp.where(inside, starts[None, :], 0), axis=1)).astype(F32)
    frequency = 10000.0 ** (-2.0 * jnp.arange(32, dtype=F32) / 64)
    angles = position[:, None] * frequency[None, :]
    cosine, sine = jnp.cos(angles), jnp.sin(angles)
    lanes = 64 * GROUP
    cos_table = jnp.tile(cosine, (1, 2 * GROUP))
    sin_table = jnp.tile(jnp.concatenate([-sine, sine], axis=1), (1, GROUP))

    d_branch, down_bias_sum = call(
        partial(branch_kernel, slots), scalars, [cotangent], [rows],
        [jax.ShapeDtypeStruct((tokens, width), BF16), jax.ShapeDtypeStruct((1, width), F32)], [rows, line], (1,),
    )
    if small:
        first_one, first_two = next_round(
            scalars, [first_one, first_two], [first_core, d_branch, up_own, down_own, cos_table, sin_table]
        )
        first_far = second_way(first_one)
        core_one, core_two, branch_core = sibling(first_one), sibling(first_two), sibling(d_branch)
        first_far, up_own = next_round(scalars, [first_far, up_own], [core_one, core_two, branch_core])
        up_one, up_two = first_way(up_own), second_way(up_own)
        first = pieces(pack, first_one, first_two, first_far, first_core, core_one, core_two, sibling(first_far))
    spread = time_features.reshape(slots, 2 * BLOCKS, -1)
    spread = jnp.pad(spread, ((0, 0), (0, 0), (0, 128 - spread.shape[2]))).reshape(slots, -1)
    extra_specs = [pl.BlockSpec((depth, columns), lambda i, s: (per // depth, 0))] * BLOCKS
    attn_in, time_rows, lines, qkv_b, up_b = call(
        partial(norm_one_kernel, slots), scalars, [activations, spread] + first,
        [rows, whole(spread.shape)] + extra_specs,
        [jax.ShapeDtypeStruct((tokens, width), BF16), jax.ShapeDtypeStruct((slots, width), F32),
         jax.ShapeDtypeStruct((8, width), F32), jax.ShapeDtypeStruct((1, qkv_columns), F32),
         jax.ShapeDtypeStruct((1, hidden), F32)],
        [rows, whole((slots, width)), whole((8, width)), whole((1, qkv_columns)), whole((1, hidden))], (1,),
        after=(d_branch,),
    )
    gain_one, shift_one, out_b, gain_two, shift_two, down_b = [lines[i : i + 1] for i in range(6)]
    groups = H // GROUP
    col = pl.BlockSpec((tokens, lanes), lambda g, s: (0, g))
    table = whole((tokens, lanes))
    mask_rooms = [pltpu.VMEM((2, tokens, lanes), BF16)] * 2
    qkv_specs = []
    for o in range(3):
        qkv_specs += piece_specs(per, lanes, lambda g, s, o=o: o * groups + g)
    queries, keys, values, attended, lse = call(
        partial(attention_kernel, slots), scalars,
        [attn_in, qkv_b, qkv_b, qkv_b, cos_table, sin_table] + first * 3,
        [rows] + [pl.BlockSpec((1, lanes), lambda g, s, o=o: (0, o * groups + g)) for o in range(3)]
        + [table, table] + qkv_specs,
        [jax.ShapeDtypeStruct((tokens, width), BF16)] * 4 + [jax.ShapeDtypeStruct((groups, tokens, 128), F32)],
        [col, col, col, col, pl.BlockSpec((1, tokens, 128), lambda g, s: (g, 0, 0))],
        (groups,), [pltpu.VMEM((tokens, width), BF16)] + mask_rooms)
    if small:
        up_one, up_two, up_own = next_round(scalars, [up_one, up_two, up_own], [attended])
        up_far = second_way(up_one)
        up_core, core_one, core_two = sibling(up_own), sibling(up_one), sibling(up_two)
        wait = (up_one,)
    else:
        wait = ()
    out_specs = piece_specs(per, width, lambda *a: qkv_columns // width)
    resid_one, mlp_in = call(
        partial(out_kernel, slots), scalars,
        [attended, activations, time_rows, out_b, gain_two, shift_two] + first,
        [rows, rows, whole((slots, width)), line, line, line] + out_specs,
        [jax.ShapeDtypeStruct((tokens, width), F32), jax.ShapeDtypeStruct((tokens, width), BF16)],
        [rows, rows], (1,), [pltpu.VMEM((tokens, width), BF16)], after=wait,
    )
    if small:
        up_far, down_own = next_round(scalars, [up_far, down_own], [core_one, core_two, up_core, mlp_in])
        up_rel = pieces(up_own, up_one, up_two, up_far, up_core, core_one, core_two, sibling(up_far))
        down_one, down_two, down_core = first_way(down_own), second_way(down_own), sibling(down_own)
        attn_in_core = sibling(attn_in)
    tile = hidden // CHIPS
    wide = pl.BlockSpec((tokens, tile), lambda i, s: (0, i))
    activated, slope = call(
        up_kernel, scalars, [mlp_in, up_b] + up_rel,
        [rows, pl.BlockSpec((1, tile), lambda i, s: (0, i))] + piece_specs(per, tile, lambda i, s: i),
        [jax.ShapeDtypeStruct((tokens, hidden), BF16)] * 2, [wide, wide], (CHIPS,),
        [pltpu.VMEM((tokens, width), BF16)])

    even_z = parity == 0

    def swap_z(x, bit):
        return lax.ppermute(x, "dp", [(i, i ^ bit) for i in range(n_dp)])

    def sum_of(*arrays, row=0, column=0, rows=None, columns=None):
        shape = arrays[0].shape
        return [(x, row, column) for x in arrays], rows or shape[0], columns or shape[1]

    def halves(*parts):
        half = parts[0].shape[0] // 2
        low, high = add(*[x[:half] for x in parts]), add(*[x[half:] for x in parts])
        return jnp.where(even_z, low, high), jnp.where(even_z, high, low)

    def quarters(*parts):
        size = parts[0].shape[0] // 4
        place = lax.axis_index("dp")
        cuts = [[lax.dynamic_slice_in_dim(x, (place ^ bits) * size, size) for x in parts] for bits in range(4)]
        return [add(*cut) for cut in cuts]

    def exchange(parts):
        return [swap_z(x, bits) for x, bits in zip(parts, (1, 2, 3))]

    def sum_four(own, came):
        one, two, three = [x.astype(F32) for x in came]
        return ((own.astype(F32) + one) + (two + three)).astype(BF16)

    def in_place(own, came):
        four = jnp.stack([own, *came]).reshape(2, 2, *own.shape)
        place = lax.axis_index("dp")
        for axis, bit in ((0, 2), (1, 1)):
            four = jnp.where((place & bit) > 0, jnp.flip(four, axis), four)
        return four.reshape(-1, own.shape[1]).astype(F32)

    def joined(own, other):
        return jnp.where(even_z, jnp.concatenate([own, other]), jnp.concatenate([other, own])).astype(F32)

    def rows_of_all(pairs, tile):
        blocks = [weight_grad(scalars, odd, pairs, tile) for odd in range(2)]
        blocks = [jnp.concatenate(x).reshape(CHIPS, -1, x[0].shape[1]) for x in blocks]
        both = jnp.stack(blocks, axis=1).reshape(-1, blocks[0].shape[2])
        return lax.psum(lax.psum_scatter(both, "fsdp", scatter_dimension=0, tiled=True), "dp").astype(F32)

    if small:
        down_one, down_two, activated = next_round(scalars, [down_one, down_two, activated], [down_core, attn_in_core])
        down_far = second_way(down_one)
        core_one, core_two, activated_core = sibling(down_one), sibling(down_two), sibling(activated)
        down_parts = weight_grad(scalars, 0, [(activated, d_branch, activated_core, branch_core)], 512)
        down_far, down_parts[2] = next_round(scalars, [down_far, down_parts[2]], [core_one, core_two])
        down_came = second_way(down_parts[2])
        down_rel = pieces(down_own, down_one, down_two, down_far, down_core, core_one, core_two, sibling(down_far))
        mlp_in_core = sibling(mlp_in)
    else:
        down_grad = rows_of_all([(activated, d_branch)], 512)

    chip_wide = pl.BlockSpec((tokens, tile), lambda i, s: (0, s[CHIP_AT + i]))
    down_rooms = [pltpu.VMEM((BLOCKS, hidden // BLOCKS, width), BF16), pltpu.SemaphoreType.DMA((BLOCKS,))]
    d_pre, up_bias_sum, d_resid_one, d_attn, sums_two = call(
        mlp_back_kernel, scalars, [d_branch, slope, resid_one, gain_two] + down_rel + up_rel,
        [rows, chip_wide, rows, line] + [pl.BlockSpec(memory_space=pl.ANY)] * BLOCKS
        + piece_specs(per, tile, lambda i, s: s[CHIP_AT + i]),
        [jax.ShapeDtypeStruct((tokens, hidden), BF16),
         jax.ShapeDtypeStruct((1, hidden), F32), jax.ShapeDtypeStruct((tokens, width), F32),
         jax.ShapeDtypeStruct((tokens, width), BF16), jax.ShapeDtypeStruct((8, width), F32)],
        [chip_wide, pl.BlockSpec((1, tile), lambda i, s: (0, s[CHIP_AT + i])), rows, rows, whole((8, width))],
        (CHIPS,), [pltpu.VMEM((tokens, width), F32)] * 2 + down_rooms,
    )
    def layer_output(after):
        return call(
            partial(down_kernel, slots), scalars, [activated, resid_one, down_b] + down_rel,
            [chip_wide, rows, line] + [pl.BlockSpec(memory_space=pl.ANY)] * BLOCKS,
            jax.ShapeDtypeStruct((tokens, width), BF16), rows, (CHIPS,), [pltpu.VMEM((tokens, width), F32)] + down_rooms,
            after=after,
        )

    if small:
        d_pre, d_attn, down_came = next_round(scalars, [d_pre, d_attn, down_came], [mlp_in_core])
        d_pre_core, d_attn_core, attended_core = sibling(d_pre), sibling(d_attn), sibling(attended)
        far = down_came.shape[0] // 2
        down_one = first_way(add(down_parts[1], down_came[far:]))
        up_parts = weight_grad(
            scalars, 0, [(mlp_in, d_pre, mlp_in_core, d_pre_core), (attended, d_attn, attended_core, d_attn_core)], width
        )
        up_parts[2], down_came, down_one = next_round(scalars, [up_parts[2], down_came, down_one])
        up_came = second_way(up_parts[2])
        down_sum, *down_send = quarters(down_parts[0], down_came[:far], down_one)
        down_z = exchange(down_send)
        wait = (down_came,)
    else:
        up_out_grad = rows_of_all([(mlp_in, d_pre), (attended, d_attn)], width)
        up_grad, out_grad = up_out_grad[:, :hidden], up_out_grad[:, hidden:]
        wait = ()
    chip_col = pl.BlockSpec((tokens, lanes), lambda g, s: (0, s[CHIP_AT + g]))
    d_qkv, sums_qkv = call(
        partial(attention_back_kernel, slots), scalars,
        [d_attn, queries, keys, values, lse, cos_table, sin_table] + first,
        [rows, chip_col, chip_col, chip_col,
         pl.BlockSpec((1, tokens, 128), lambda g, s: (s[CHIP_AT + g], 0, 0)), table, table] + out_specs,
        [jax.ShapeDtypeStruct((3, tokens, width), BF16), jax.ShapeDtypeStruct((8, width), F32)],
        [pl.BlockSpec((3, tokens, lanes), lambda g, s: (0, 0, s[CHIP_AT + g])),
         pl.BlockSpec((8, lanes), lambda g, s: (0, s[CHIP_AT + g]))],
        (groups,), mask_rooms + [pltpu.VMEM((tokens, lanes), F32)] * 3 + [pltpu.VMEM((tokens, lanes), BF16)],
        after=wait,
    )
    if small:
        d_qkv, up_came, *down_z = next_round(scalars, [d_qkv, up_came, *down_z])
        d_qkv_core = sibling(d_qkv)
        up_one = first_way(add(up_parts[1], up_came[per:]))
        down_sum = sum_four(down_sum, down_z)
        down_z = exchange([down_sum] * 3)
    else:
        qkv_grad = rows_of_all([(attn_in, d_qkv)], width)
    input_grad, sums_one = call(
        partial(d_input_kernel, slots), scalars,
        [d_qkv, activations, time_rows, gain_one, d_resid_one] + first,
        [pl.BlockSpec((1, tokens, width), lambda i, s: (i, 0, 0)), rows, whole((slots, width)), line, rows]
        + piece_specs(per, width, lambda i, s: i),
        [jax.ShapeDtypeStruct((tokens, width), BF16), jax.ShapeDtypeStruct((8, width), F32)],
        [rows, whole((8, width))], (3,), [pltpu.VMEM((tokens, width), F32)] * 2,
    )
    if small:
        qkv_parts = weight_grad(scalars, 0, [(attn_in, d_qkv, attn_in_core, d_qkv_core)], width, after=(sums_one,))
        qkv_parts[2], up_came, up_one, sums_one = next_round(scalars, [qkv_parts[2], up_came, up_one, sums_one], down_z)
        qkv_came = second_way(qkv_parts[2])
        up_sum, up_send = halves(up_parts[0], up_came[:per], up_one)
        up_z = swap_z(up_send, 1)
        time_cols = time_features.astype(F32).T
        depth = 64
        v_odd, v_even = call(
            partial(pack_grads_kernel, slots), scalars,
            [sums_one, sums_qkv, sums_two, up_bias_sum, down_bias_sum, time_cols],
            [whole((8, width)), whole((8, width)), whole((8, width)), whole((1, hidden)), line, whole(time_cols.shape)],
            [jax.ShapeDtypeStruct((4, depth, width), BF16)] * 2, [whole((4, depth, width))] * 2, (1,),
        )
        v_odd, v_even = v_odd.reshape(-1, width), v_even.reshape(-1, width)
        v_came = sibling(v_odd)
        to_one, up_sum, *parts = next_round(
            scalars, [], [],
            [([(qkv_parts[1], 0, 0), (qkv_came, per, 0)], per, qkv_columns), sum_of(up_sum, up_z)]
            + [sum_of(v_even, v_came, row=k * depth, rows=depth) for k in range(4)],
        )
        qkv_one = first_way(to_one)
        up_z = swap_z(up_sum, 2)
        qkv_one, *parts = next_round(scalars, [qkv_one, *parts])
        qkv_sum, qkv_send = halves(qkv_parts[0], qkv_came[:per], qkv_one)
        qkv_z = swap_z(qkv_send, 1)
        v_came = [first_way(parts[1]), second_way(parts[2]), swap(parts[3], 6, 6)]
        down_sum, qkv_sum, up_sum, part = next_round(
            scalars, [down_sum], [], [sum_of(qkv_sum, qkv_z), sum_of(up_sum, up_z), sum_of(parts[0], *v_came)]
        )
        wait = (part,)
        qkv_z = swap_z(qkv_sum, 2)
        up_z = swap_z(up_sum, 1)
        v_came = swap_z(part, 1)
        output = layer_output(wait)
        down_grad = in_place(down_sum, down_z)
        qkv_z, v_came = next_round(scalars, [qkv_z, v_came], [output])
        qkv_sum = add(qkv_sum, qkv_z)
        qkv_grad = joined(qkv_sum, swap_z(qkv_sum, 1))
        part = add(part, v_came)
        share = part.astype(F32) + swap_z(part, 2).astype(F32)
        up_out_grad = joined(up_sum, up_z)
        up_grad, out_grad = up_out_grad[:, :hidden], up_out_grad[:, hidden:]
        time_rows_here = time_weight.shape[0]
        time_grad = share[:time_rows_here]
        one, two, ff = width // BLOCKS, 2 * width // BLOCKS, hidden // BLOCKS
        row = share[time_rows_here]
        (gain_one_grad, shift_one_grad, out_bias_grad, gain_two_grad, shift_two_grad, down_bias_grad,
         value_bias_grad) = [row[i * one : (i + 1) * one] for i in range(7)]
        row = share[time_rows_here + 1]
        qk_bias_grad, up_bias_grad = row[:two], row[two : two + ff]
        time_bias_grad = share[time_rows_here + 2, :one]
    else:
        output = layer_output(())
        d_time = sums_one[2 : 2 + slots]
        time_grad = lax.dot_general(
            time_features.astype(F32), d_time, (((0,), (0,)), ((), ())), precision=lax.Precision.HIGHEST
        )
        vector_sums = (
            sums_one[0], sums_one[1], sums_qkv[:2].reshape(-1), sums_qkv[2], sums_two[2], sums_two[0], sums_two[1],
            up_bias_sum[0], down_bias_sum[0], jnp.sum(d_time, axis=0),
        )
        shares = jnp.concatenate(
            [time_grad.reshape(n_fsdp, -1)] + [v.reshape(n_fsdp, -1) for v in vector_sums], axis=1
        )
        sizes = [time_weight.size] + [v.size // n_fsdp for v in vector_sums]
        shares = jnp.pad(shares, ((0, 0), (0, -shares.shape[1] % 4096))).reshape(n_fsdp, -1, 128)
        shares = lax.psum_scatter(shares.astype(BF16), "fsdp", scatter_dimension=0, tiled=False)
        share = lax.psum(shares, "dp").astype(F32).reshape(-1)
        got = []
        at = 0
        for size in sizes:
            got.append(share[at : at + size])
            at += size
        (time_grad, gain_one_grad, shift_one_grad, qk_bias_grad, value_bias_grad, out_bias_grad, gain_two_grad,
         shift_two_grad, up_bias_grad, down_bias_grad, time_bias_grad) = got
    return (
        output, input_grad, gain_one_grad, shift_one_grad, qkv_grad, qk_bias_grad, value_bias_grad, out_grad, out_bias_grad,
        gain_two_grad, shift_two_grad, up_grad, up_bias_grad, down_grad, down_bias_grad,
        time_grad.reshape(time_weight.shape), time_bias_grad,
    )


def solution(mesh):
    tokens = P(("dp", "fsdp"), None)
    vector = P("fsdp")
    matrix = P("fsdp", None)
    in_specs = (
        tokens, tokens, tokens, vector, vector, matrix, vector, matrix, vector, vector, vector, matrix, vector, matrix,
        vector, matrix, vector, tokens,
    )
    out_specs = (
        tokens, tokens, vector, vector, matrix, vector, vector, matrix, vector, vector, vector, matrix, vector, matrix,
        vector, matrix, vector,
    )
    body = partial(per_device, mesh.shape["dp"], mesh.shape["fsdp"])
    return jax.shard_map(body, mesh=mesh, in_specs=in_specs, out_specs=out_specs, check_vma=False)
```

```python
from functools import partial

import jax
import jax.numpy as jnp
from jax import lax
from jax.experimental import pallas as pl
from jax.experimental.pallas import tpu as pltpu
from jax.sharding import PartitionSpec as P

H = 16
GROUP = 4
BLOCKS = 8
CHIPS = 4
CHIP_AT = BLOCKS
PARITY_AT = CHIP_AT + CHIPS
ENDS_AT = PARITY_AT + 1
FAR = -1e30
NO_COST = pl.CostEstimate(flops=0, bytes_accessed=0, transcendentals=0)
SOME_COST = pl.CostEstimate(flops=30 * 10**9, bytes_accessed=100 * 10**6, transcendentals=0)
F32 = jnp.float32
BF16 = jnp.bfloat16


def rows_by_cols(a, b):
    return lax.dot_general(a, b, (((1,), (0,)), ((), ())), preferred_element_type=F32)


def rows_by_rows(a, b):
    return lax.dot_general(a, b, (((1,), (1,)), ((), ())), preferred_element_type=F32)


def cols_by_cols(a, b):
    return lax.dot_general(a, b, (((0,), (0,)), ((), ())), preferred_element_type=F32)


def call(kernel, scalars, inputs, in_specs, out_shapes, out_specs, grid, scratch=(), aliases=None, after=(), cost=NO_COST):
    count = len(inputs)

    def body(s_ref, *refs):
        kernel(s_ref, *refs[:count], *refs[count + len(after) :])

    return pl.pallas_call(
        body,
        name=getattr(kernel, "func", kernel).__name__,
        grid_spec=pltpu.PrefetchScalarGridSpec(
            num_scalar_prefetch=1,
            grid=grid,
            in_specs=list(in_specs) + [pl.BlockSpec(memory_space=pl.ANY)] * len(after),
            out_specs=out_specs,
            scratch_shapes=list(scratch),
        ),
        out_shape=out_shapes,
        input_output_aliases=aliases or {},
        compiler_params=pltpu.CompilerParams(
            dimension_semantics=("arbitrary",) * len(grid), vmem_limit_bytes=64 * 2**20
        ),
        cost_estimate=cost,
    )(scalars, *inputs, *after)


def round_kernel(counts, s_ref, *refs):
    outs = refs[-len(counts) :] if counts else ()
    at = 0
    for count, out in zip(counts, outs):
        total = refs[at][...].astype(F32)
        for ref in refs[at + 1 : at + count]:
            total = total + ref[...].astype(F32)
        out[...] = total.astype(BF16)
        at += count


def next_round(scalars, passed, others=(), sums=()):
    anywhere = pl.BlockSpec(memory_space=pl.ANY)
    steps = 2
    specs, inputs, counts, shapes, out_specs = [], [], [], [], []
    for parts, rows, columns in sums:
        size = rows // steps
        for array, row, column in parts:
            even, odd = row if isinstance(row, tuple) else (row, row)

            def at(i, s, even=even // size, odd=odd // size, column=column // columns):
                return (i + even + s[PARITY_AT] * (odd - even), column)

            specs.append(pl.BlockSpec((size, columns), at))
            inputs.append(array)
        counts.append(len(parts))
        shapes.append(jax.ShapeDtypeStruct((rows, columns), BF16))
        out_specs.append(pl.BlockSpec((size, columns), lambda i, s: (i, 0)))
    first = len(inputs)

    def kernel(s_ref, *refs):
        given = first + len(passed) + len(others)
        round_kernel(counts, s_ref, *refs[:first], *refs[given + len(passed) :])

    out = pl.pallas_call(
        kernel,
        name="next_round",
        grid_spec=pltpu.PrefetchScalarGridSpec(
            num_scalar_prefetch=1,
            grid=(steps if sums else 1,),
            in_specs=specs + [anywhere] * (len(passed) + len(others)),
            out_specs=[anywhere] * len(passed) + out_specs,
        ),
        out_shape=[jax.ShapeDtypeStruct(x.shape, x.dtype) for x in passed] + shapes,
        input_output_aliases={1 + first + i: i for i in range(len(passed))},
        compiler_params=pltpu.CompilerParams(dimension_semantics=("arbitrary",), vmem_limit_bytes=64 * 2**20),
        cost_estimate=NO_COST,
    )(scalars, *inputs, *passed, *others)
    return list(out)


def copy_after(x, *others):
    def kernel(x_ref, *refs):
        refs[-1][...] = x_ref[...]

    block = pl.BlockSpec((x.shape[0] // 2, x.shape[1]), lambda i: (i, 0))
    return pl.pallas_call(
        kernel,
        grid=(2,),
        out_shape=jax.ShapeDtypeStruct(x.shape, x.dtype),
        in_specs=[block] + [pl.BlockSpec(memory_space=pl.ANY)] * len(others),
        out_specs=block,
        cost_estimate=NO_COST,
    )(x, *others)


def whole(shape):
    zeros = (0,) * len(shape)
    return pl.BlockSpec(shape, lambda *_: zeros)


def normalize(x):
    center = x - jnp.mean(x, axis=-1, keepdims=True)
    variance = jnp.mean(center * center, axis=-1, keepdims=True)
    inverse = lax.rsqrt(variance + 1e-05)
    return center * inverse, inverse


def normalize_back(grad, normal, inverse, gain):
    scaled = grad * gain
    return inverse * (
        scaled
        - jnp.mean(scaled, axis=-1, keepdims=True)
        - normal * jnp.mean(scaled * normal, axis=-1, keepdims=True)
    )


def row_ids(count, first=0):
    return lax.broadcasted_iota(jnp.int32, (count, 1), 0) + first


def members_of(s_ref, ids, slots):
    out = []
    start = 0
    for slot in range(slots):
        end = s_ref[ENDS_AT + slot]
        out.append((ids >= start) & (ids < end))
        start = end
    return out


def segment_of(s_ref, ids, slots):
    segment = jnp.zeros(ids.shape, jnp.int32)
    for slot in range(slots):
        segment = segment + (ids >= s_ref[ENDS_AT + slot]).astype(jnp.int32)
    return segment


def resid_zero_of(s_ref, act, time_rows, first, slots):
    x = act.astype(F32)
    for slot, inside in enumerate(members_of(s_ref, row_ids(act.shape[0], first), slots)):
        x = x + jnp.where(inside, time_rows[slot : slot + 1, :], 0.0)
    return x


def piece_specs(rows, columns, at):
    return [pl.BlockSpec((rows, columns), lambda *a: (0, at(*a)))] * BLOCKS


def rows_of(refs, at=slice(None)):
    return jnp.concatenate([ref[:, at] for ref in refs], axis=0)


def pack_kernel(s_ref, qkv_ref, out_ref, time_ref, *refs):
    vectors, pack_ref = refs[:-1], refs[-1]
    rows, columns = qkv_ref.shape
    pack_ref[0:rows, 0:columns] = qkv_ref[...]
    pack_ref[0:rows, columns:] = out_ref[...]
    depth = pack_ref.shape[0] - rows
    width = out_ref.shape[1]
    pack_ref[rows:, 0:width] = time_ref[0:depth, :]
    pack_ref[rows:, width : 2 * width] = time_ref[depth:, :]
    line = jnp.concatenate([v[...].astype(F32).reshape(1, -1) for v in vectors], axis=1)
    line = jnp.concatenate([line, jnp.zeros((1, pack_ref.shape[1] - 2 * width - line.shape[1]), F32)], axis=1)
    lines = jnp.where(row_ids(depth) == 0, line, 0.0).astype(BF16)
    pack_ref[rows:, 2 * width :] = lines


def norm_one_kernel(slots, s_ref, act_ref, feat_ref, *refs):
    extras = refs[:BLOCKS]
    out_ref, time_ref, lines_ref, qkv_b_ref, up_b_ref = refs[BLOCKS:]
    depth = extras[0].shape[0]
    width = act_ref.shape[1]
    small = width // BLOCKS
    time_rows = jnp.zeros((slots, width), F32)
    for j in range(BLOCKS):
        block = s_ref[j]
        for half in range(2):
            at = pl.multiple_of((block * 2 + half) * 128, 128)
            part = feat_ref[:, pl.ds(at, 128)]
            time_rows = time_rows + rows_by_cols(part[:, 0:depth], extras[j][:, half * width : (half + 1) * width])
        line = extras[j][:, 2 * width :].astype(F32)[0:1]
        at = pl.ds(pl.multiple_of(block * small, 128), small)
        for v in range(7):
            lines_ref[v : v + 1, at] = line[:, v * small : (v + 1) * small]
        first = 7 * small
        for ref in (qkv_b_ref, up_b_ref):
            size = ref.shape[1] // BLOCKS
            ref[0:1, pl.ds(pl.multiple_of(block * size, 128), size)] = line[:, first : first + size]
            first += size
    lines_ref[7:8, :] = jnp.zeros((1, width), F32)
    time_rows = time_rows + lines_ref[6:7, :]
    time_ref[...] = time_rows
    x = resid_zero_of(s_ref, act_ref[...], time_rows, 0, slots)
    normal, _ = normalize(x)
    out_ref[...] = (normal * lines_ref[0:1, :] + lines_ref[1:2, :]).astype(BF16)


def by_block(s_ref, x_ref, out_ref, back=False):
    width = x_ref.shape[1] // BLOCKS
    for j in range(BLOCKS):
        at = pl.ds(pl.multiple_of(s_ref[j] * width, 128), width)
        if back:
            out_ref[:, at] = x_ref[:, j * width : (j + 1) * width]
        else:
            out_ref[:, j * width : (j + 1) * width] = x_ref[:, at]


def turn(x, cosine, sine):
    lanes = lax.broadcasted_iota(jnp.int32, x.shape, 1)
    width = x.shape[1]
    swapped = jnp.where(lanes % 64 < 32, pltpu.roll(x, width - 32, 1), pltpu.roll(x, 32, 1))
    return x * cosine + swapped * sine


def lane_ids(width):
    return lax.broadcasted_iota(jnp.int32, (1, width), 1)


def head_lanes(h, width):
    lanes = lane_ids(width)
    return (lanes >= h * 64) & (lanes < (h + 1) * 64)


def spare_head(h):
    return 1 if h == 0 else 0


def mask_lanes(s_ref, tokens, width, slots, query_ref, key_ref):
    segment = segment_of(s_ref, row_ids(tokens), slots)
    for p in range(2):
        at = lane_ids(width) - 64 * p
        inside = (at >= 0) & (at <= slots)
        more = (at > slots) & (at <= slots + 3)
        query_ref[p] = jnp.where(inside & (at != segment), FAR, 0.0).astype(BF16)
        key_ref[p] = jnp.where((inside & (at == segment)) | more, 1.0, 0.0).astype(BF16)


def attention_kernel(slots, s_ref, x_ref, bq_ref, bk_ref, bv_ref, cos_ref, sin_ref, *refs):
    wq, wk, wv = refs[:BLOCKS], refs[BLOCKS : 2 * BLOCKS], refs[2 * BLOCKS : 3 * BLOCKS]
    q_ref, k_ref, v_ref, att_ref, lse_ref, rel_ref, qm_ref, km_ref = refs[3 * BLOCKS :]
    tokens, width = q_ref.shape

    @pl.when(pl.program_id(0) == 0)
    def _():
        by_block(s_ref, x_ref, rel_ref)
        mask_lanes(s_ref, tokens, width, slots, qm_ref, km_ref)

    x = rel_ref[...]
    cosine, sine = cos_ref[...], sin_ref[...]
    q = turn(rows_by_cols(x, rows_of(wq)) + bq_ref[...], cosine, sine).astype(BF16)
    k = turn(rows_by_cols(x, rows_of(wk)) + bk_ref[...], cosine, sine).astype(BF16)
    v = (rows_by_cols(x, rows_of(wv)) + bv_ref[...]).astype(BF16)
    q = q * jnp.asarray(0.125, BF16)
    q_ref[...] = q
    k_ref[...] = k
    v_ref[...] = v
    masked_keys = [jnp.where(head_lanes(p, width), km_ref[p], k) for p in range(2)]
    total = jnp.zeros((tokens, width), F32)
    lse = jnp.zeros((tokens, 128), F32)
    for h in range(GROUP):
        p = spare_head(h)
        mine = head_lanes(h, width)
        scores = rows_by_rows(jnp.where(mine, q, qm_ref[p]), masked_keys[p])
        top = jnp.max(scores, axis=1, keepdims=True)
        e = jnp.exp(scores - top)
        denominator = jnp.sum(e, axis=1, keepdims=True)
        part = rows_by_cols(e.astype(BF16), v) * (1.0 / denominator)
        total = jnp.where(mine, part, total)
        lse = jnp.where(lane_ids(128) == h, top + jnp.log(denominator), lse)
    att_ref[...] = total.astype(BF16)
    lse_ref[0] = lse


def out_kernel(slots, s_ref, att_ref, act_ref, time_ref, bias_ref, gain_ref, shift_ref, *refs):
    w, (res_ref, mlp_ref, rel_ref) = refs[:BLOCKS], refs[BLOCKS:]
    by_block(s_ref, att_ref, rel_ref)
    x = resid_zero_of(s_ref, act_ref[...], time_ref[...], 0, slots)
    x = x + rows_by_cols(rel_ref[...], rows_of(w)) + bias_ref[...]
    res_ref[...] = x
    normal, _ = normalize(x)
    mlp_ref[...] = (normal * gain_ref[...] + shift_ref[...]).astype(BF16)


def up_kernel(s_ref, x_ref, bias_ref, *refs):
    w, (act_ref, slope_ref, rel_ref) = refs[:BLOCKS], refs[BLOCKS:]

    @pl.when(pl.program_id(0) == 0)
    def _():
        by_block(s_ref, x_ref, rel_ref)

    pre = rows_by_cols(rel_ref[...], rows_of(w)) + bias_ref[...]
    cdf = 0.5 + 0.5 * lax.erf(pre * 0.7071067811865476)
    density = 0.3989422804014327 * jnp.exp(-0.5 * pre * pre)
    act_ref[...] = (pre * cdf).astype(BF16)
    slope_ref[...] = (cdf + pre * density).astype(BF16)


def down_copies(refs, held_ref, sems):
    return [(n // 2, pltpu.make_async_copy(ref, held_ref.at[n], sems.at[n])) for n, ref in enumerate(refs)]


def fetch_down(step, copies):
    @pl.when(step == 0)
    def _():
        for _, copy in copies:
            copy.start()

    for chip in range(CHIPS):

        @pl.when(step == chip)
        def _():
            for owner, copy in copies:
                if owner == chip:
                    copy.wait()


def halves_of(s_ref, width):
    core = s_ref[0] % 2
    return [pl.ds(pl.multiple_of(at * width, 128), width) for at in (core, 1 - core)]


def down_kernel(slots, s_ref, a_ref, res_ref, bias_ref, *refs):
    w, (out_ref, acc_ref, held_ref, sems) = refs[:BLOCKS], refs[BLOCKS:]
    c = pl.program_id(0)
    fetch_down(c, down_copies(w, held_ref, sems))

    @pl.when(c == 0)
    def _():
        acc_ref[...] = res_ref[...] + bias_ref[...]

    for n, at in enumerate(halves_of(s_ref, held_ref.shape[1])):
        acc_ref[...] += rows_by_cols(a_ref[:, at], held_ref[2 * c + n])

    @pl.when(c == pl.num_programs(0) - 1)
    def _():
        valid = row_ids(out_ref.shape[0]) < s_ref[ENDS_AT + slots - 1]
        out_ref[...] = jnp.where(valid, acc_ref[...], 0.0).astype(BF16)


def branch_kernel(slots, s_ref, cot_ref, branch_ref, bias_ref):
    valid = row_ids(cot_ref.shape[0]) < s_ref[ENDS_AT + slots - 1]
    branch = jnp.where(valid, cot_ref[...].astype(F32), 0.0)
    branch_ref[...] = branch.astype(BF16)
    bias_ref[...] = jnp.sum(branch, axis=0, keepdims=True)


def mlp_back_kernel(s_ref, branch_ref, slope_ref, res_ref, gain_ref, *refs):
    down, up = refs[:BLOCKS], refs[BLOCKS : 2 * BLOCKS]
    pre_ref, bias_ref, dres_ref, datt_ref, sums_ref, acc_ref, grad_ref, held_ref, sems = refs[2 * BLOCKS :]
    c = pl.program_id(0)
    fetch_down(c, down_copies(down, held_ref, sems))

    @pl.when(c == 0)
    def _():
        acc_ref[...] = jnp.zeros_like(acc_ref)

    branch = branch_ref[...]
    for n, at in enumerate(halves_of(s_ref, held_ref.shape[1])):
        d_pre = (rows_by_rows(branch, held_ref[2 * c + n]) * slope_ref[:, at].astype(F32)).astype(BF16)
        pre_ref[:, at] = d_pre
        bias_ref[:, at] = jnp.sum(d_pre.astype(F32), axis=0, keepdims=True)
        acc_ref[...] += rows_by_rows(d_pre, rows_of(up, at))

    @pl.when(c == pl.num_programs(0) - 1)
    def _():
        by_block(s_ref, acc_ref, grad_ref, back=True)
        grad = grad_ref[...]
        normal, inverse = normalize(res_ref[...])
        d_res = branch.astype(F32) + normalize_back(grad, normal, inverse, gain_ref[...])
        dres_ref[...] = d_res
        d_att = d_res.astype(BF16)
        datt_ref[...] = d_att
        sums_ref[0:1, :] = jnp.sum(grad * normal, axis=0, keepdims=True)
        sums_ref[1:2, :] = jnp.sum(grad, axis=0, keepdims=True)
        sums_ref[2:3, :] = jnp.sum(d_att.astype(F32), axis=0, keepdims=True)
        sums_ref[3:8, :] = jnp.zeros((5, sums_ref.shape[1]), F32)


def three_lanes(x, p, slots):
    first = x.astype(BF16)
    rest = x - first.astype(F32)
    second = rest.astype(BF16)
    third = (rest - second.astype(F32)).astype(BF16)
    at = lane_ids(64 * GROUP) - 64 * p - slots - 1
    spread = jnp.where(at == 0, first, jnp.where(at == 1, second, third))
    return jnp.where((at >= 0) & (at < 3), spread, jnp.zeros((), BF16))


def attention_back_kernel(slots, s_ref, d_ref, q_ref, k_ref, v_ref, lse_ref, cos_ref, sin_ref, *refs):
    w, (out_ref, sums_ref, qm_ref, km_ref, dq_ref, dk_ref, dv_ref, heads_ref) = refs[:BLOCKS], refs[BLOCKS:]
    tokens, width = q_ref.shape
    step = pl.program_id(0)

    @pl.when(pl.program_id(0) == 0)
    def _():
        mask_lanes(s_ref, tokens, width, slots, qm_ref, km_ref)

    for chip, pieces in enumerate((w[0:2], w[2:4], w[4:6], w[6:8])):

        @pl.when(step == chip)
        def _():
            both = rows_by_rows(d_ref[...], rows_of(pieces)).astype(BF16)
            for n, at in enumerate(halves_of(s_ref, width // 2)):
                heads_ref[:, at] = both[:, n * (width // 2) : (n + 1) * (width // 2)]

    d_heads = heads_ref[...]
    q, k, v = q_ref[...], k_ref[...], v_ref[...]
    for h in range(GROUP):
        p = spare_head(h)
        mine, spare = head_lanes(h, width), head_lanes(p, width)
        queries = jnp.where(spare, qm_ref[p] + three_lanes(-lse_ref[0, :, h : h + 1], p, slots), q)
        soft = jnp.exp(rows_by_rows(jnp.where(mine, k, km_ref[p]), queries))
        product = soft * rows_by_rows(jnp.where(mine, v, jnp.zeros((), BF16)), d_heads)
        row_terms = jnp.sum(product, axis=0, keepdims=True)
        d_scores = (product - soft * row_terms).astype(BF16)
        d_v = rows_by_cols(soft.astype(BF16), d_heads)
        d_k = rows_by_cols(d_scores, q)
        d_q = cols_by_cols(d_scores, k)
        if h == 0:
            dq_ref[...], dk_ref[...], dv_ref[...] = d_q, d_k, d_v
        else:
            dq_ref[...] = jnp.where(mine, d_q, dq_ref[...])
            dk_ref[...] = jnp.where(mine, d_k, dk_ref[...])
            dv_ref[...] = jnp.where(mine, d_v, dv_ref[...])
    cosine, sine = cos_ref[...], sin_ref[...]
    sums_ref[...] = jnp.zeros_like(sums_ref)
    parts = (turn(dq_ref[...] * 0.125, cosine, -sine), turn(dk_ref[...], cosine, -sine), dv_ref[...])
    for i, part in enumerate(parts):
        part = part.astype(BF16)
        out_ref[i] = part
        sums_ref[i : i + 1, :] = jnp.sum(part.astype(F32), axis=0, keepdims=True)


def d_input_kernel(slots, s_ref, d_ref, act_ref, time_ref, gain_ref, dres_ref, *refs):
    w, (out_ref, sums_ref, acc_ref, grad_ref) = refs[:BLOCKS], refs[BLOCKS:]
    j = pl.program_id(0)

    @pl.when(j == 0)
    def _():
        acc_ref[...] = jnp.zeros_like(acc_ref)

    acc_ref[...] += rows_by_rows(d_ref[0], rows_of(w))

    @pl.when(j == pl.num_programs(0) - 1)
    def _():
        by_block(s_ref, acc_ref, grad_ref, back=True)
        grad = grad_ref[...]
        normal, inverse = normalize(resid_zero_of(s_ref, act_ref[...], time_ref[...], 0, slots))
        d_in = dres_ref[...] + normalize_back(grad, normal, inverse, gain_ref[...])
        out_ref[...] = d_in.astype(BF16)
        sums_ref[...] = jnp.zeros_like(sums_ref)
        sums_ref[0:1, :] = jnp.sum(grad * normal, axis=0, keepdims=True)
        sums_ref[1:2, :] = jnp.sum(grad, axis=0, keepdims=True)
        for slot, inside in enumerate(members_of(s_ref, row_ids(act_ref.shape[0]), slots)):
            sums_ref[2 + slot : 3 + slot, :] = jnp.sum(jnp.where(inside, d_in, 0.0), axis=0, keepdims=True)


def grad_kernel(steps, sources, groups, s_ref, *refs):
    per = 5 * sources
    outs = refs[per * len(steps) :]
    i = pl.program_id(0)
    first = 0
    for n, (count, lead) in enumerate(steps):
        mine = refs[per * n : per * (n + 1)]

        @pl.when((i >= first) & (i < first + count))
        def _():
            product = None
            for source in range(sources):
                *a_refs, b_ref = mine[5 * source : 5 * source + 5]
                a = jnp.concatenate([ref[...] for ref in a_refs], axis=1)
                part = cols_by_cols(a, b_ref[0] if lead else b_ref[...])
                product = part if product is None else product + part
            rows = product.shape[0] // 4
            for out, group in zip(outs, groups):
                out[...] = product[group[0] * rows : (group[-1] + 1) * rows].astype(BF16)

        first += count


def weight_grad(scalars, odd, pairs, tile, after=(), groups=((0,), (1,), (2, 3))):
    tokens, width = pairs[0][0].shape[0], pairs[0][0].shape[1] // BLOCKS
    sources = len(pairs[0]) // 2
    specs, inputs, steps = [], [], []
    first = 0
    for pair in pairs:
        lead = pair[1].ndim == 3
        per = pair[1].shape[-1] // tile
        count = per * (pair[1].shape[0] if lead else 1)

        def local(i, first=first, count=count):
            return jnp.clip(i - first, 0, count - 1)

        for a, b in zip(pair[::2], pair[1::2]):
            for j in range(4):
                specs.append(pl.BlockSpec((tokens, width), lambda i, s, j=j: (0, s[2 * j + odd])))
                inputs.append(a)
            if lead:
                specs.append(
                    pl.BlockSpec((1, tokens, tile), lambda i, s, at=local, per=per: (at(i) // per, 0, at(i) % per))
                )
            else:
                specs.append(pl.BlockSpec((tokens, tile), lambda i, s, at=local: (0, at(i))))
            inputs.append(b)
        steps.append((count, lead))
        first += count
    sizes = [len(group) * width for group in groups]
    out = call(
        partial(grad_kernel, tuple(steps), sources, groups), scalars, inputs, specs,
        [jax.ShapeDtypeStruct((rows, first * tile), BF16) for rows in sizes],
        [pl.BlockSpec((rows, tile), lambda i, s: (0, i)) for rows in sizes], (first,), after=after,
    )
    return list(out)


def pack_grads_kernel(slots, s_ref, one_ref, qkv_ref, two_ref, up_ref, down_ref, time_ref, odd_ref, even_ref):
    rows = time_ref.shape[0] // BLOCKS
    d_time = one_ref[2 : 2 + slots, :]
    one, two = d_time.shape[1] // BLOCKS, 2 * d_time.shape[1] // BLOCKS
    ff = up_ref.shape[1] // BLOCKS
    odd_ref[...] = jnp.zeros_like(odd_ref)
    even_ref[...] = jnp.zeros_like(even_ref)
    for j in range(BLOCKS):
        block = s_ref[j]
        out, chip = (odd_ref, (0, 2, 1, 3)[j // 2]) if j % 2 else (even_ref, j // 2)
        features = time_ref[pl.ds(pl.multiple_of(block * rows, 8), rows), :]
        out[chip, 0:rows, :] = sum(features[:, s : s + 1] * d_time[s : s + 1, :] for s in range(slots)).astype(BF16)
        at = pl.ds(pl.multiple_of(block * one, 128), one)
        sources = (one_ref[0:1, at], one_ref[1:2, at], two_ref[2:3, at], two_ref[0:1, at], two_ref[1:2, at],
                   down_ref[0:1, at], qkv_ref[2:3, at])
        line = jnp.concatenate(sources, axis=1)
        out[chip, rows : rows + 1, 0 : line.shape[1]] = line.astype(BF16)
        wide = pl.ds(pl.multiple_of((block % 4) * two, 128), two)
        pair = jnp.where(block < 4, qkv_ref[0:1, wide], qkv_ref[1:2, wide])
        hidden = up_ref[0:1, pl.ds(pl.multiple_of(block * ff, 128), ff)]
        out[chip, rows + 1 : rows + 2, 0 : two + ff] = jnp.concatenate([pair, hidden], axis=1).astype(BF16)
        bias = jnp.sum(one_ref[2 : 2 + slots, at], axis=0, keepdims=True)
        out[chip, rows + 2 : rows + 3, 0:one] = bias.astype(BF16)


def per_device(
    n_dp, n_fsdp, activations, time_features, lengths, attn_gain, attn_shift, qkv_weight, qkv_bias, out_weight, out_bias,
    mlp_gain, mlp_shift, up_weight, up_bias, down_weight, down_bias, time_weight, time_bias, cotangent,
):
    tokens, width = activations.shape
    slots = lengths.shape[1]
    hidden = down_weight.shape[0] * n_fsdp
    small = n_fsdp == BLOCKS
    me = lax.axis_index("fsdp")
    blocks = jnp.arange(BLOCKS, dtype=jnp.int32)
    chips = jnp.arange(CHIPS, dtype=jnp.int32)
    if small:
        turned = jnp.where(chips % 3 > 0, 3 - chips, chips)
        chips = jnp.where(me % 2 == 0, turned, chips)
        blocks = (2 * chips[:, None] + jnp.arange(2, dtype=jnp.int32)[None, :]).reshape(-1) ^ me
        chips = chips ^ (me // 2)
    upto = jnp.arange(slots)[:, None] >= jnp.arange(slots)[None, :]
    ends = jnp.sum(jnp.where(upto, lengths, 0), axis=1)
    parity = lax.axis_index("dp") % 2
    scalars = jnp.concatenate([blocks, chips, parity[None], ends]).astype(jnp.int32)

    def swap(x, even, odd):
        return lax.ppermute(x, "fsdp", [(i, i ^ (odd if i % 2 else even)) for i in range(n_fsdp)])

    def sibling(x):
        return swap(x, 1, 1)

    def first_way(x):
        return swap(x, 4, 2)

    def second_way(x):
        return swap(x, 2, 4)

    def pieces(own, first, second, far, own_sibling, first_sibling, second_sibling, far_sibling):
        return [own, own_sibling, first, second_sibling, second, first_sibling, far, far_sibling]

    def add(*parts):
        total = parts[0].astype(F32)
        for part in parts[1:]:
            total = total + part.astype(F32)
        return total.astype(BF16)

    def gather_rows(w):
        return lax.all_gather(w, "fsdp", axis=0, tiled=True).reshape(BLOCKS, -1, w.shape[1])

    rows = whole((tokens, width))
    line = whole((1, width))
    vectors = [attn_gain, attn_shift, out_bias, mlp_gain, mlp_shift, down_bias, time_bias, qkv_bias, up_bias]
    per = width // BLOCKS
    qkv_columns = qkv_weight.shape[1]
    columns = qkv_columns + width
    depth = 16
    if small:
        sources = [qkv_weight, out_weight, time_weight] + vectors
        pack = call(
            pack_kernel, scalars, sources, [whole(x.shape) for x in sources],
            jax.ShapeDtypeStruct((per + depth, columns), BF16), whole((per + depth, columns)), (1,),
        )
        first_one, first_two, first_core = first_way(pack), second_way(pack), sibling(pack)
        up_own, down_own = copy_after(up_weight, pack), copy_after(down_weight, pack)
    else:
        gathered = [lax.all_gather(v, "fsdp", axis=0, tiled=True).reshape(BLOCKS, -1) for v in vectors]
        matrices = jnp.concatenate([gather_rows(qkv_weight), gather_rows(out_weight)], axis=2)
        times = lax.all_gather(time_weight, "fsdp", axis=0, tiled=True).reshape(BLOCKS, 2, depth, width)
        lines = jnp.concatenate(gathered, axis=1)
        lines = jnp.pad(lines, ((0, 0), (0, columns - 2 * width - lines.shape[1])))[:, None]
        lines = jnp.pad(lines, ((0, 0), (0, depth - 1), (0, 0)))
        extra = jnp.concatenate([times[:, 0], times[:, 1], lines], axis=2)
        first = list(jnp.concatenate([matrices, extra], axis=1))
        up_rel = list(gather_rows(up_weight))
        down_rel = list(gather_rows(down_weight))

    ids = jnp.arange(tokens, dtype=jnp.int32)[:, None]
    starts = ends - lengths[0]
    inside = (ids >= starts[None, :]) & (ids < ends[None, :])
    position = (ids[:, 0] - jnp.sum(jnp.where(inside, starts[None, :], 0), axis=1)).astype(F32)
    frequency = 10000.0 ** (-2.0 * jnp.arange(32, dtype=F32) / 64)
    angles = position[:, None] * frequency[None, :]
    cosine, sine = jnp.cos(angles), jnp.sin(angles)
    lanes = 64 * GROUP
    cos_table = jnp.tile(cosine, (1, 2 * GROUP))
    sin_table = jnp.tile(jnp.concatenate([-sine, sine], axis=1), (1, GROUP))

    d_branch, down_bias_sum = call(
        partial(branch_kernel, slots), scalars, [cotangent], [rows],
        [jax.ShapeDtypeStruct((tokens, width), BF16), jax.ShapeDtypeStruct((1, width), F32)], [rows, line], (1,),
    )
    if small:
        first_one, first_two = next_round(
            scalars, [first_one, first_two], [first_core, d_branch, up_own, down_own, cos_table, sin_table]
        )
        first_far = second_way(first_one)
        core_one, core_two, branch_core = sibling(first_one), sibling(first_two), sibling(d_branch)
        first_far, up_own = next_round(scalars, [first_far, up_own], [core_one, core_two, branch_core])
        up_one, up_two = first_way(up_own), second_way(up_own)
        first = pieces(pack, first_one, first_two, first_far, first_core, core_one, core_two, sibling(first_far))
    spread = time_features.reshape(slots, 2 * BLOCKS, -1)
    spread = jnp.pad(spread, ((0, 0), (0, 0), (0, 128 - spread.shape[2]))).reshape(slots, -1)
    extra_specs = [pl.BlockSpec((depth, columns), lambda i, s: (per // depth, 0))] * BLOCKS
    attn_in, time_rows, lines, qkv_b, up_b = call(
        partial(norm_one_kernel, slots), scalars, [activations, spread] + first,
        [rows, whole(spread.shape)] + extra_specs,
        [jax.ShapeDtypeStruct((tokens, width), BF16), jax.ShapeDtypeStruct((slots, width), F32),
         jax.ShapeDtypeStruct((8, width), F32), jax.ShapeDtypeStruct((1, qkv_columns), F32),
         jax.ShapeDtypeStruct((1, hidden), F32)],
        [rows, whole((slots, width)), whole((8, width)), whole((1, qkv_columns)), whole((1, hidden))], (1,),
        after=(d_branch,),
    )
    gain_one, shift_one, out_b, gain_two, shift_two, down_b = [lines[i : i + 1] for i in range(6)]
    groups = H // GROUP
    col = pl.BlockSpec((tokens, lanes), lambda g, s: (0, g))
    table = whole((tokens, lanes))
    mask_rooms = [pltpu.VMEM((2, tokens, lanes), BF16)] * 2
    qkv_specs = []
    for o in range(3):
        qkv_specs += piece_specs(per, lanes, lambda g, s, o=o: o * groups + g)
    queries, keys, values, attended, lse = call(
        partial(attention_kernel, slots), scalars,
        [attn_in, qkv_b, qkv_b, qkv_b, cos_table, sin_table] + first * 3,
        [rows] + [pl.BlockSpec((1, lanes), lambda g, s, o=o: (0, o * groups + g)) for o in range(3)]
        + [table, table] + qkv_specs,
        [jax.ShapeDtypeStruct((tokens, width), BF16)] * 4 + [jax.ShapeDtypeStruct((groups, tokens, 128), F32)],
        [col, col, col, col, pl.BlockSpec((1, tokens, 128), lambda g, s: (g, 0, 0))],
        (groups,), [pltpu.VMEM((tokens, width), BF16)] + mask_rooms)
    if small:
        up_one, up_two, up_own = next_round(scalars, [up_one, up_two, up_own], [attended])
        up_far = second_way(up_one)
        up_core, core_one, core_two = sibling(up_own), sibling(up_one), sibling(up_two)
        wait = (up_one,)
    else:
        wait = ()
    out_specs = piece_specs(per, width, lambda *a: qkv_columns // width)
    resid_one, mlp_in = call(
        partial(out_kernel, slots), scalars,
        [attended, activations, time_rows, out_b, gain_two, shift_two] + first,
        [rows, rows, whole((slots, width)), line, line, line] + out_specs,
        [jax.ShapeDtypeStruct((tokens, width), F32), jax.ShapeDtypeStruct((tokens, width), BF16)],
        [rows, rows], (1,), [pltpu.VMEM((tokens, width), BF16)], after=wait,
    )
    if small:
        up_far, down_own = next_round(scalars, [up_far, down_own], [core_one, core_two, up_core, mlp_in])
        up_rel = pieces(up_own, up_one, up_two, up_far, up_core, core_one, core_two, sibling(up_far))
        down_one, down_two, down_core = first_way(down_own), second_way(down_own), sibling(down_own)
        attn_in_core = sibling(attn_in)
    tile = hidden // CHIPS
    wide = pl.BlockSpec((tokens, tile), lambda i, s: (0, i))
    activated, slope = call(
        up_kernel, scalars, [mlp_in, up_b] + up_rel,
        [rows, pl.BlockSpec((1, tile), lambda i, s: (0, i))] + piece_specs(per, tile, lambda i, s: i),
        [jax.ShapeDtypeStruct((tokens, hidden), BF16)] * 2, [wide, wide], (CHIPS,),
        [pltpu.VMEM((tokens, width), BF16)])

    even_z = parity == 0

    def swap_z(x, bit):
        return lax.ppermute(x, "dp", [(i, i ^ bit) for i in range(n_dp)])

    def sum_of(*arrays, row=0, column=0, rows=None, columns=None):
        shape = arrays[0].shape
        return [(x, row, column) for x in arrays], rows or shape[0], columns or shape[1]

    def halves(*parts):
        half = parts[0].shape[0] // 2
        low, high = add(*[x[:half] for x in parts]), add(*[x[half:] for x in parts])
        return jnp.where(even_z, low, high), jnp.where(even_z, high, low)

    def quarters(*parts):
        size = parts[0].shape[0] // 4
        place = lax.axis_index("dp")
        cuts = [[lax.dynamic_slice_in_dim(x, (place ^ bits) * size, size) for x in parts] for bits in range(4)]
        return [add(*cut) for cut in cuts]

    def exchange(parts):
        return [swap_z(x, bits) for x, bits in zip(parts, (1, 2, 3))]

    def sum_four(own, came):
        one, two, three = [x.astype(F32) for x in came]
        return ((own.astype(F32) + one) + (two + three)).astype(BF16)

    def in_place(own, came):
        four = jnp.stack([own, *came]).reshape(2, 2, *own.shape)
        place = lax.axis_index("dp")
        for axis, bit in ((0, 2), (1, 1)):
            four = jnp.where((place & bit) > 0, jnp.flip(four, axis), four)
        return four.reshape(-1, own.shape[1]).astype(F32)

    def joined(own, other):
        return jnp.where(even_z, jnp.concatenate([own, other]), jnp.concatenate([other, own])).astype(F32)

    def rows_of_all(pairs, tile):
        blocks = [weight_grad(scalars, odd, pairs, tile) for odd in range(2)]
        blocks = [jnp.concatenate(x).reshape(CHIPS, -1, x[0].shape[1]) for x in blocks]
        both = jnp.stack(blocks, axis=1).reshape(-1, blocks[0].shape[2])
        return lax.psum(lax.psum_scatter(both, "fsdp", scatter_dimension=0, tiled=True), "dp").astype(F32)

    if small:
        down_one, down_two, activated = next_round(scalars, [down_one, down_two, activated], [down_core, attn_in_core])
        down_far = second_way(down_one)
        core_one, core_two, activated_core = sibling(down_one), sibling(down_two), sibling(activated)
        down_parts = weight_grad(scalars, 0, [(activated, d_branch, activated_core, branch_core)], 512)
        down_far, down_parts[2] = next_round(scalars, [down_far, down_parts[2]], [core_one, core_two])
        down_came = second_way(down_parts[2])
        down_rel = pieces(down_own, down_one, down_two, down_far, down_core, core_one, core_two, sibling(down_far))
        mlp_in_core = sibling(mlp_in)
    else:
        down_grad = rows_of_all([(activated, d_branch)], 512)

    chip_wide = pl.BlockSpec((tokens, tile), lambda i, s: (0, s[CHIP_AT + i]))
    down_rooms = [pltpu.VMEM((BLOCKS, hidden // BLOCKS, width), BF16), pltpu.SemaphoreType.DMA((BLOCKS,))]
    d_pre, up_bias_sum, d_resid_one, d_attn, sums_two = call(
        mlp_back_kernel, scalars, [d_branch, slope, resid_one, gain_two] + down_rel + up_rel,
        [rows, chip_wide, rows, line] + [pl.BlockSpec(memory_space=pl.ANY)] * BLOCKS
        + piece_specs(per, tile, lambda i, s: s[CHIP_AT + i]),
        [jax.ShapeDtypeStruct((tokens, hidden), BF16),
         jax.ShapeDtypeStruct((1, hidden), F32), jax.ShapeDtypeStruct((tokens, width), F32),
         jax.ShapeDtypeStruct((tokens, width), BF16), jax.ShapeDtypeStruct((8, width), F32)],
        [chip_wide, pl.BlockSpec((1, tile), lambda i, s: (0, s[CHIP_AT + i])), rows, rows, whole((8, width))],
        (CHIPS,), [pltpu.VMEM((tokens, width), F32)] * 2 + down_rooms,
    )
    def layer_output(after):
        return call(
            partial(down_kernel, slots), scalars, [activated, resid_one, down_b] + down_rel,
            [chip_wide, rows, line] + [pl.BlockSpec(memory_space=pl.ANY)] * BLOCKS,
            jax.ShapeDtypeStruct((tokens, width), BF16), rows, (CHIPS,), [pltpu.VMEM((tokens, width), F32)] + down_rooms,
            after=after,
        )

    if small:
        d_pre, d_attn, down_came = next_round(scalars, [d_pre, d_attn, down_came], [mlp_in_core])
        d_pre_core, d_attn_core, attended_core = sibling(d_pre), sibling(d_attn), sibling(attended)
        far = down_came.shape[0] // 2
        down_one = first_way(add(down_parts[1], down_came[far:]))
        up_parts = weight_grad(
            scalars, 0, [(mlp_in, d_pre, mlp_in_core, d_pre_core), (attended, d_attn, attended_core, d_attn_core)], width
        )
        up_parts[2], down_came, down_one = next_round(scalars, [up_parts[2], down_came, down_one])
        up_came = second_way(up_parts[2])
        down_sum, *down_send = quarters(down_parts[0], down_came[:far], down_one)
        down_z = exchange(down_send)
        wait = (down_came,)
    else:
        up_out_grad = rows_of_all([(mlp_in, d_pre), (attended, d_attn)], width)
        up_grad, out_grad = up_out_grad[:, :hidden], up_out_grad[:, hidden:]
        wait = ()
    chip_col = pl.BlockSpec((tokens, lanes), lambda g, s: (0, s[CHIP_AT + g]))
    d_qkv, sums_qkv = call(
        partial(attention_back_kernel, slots), scalars,
        [d_attn, queries, keys, values, lse, cos_table, sin_table] + first,
        [rows, chip_col, chip_col, chip_col,
         pl.BlockSpec((1, tokens, 128), lambda g, s: (s[CHIP_AT + g], 0, 0)), table, table] + out_specs,
        [jax.ShapeDtypeStruct((3, tokens, width), BF16), jax.ShapeDtypeStruct((8, width), F32)],
        [pl.BlockSpec((3, tokens, lanes), lambda g, s: (0, 0, s[CHIP_AT + g])),
         pl.BlockSpec((8, lanes), lambda g, s: (0, s[CHIP_AT + g]))],
        (groups,), mask_rooms + [pltpu.VMEM((tokens, lanes), F32)] * 3 + [pltpu.VMEM((tokens, lanes), BF16)],
        after=wait,
    )
    if small:
        d_qkv, up_came, *down_z = next_round(scalars, [d_qkv, up_came, *down_z])
        d_qkv_core = sibling(d_qkv)
        up_one = first_way(add(up_parts[1], up_came[per:]))
        down_sum = sum_four(down_sum, down_z)
        down_z = exchange([down_sum] * 3)
    else:
        qkv_grad = rows_of_all([(attn_in, d_qkv)], width)
    input_grad, sums_one = call(
        partial(d_input_kernel, slots), scalars,
        [d_qkv, activations, time_rows, gain_one, d_resid_one] + first,
        [pl.BlockSpec((1, tokens, width), lambda i, s: (i, 0, 0)), rows, whole((slots, width)), line, rows]
        + piece_specs(per, width, lambda i, s: i),
        [jax.ShapeDtypeStruct((tokens, width), BF16), jax.ShapeDtypeStruct((8, width), F32)],
        [rows, whole((8, width))], (3,), [pltpu.VMEM((tokens, width), F32)] * 2,
    )
    if small:
        half = per // 2
        up_sum, up_send = next_round(
            scalars, [], [sums_one],
            [sum_of(up_parts[0], up_came, up_one, row=rows_, rows=half) for rows_ in ((0, half), (half, 0))],
        )
        up_z = swap_z(up_send, 1)
        qkv_parts = weight_grad(scalars, 0, [(attn_in, d_qkv, attn_in_core, d_qkv_core)], width, after=(up_sum,))
        qkv_parts[2], sums_one = next_round(scalars, [qkv_parts[2], sums_one], down_z)
        qkv_came = second_way(qkv_parts[2])
        time_cols = time_features.astype(F32).T
        depth = 64
        v_odd, v_even = call(
            partial(pack_grads_kernel, slots), scalars,
            [sums_one, sums_qkv, sums_two, up_bias_sum, down_bias_sum, time_cols],
            [whole((8, width)), whole((8, width)), whole((8, width)), whole((1, hidden)), line, whole(time_cols.shape)],
            [jax.ShapeDtypeStruct((4, depth, width), BF16)] * 2, [whole((4, depth, width))] * 2, (1,), cost=SOME_COST,
        )
        v_odd, v_even = v_odd.reshape(-1, width), v_even.reshape(-1, width)
        v_odd, up_z = next_round(scalars, [v_odd, up_z])
        up_sum = add(up_sum, up_z)
        up_z = swap_z(up_sum, 2)
        v_came = sibling(v_odd)
        v_came, *to_one = next_round(
            scalars, [v_came], [up_sum],
            [([(qkv_parts[1], row, 0), (qkv_came, per + row, 0)], half, qkv_columns) for row in (0, half)],
        )
        qkv_one = [first_way(x) for x in to_one]
        *qkv_one, v_came, up_z = next_round(scalars, [*qkv_one, v_came, up_z])
        low, high = [
            add(qkv_parts[0][row : row + half], qkv_came[row : row + half], x) for row, x in zip((0, half), qkv_one)
        ]
        qkv_sum, qkv_send = jnp.where(even_z, low, high), jnp.where(even_z, high, low)
        qkv_z = swap_z(qkv_send, 1)
        part = add(v_even, v_came).reshape(4, depth, width)
        parts = [part[k] for k in range(4)]
        v_came = [first_way(parts[1]), second_way(parts[2]), swap(parts[3], 6, 6)]
        down_sum, qkv_sum, up_sum, part = next_round(
            scalars, [down_sum], [], [sum_of(qkv_sum, qkv_z), sum_of(up_sum, up_z), sum_of(parts[0], *v_came)]
        )
        wait = (part,)
        qkv_z = swap_z(qkv_sum, 2)
        up_z = swap_z(up_sum, 1)
        v_came = swap_z(part, 1)
        output = layer_output(wait)
        down_grad = in_place(down_sum, down_z)
        qkv_z, v_came = next_round(scalars, [qkv_z, v_came], [output])
        qkv_sum = add(qkv_sum, qkv_z)
        qkv_grad = joined(qkv_sum, swap_z(qkv_sum, 1))
        part = add(part, v_came)
        share = part.astype(F32) + swap_z(part, 2).astype(F32)
        up_out_grad = joined(up_sum, up_z)
        up_grad, out_grad = up_out_grad[:, :hidden], up_out_grad[:, hidden:]
        time_rows_here = time_weight.shape[0]
        time_grad = share[:time_rows_here]
        one, two, ff = width // BLOCKS, 2 * width // BLOCKS, hidden // BLOCKS
        row = share[time_rows_here]
        (gain_one_grad, shift_one_grad, out_bias_grad, gain_two_grad, shift_two_grad, down_bias_grad,
         value_bias_grad) = [row[i * one : (i + 1) * one] for i in range(7)]
        row = share[time_rows_here + 1]
        qk_bias_grad, up_bias_grad = row[:two], row[two : two + ff]
        time_bias_grad = share[time_rows_here + 2, :one]
    else:
        output = layer_output(())
        d_time = sums_one[2 : 2 + slots]
        time_grad = lax.dot_general(
            time_features.astype(F32), d_time, (((0,), (0,)), ((), ())), precision=lax.Precision.HIGHEST
        )
        vector_sums = (
            sums_one[0], sums_one[1], sums_qkv[:2].reshape(-1), sums_qkv[2], sums_two[2], sums_two[0], sums_two[1],
            up_bias_sum[0], down_bias_sum[0], jnp.sum(d_time, axis=0),
        )
        shares = jnp.concatenate(
            [time_grad.reshape(n_fsdp, -1)] + [v.reshape(n_fsdp, -1) for v in vector_sums], axis=1
        )
        sizes = [time_weight.size] + [v.size // n_fsdp for v in vector_sums]
        shares = jnp.pad(shares, ((0, 0), (0, -shares.shape[1] % 4096))).reshape(n_fsdp, -1, 128)
        shares = lax.psum_scatter(shares.astype(BF16), "fsdp", scatter_dimension=0, tiled=False)
        share = lax.psum(shares, "dp").astype(F32).reshape(-1)
        got = []
        at = 0
        for size in sizes:
            got.append(share[at : at + size])
            at += size
        (time_grad, gain_one_grad, shift_one_grad, qk_bias_grad, value_bias_grad, out_bias_grad, gain_two_grad,
         shift_two_grad, up_bias_grad, down_bias_grad, time_bias_grad) = got
    return (
        output, input_grad, gain_one_grad, shift_one_grad, qkv_grad, qk_bias_grad, value_bias_grad, out_grad, out_bias_grad,
        gain_two_grad, shift_two_grad, up_grad, up_bias_grad, down_grad, down_bias_grad,
        time_grad.reshape(time_weight.shape), time_bias_grad,
    )


def solution(mesh):
    tokens = P(("dp", "fsdp"), None)
    vector = P("fsdp")
    matrix = P("fsdp", None)
    in_specs = (
        tokens, tokens, tokens, vector, vector, matrix, vector, matrix, vector, vector, vector, matrix, vector, matrix,
        vector, matrix, vector, tokens,
    )
    out_specs = (
        tokens, tokens, vector, vector, matrix, vector, vector, matrix, vector, vector, vector, matrix, vector, matrix,
        vector, matrix, vector,
    )
    body = partial(per_device, mesh.shape["dp"], mesh.shape["fsdp"])
    return jax.shard_map(body, mesh=mesh, in_specs=in_specs, out_specs=out_specs, check_vma=False)
```

```python
from functools import partial

import jax
import jax.numpy as jnp
from jax import lax
from jax.experimental import pallas as pl
from jax.experimental.pallas import tpu as pltpu
from jax.sharding import PartitionSpec as P

H = 16
GROUP = 4
BLOCKS = 8
CHIPS = 4
CHIP_AT = BLOCKS
PARITY_AT = CHIP_AT + CHIPS
ENDS_AT = PARITY_AT + 1
FAR = -1e30
NO_COST = pl.CostEstimate(flops=0, bytes_accessed=0, transcendentals=0)
SOME_COST = pl.CostEstimate(flops=30 * 10**9, bytes_accessed=100 * 10**6, transcendentals=0)
F32 = jnp.float32
BF16 = jnp.bfloat16


def rows_by_cols(a, b):
    return lax.dot_general(a, b, (((1,), (0,)), ((), ())), preferred_element_type=F32)


def rows_by_rows(a, b):
    return lax.dot_general(a, b, (((1,), (1,)), ((), ())), preferred_element_type=F32)


def cols_by_cols(a, b):
    return lax.dot_general(a, b, (((0,), (0,)), ((), ())), preferred_element_type=F32)


def call(kernel, scalars, inputs, in_specs, out_shapes, out_specs, grid, scratch=(), aliases=None, after=(), cost=NO_COST):
    count = len(inputs)

    def body(s_ref, *refs):
        kernel(s_ref, *refs[:count], *refs[count + len(after) :])

    return pl.pallas_call(
        body,
        name=getattr(kernel, "func", kernel).__name__,
        grid_spec=pltpu.PrefetchScalarGridSpec(
            num_scalar_prefetch=1,
            grid=grid,
            in_specs=list(in_specs) + [pl.BlockSpec(memory_space=pl.ANY)] * len(after),
            out_specs=out_specs,
            scratch_shapes=list(scratch),
        ),
        out_shape=out_shapes,
        input_output_aliases=aliases or {},
        compiler_params=pltpu.CompilerParams(
            dimension_semantics=("arbitrary",) * len(grid), vmem_limit_bytes=64 * 2**20
        ),
        cost_estimate=cost,
    )(scalars, *inputs, *after)


def round_kernel(counts, s_ref, *refs):
    outs = refs[-len(counts) :] if counts else ()
    at = 0
    for count, out in zip(counts, outs):
        total = refs[at][...].astype(F32)
        for ref in refs[at + 1 : at + count]:
            total = total + ref[...].astype(F32)
        out[...] = total.astype(BF16)
        at += count


def next_round(scalars, passed, others=(), sums=()):
    anywhere = pl.BlockSpec(memory_space=pl.ANY)
    steps = 2
    specs, inputs, counts, shapes, out_specs = [], [], [], [], []
    for parts, rows, columns in sums:
        size = rows // steps
        for array, row, column in parts:
            even, odd = row if isinstance(row, tuple) else (row, row)

            def at(i, s, even=even // size, odd=odd // size, column=column // columns):
                return (i + even + s[PARITY_AT] * (odd - even), column)

            specs.append(pl.BlockSpec((size, columns), at))
            inputs.append(array)
        counts.append(len(parts))
        shapes.append(jax.ShapeDtypeStruct((rows, columns), BF16))
        out_specs.append(pl.BlockSpec((size, columns), lambda i, s: (i, 0)))
    first = len(inputs)

    def kernel(s_ref, *refs):
        given = first + len(passed) + len(others)
        round_kernel(counts, s_ref, *refs[:first], *refs[given + len(passed) :])

    out = pl.pallas_call(
        kernel,
        name="next_round",
        grid_spec=pltpu.PrefetchScalarGridSpec(
            num_scalar_prefetch=1,
            grid=(steps if sums else 1,),
            in_specs=specs + [anywhere] * (len(passed) + len(others)),
            out_specs=[anywhere] * len(passed) + out_specs,
        ),
        out_shape=[jax.ShapeDtypeStruct(x.shape, x.dtype) for x in passed] + shapes,
        input_output_aliases={1 + first + i: i for i in range(len(passed))},
        compiler_params=pltpu.CompilerParams(dimension_semantics=("arbitrary",), vmem_limit_bytes=64 * 2**20),
        cost_estimate=NO_COST,
    )(scalars, *inputs, *passed, *others)
    return list(out)


def copy_after(x, *others):
    def kernel(x_ref, *refs):
        refs[-1][...] = x_ref[...]

    block = pl.BlockSpec((x.shape[0] // 2, x.shape[1]), lambda i: (i, 0))
    return pl.pallas_call(
        kernel,
        grid=(2,),
        out_shape=jax.ShapeDtypeStruct(x.shape, x.dtype),
        in_specs=[block] + [pl.BlockSpec(memory_space=pl.ANY)] * len(others),
        out_specs=block,
        cost_estimate=NO_COST,
    )(x, *others)


def whole(shape):
    zeros = (0,) * len(shape)
    return pl.BlockSpec(shape, lambda *_: zeros)


def normalize(x):
    center = x - jnp.mean(x, axis=-1, keepdims=True)
    variance = jnp.mean(center * center, axis=-1, keepdims=True)
    inverse = lax.rsqrt(variance + 1e-05)
    return center * inverse, inverse


def normalize_back(grad, normal, inverse, gain):
    scaled = grad * gain
    return inverse * (
        scaled
        - jnp.mean(scaled, axis=-1, keepdims=True)
        - normal * jnp.mean(scaled * normal, axis=-1, keepdims=True)
    )


def row_ids(count, first=0):
    return lax.broadcasted_iota(jnp.int32, (count, 1), 0) + first


def members_of(s_ref, ids, slots):
    out = []
    start = 0
    for slot in range(slots):
        end = s_ref[ENDS_AT + slot]
        out.append((ids >= start) & (ids < end))
        start = end
    return out


def segment_of(s_ref, ids, slots):
    segment = jnp.zeros(ids.shape, jnp.int32)
    for slot in range(slots):
        segment = segment + (ids >= s_ref[ENDS_AT + slot]).astype(jnp.int32)
    return segment


def resid_zero_of(s_ref, act, time_rows, first, slots):
    x = act.astype(F32)
    for slot, inside in enumerate(members_of(s_ref, row_ids(act.shape[0], first), slots)):
        x = x + jnp.where(inside, time_rows[slot : slot + 1, :], 0.0)
    return x


def piece_specs(rows, columns, at):
    return [pl.BlockSpec((rows, columns), lambda *a: (0, at(*a)))] * BLOCKS


def rows_of(refs, at=slice(None)):
    return jnp.concatenate([ref[:, at] for ref in refs], axis=0)


def pack_kernel(s_ref, qkv_ref, out_ref, time_ref, *refs):
    vectors, pack_ref = refs[:-1], refs[-1]
    rows, columns = qkv_ref.shape
    pack_ref[0:rows, 0:columns] = qkv_ref[...]
    pack_ref[0:rows, columns:] = out_ref[...]
    depth = pack_ref.shape[0] - rows
    width = out_ref.shape[1]
    pack_ref[rows:, 0:width] = time_ref[0:depth, :]
    pack_ref[rows:, width : 2 * width] = time_ref[depth:, :]
    line = jnp.concatenate([v[...].astype(F32).reshape(1, -1) for v in vectors], axis=1)
    line = jnp.concatenate([line, jnp.zeros((1, pack_ref.shape[1] - 2 * width - line.shape[1]), F32)], axis=1)
    lines = jnp.where(row_ids(depth) == 0, line, 0.0).astype(BF16)
    pack_ref[rows:, 2 * width :] = lines


def norm_one_kernel(slots, s_ref, act_ref, feat_ref, *refs):
    extras = refs[:BLOCKS]
    out_ref, time_ref, lines_ref, qkv_b_ref, up_b_ref = refs[BLOCKS:]
    depth = extras[0].shape[0]
    width = act_ref.shape[1]
    small = width // BLOCKS
    time_rows = jnp.zeros((slots, width), F32)
    for j in range(BLOCKS):
        block = s_ref[j]
        for half in range(2):
            at = pl.multiple_of((block * 2 + half) * 128, 128)
            part = feat_ref[:, pl.ds(at, 128)]
            time_rows = time_rows + rows_by_cols(part[:, 0:depth], extras[j][:, half * width : (half + 1) * width])
        line = extras[j][:, 2 * width :].astype(F32)[0:1]
        at = pl.ds(pl.multiple_of(block * small, 128), small)
        for v in range(7):
            lines_ref[v : v + 1, at] = line[:, v * small : (v + 1) * small]
        first = 7 * small
        for ref in (qkv_b_ref, up_b_ref):
            size = ref.shape[1] // BLOCKS
            ref[0:1, pl.ds(pl.multiple_of(block * size, 128), size)] = line[:, first : first + size]
            first += size
    lines_ref[7:8, :] = jnp.zeros((1, width), F32)
    time_rows = time_rows + lines_ref[6:7, :]
    time_ref[...] = time_rows
    x = resid_zero_of(s_ref, act_ref[...], time_rows, 0, slots)
    normal, _ = normalize(x)
    out_ref[...] = (normal * lines_ref[0:1, :] + lines_ref[1:2, :]).astype(BF16)


def by_block(s_ref, x_ref, out_ref, back=False):
    width = x_ref.shape[1] // BLOCKS
    for j in range(BLOCKS):
        at = pl.ds(pl.multiple_of(s_ref[j] * width, 128), width)
        if back:
            out_ref[:, at] = x_ref[:, j * width : (j + 1) * width]
        else:
            out_ref[:, j * width : (j + 1) * width] = x_ref[:, at]


def turn(x, cosine, sine):
    lanes = lax.broadcasted_iota(jnp.int32, x.shape, 1)
    width = x.shape[1]
    swapped = jnp.where(lanes % 64 < 32, pltpu.roll(x, width - 32, 1), pltpu.roll(x, 32, 1))
    return x * cosine + swapped * sine


def lane_ids(width):
    return lax.broadcasted_iota(jnp.int32, (1, width), 1)


def head_lanes(h, width):
    lanes = lane_ids(width)
    return (lanes >= h * 64) & (lanes < (h + 1) * 64)


def spare_head(h):
    return 1 if h == 0 else 0


def mask_lanes(s_ref, tokens, width, slots, query_ref, key_ref):
    segment = segment_of(s_ref, row_ids(tokens), slots)
    for p in range(2):
        at = lane_ids(width) - 64 * p
        inside = (at >= 0) & (at <= slots)
        more = (at > slots) & (at <= slots + 3)
        query_ref[p] = jnp.where(inside & (at != segment), FAR, 0.0).astype(BF16)
        key_ref[p] = jnp.where((inside & (at == segment)) | more, 1.0, 0.0).astype(BF16)


def attention_kernel(slots, s_ref, x_ref, bq_ref, bk_ref, bv_ref, cos_ref, sin_ref, *refs):
    wq, wk, wv = refs[:BLOCKS], refs[BLOCKS : 2 * BLOCKS], refs[2 * BLOCKS : 3 * BLOCKS]
    q_ref, k_ref, v_ref, att_ref, lse_ref, rel_ref, qm_ref, km_ref = refs[3 * BLOCKS :]
    tokens, width = q_ref.shape

    @pl.when(pl.program_id(0) == 0)
    def _():
        by_block(s_ref, x_ref, rel_ref)
        mask_lanes(s_ref, tokens, width, slots, qm_ref, km_ref)

    x = rel_ref[...]
    cosine, sine = cos_ref[...], sin_ref[...]
    q = turn(rows_by_cols(x, rows_of(wq)) + bq_ref[...], cosine, sine).astype(BF16)
    k = turn(rows_by_cols(x, rows_of(wk)) + bk_ref[...], cosine, sine).astype(BF16)
    v = (rows_by_cols(x, rows_of(wv)) + bv_ref[...]).astype(BF16)
    q = q * jnp.asarray(0.125, BF16)
    q_ref[...] = q
    k_ref[...] = k
    v_ref[...] = v
    masked_keys = [jnp.where(head_lanes(p, width), km_ref[p], k) for p in range(2)]
    total = jnp.zeros((tokens, width), F32)
    lse = jnp.zeros((tokens, 128), F32)
    for h in range(GROUP):
        p = spare_head(h)
        mine = head_lanes(h, width)
        scores = rows_by_rows(jnp.where(mine, q, qm_ref[p]), masked_keys[p])
        top = jnp.max(scores, axis=1, keepdims=True)
        e = jnp.exp(scores - top)
        denominator = jnp.sum(e, axis=1, keepdims=True)
        part = rows_by_cols(e.astype(BF16), v) * (1.0 / denominator)
        total = jnp.where(mine, part, total)
        lse = jnp.where(lane_ids(128) == h, top + jnp.log(denominator), lse)
    att_ref[...] = total.astype(BF16)
    lse_ref[0] = lse


def out_kernel(slots, s_ref, att_ref, act_ref, time_ref, bias_ref, gain_ref, shift_ref, *refs):
    w, (res_ref, mlp_ref, rel_ref) = refs[:BLOCKS], refs[BLOCKS:]
    by_block(s_ref, att_ref, rel_ref)
    x = resid_zero_of(s_ref, act_ref[...], time_ref[...], 0, slots)
    x = x + rows_by_cols(rel_ref[...], rows_of(w)) + bias_ref[...]
    res_ref[...] = x
    normal, _ = normalize(x)
    mlp_ref[...] = (normal * gain_ref[...] + shift_ref[...]).astype(BF16)


def up_kernel(s_ref, x_ref, bias_ref, *refs):
    w, (act_ref, slope_ref, rel_ref) = refs[:BLOCKS], refs[BLOCKS:]

    @pl.when(pl.program_id(0) == 0)
    def _():
        by_block(s_ref, x_ref, rel_ref)

    pre = rows_by_cols(rel_ref[...], rows_of(w)) + bias_ref[...]
    cdf = 0.5 + 0.5 * lax.erf(pre * 0.7071067811865476)
    density = 0.3989422804014327 * jnp.exp(-0.5 * pre * pre)
    act_ref[...] = (pre * cdf).astype(BF16)
    slope_ref[...] = (cdf + pre * density).astype(BF16)


def down_copies(refs, held_ref, sems):
    return [(n // 2, pltpu.make_async_copy(ref, held_ref.at[n], sems.at[n])) for n, ref in enumerate(refs)]


def fetch_down(step, copies):
    @pl.when(step == 0)
    def _():
        for _, copy in copies:
            copy.start()

    for chip in range(CHIPS):

        @pl.when(step == chip)
        def _():
            for owner, copy in copies:
                if owner == chip:
                    copy.wait()


def halves_of(s_ref, width):
    core = s_ref[0] % 2
    return [pl.ds(pl.multiple_of(at * width, 128), width) for at in (core, 1 - core)]


def down_kernel(slots, s_ref, a_ref, res_ref, bias_ref, *refs):
    w, (out_ref, acc_ref, held_ref, sems) = refs[:BLOCKS], refs[BLOCKS:]
    c = pl.program_id(0)
    fetch_down(c, down_copies(w, held_ref, sems))

    @pl.when(c == 0)
    def _():
        acc_ref[...] = res_ref[...] + bias_ref[...]

    for n, at in enumerate(halves_of(s_ref, held_ref.shape[1])):
        acc_ref[...] += rows_by_cols(a_ref[:, at], held_ref[2 * c + n])

    @pl.when(c == pl.num_programs(0) - 1)
    def _():
        valid = row_ids(out_ref.shape[0]) < s_ref[ENDS_AT + slots - 1]
        out_ref[...] = jnp.where(valid, acc_ref[...], 0.0).astype(BF16)


def branch_kernel(slots, s_ref, cot_ref, branch_ref, bias_ref):
    valid = row_ids(cot_ref.shape[0]) < s_ref[ENDS_AT + slots - 1]
    branch = jnp.where(valid, cot_ref[...].astype(F32), 0.0)
    branch_ref[...] = branch.astype(BF16)
    bias_ref[...] = jnp.sum(branch, axis=0, keepdims=True)


def mlp_back_kernel(s_ref, branch_ref, slope_ref, res_ref, gain_ref, *refs):
    down, up = refs[:BLOCKS], refs[BLOCKS : 2 * BLOCKS]
    pre_ref, bias_ref, dres_ref, datt_ref, sums_ref, acc_ref, grad_ref, held_ref, sems = refs[2 * BLOCKS :]
    c = pl.program_id(0)
    fetch_down(c, down_copies(down, held_ref, sems))

    @pl.when(c == 0)
    def _():
        acc_ref[...] = jnp.zeros_like(acc_ref)

    branch = branch_ref[...]
    for n, at in enumerate(halves_of(s_ref, held_ref.shape[1])):
        d_pre = (rows_by_rows(branch, held_ref[2 * c + n]) * slope_ref[:, at].astype(F32)).astype(BF16)
        pre_ref[:, at] = d_pre
        bias_ref[:, at] = jnp.sum(d_pre.astype(F32), axis=0, keepdims=True)
        acc_ref[...] += rows_by_rows(d_pre, rows_of(up, at))

    @pl.when(c == pl.num_programs(0) - 1)
    def _():
        by_block(s_ref, acc_ref, grad_ref, back=True)
        grad = grad_ref[...]
        normal, inverse = normalize(res_ref[...])
        d_res = branch.astype(F32) + normalize_back(grad, normal, inverse, gain_ref[...])
        dres_ref[...] = d_res
        d_att = d_res.astype(BF16)
        datt_ref[...] = d_att
        sums_ref[0:1, :] = jnp.sum(grad * normal, axis=0, keepdims=True)
        sums_ref[1:2, :] = jnp.sum(grad, axis=0, keepdims=True)
        sums_ref[2:3, :] = jnp.sum(d_att.astype(F32), axis=0, keepdims=True)
        sums_ref[3:8, :] = jnp.zeros((5, sums_ref.shape[1]), F32)


def three_lanes(x, p, slots):
    first = x.astype(BF16)
    rest = x - first.astype(F32)
    second = rest.astype(BF16)
    third = (rest - second.astype(F32)).astype(BF16)
    at = lane_ids(64 * GROUP) - 64 * p - slots - 1
    spread = jnp.where(at == 0, first, jnp.where(at == 1, second, third))
    return jnp.where((at >= 0) & (at < 3), spread, jnp.zeros((), BF16))


def attention_back_kernel(slots, s_ref, d_ref, q_ref, k_ref, v_ref, lse_ref, cos_ref, sin_ref, *refs):
    w, (out_ref, sums_ref, qm_ref, km_ref, dq_ref, dk_ref, dv_ref, heads_ref) = refs[:BLOCKS], refs[BLOCKS:]
    tokens, width = q_ref.shape
    step = pl.program_id(0)

    @pl.when(pl.program_id(0) == 0)
    def _():
        mask_lanes(s_ref, tokens, width, slots, qm_ref, km_ref)

    for chip, pieces in enumerate((w[0:2], w[2:4], w[4:6], w[6:8])):

        @pl.when(step == chip)
        def _():
            both = rows_by_rows(d_ref[...], rows_of(pieces)).astype(BF16)
            for n, at in enumerate(halves_of(s_ref, width // 2)):
                heads_ref[:, at] = both[:, n * (width // 2) : (n + 1) * (width // 2)]

    d_heads = heads_ref[...]
    q, k, v = q_ref[...], k_ref[...], v_ref[...]
    for h in range(GROUP):
        p = spare_head(h)
        mine, spare = head_lanes(h, width), head_lanes(p, width)
        queries = jnp.where(spare, qm_ref[p] + three_lanes(-lse_ref[0, :, h : h + 1], p, slots), q)
        soft = jnp.exp(rows_by_rows(jnp.where(mine, k, km_ref[p]), queries))
        product = soft * rows_by_rows(jnp.where(mine, v, jnp.zeros((), BF16)), d_heads)
        row_terms = jnp.sum(product, axis=0, keepdims=True)
        d_scores = (product - soft * row_terms).astype(BF16)
        d_v = rows_by_cols(soft.astype(BF16), d_heads)
        d_k = rows_by_cols(d_scores, q)
        d_q = cols_by_cols(d_scores, k)
        if h == 0:
            dq_ref[...], dk_ref[...], dv_ref[...] = d_q, d_k, d_v
        else:
            dq_ref[...] = jnp.where(mine, d_q, dq_ref[...])
            dk_ref[...] = jnp.where(mine, d_k, dk_ref[...])
            dv_ref[...] = jnp.where(mine, d_v, dv_ref[...])
    cosine, sine = cos_ref[...], sin_ref[...]
    sums_ref[...] = jnp.zeros_like(sums_ref)
    parts = (turn(dq_ref[...] * 0.125, cosine, -sine), turn(dk_ref[...], cosine, -sine), dv_ref[...])
    for i, part in enumerate(parts):
        part = part.astype(BF16)
        out_ref[i] = part
        sums_ref[i : i + 1, :] = jnp.sum(part.astype(F32), axis=0, keepdims=True)


def d_input_kernel(slots, s_ref, d_ref, act_ref, time_ref, gain_ref, dres_ref, *refs):
    w, (out_ref, sums_ref, acc_ref, grad_ref) = refs[:BLOCKS], refs[BLOCKS:]
    j = pl.program_id(0)

    @pl.when(j == 0)
    def _():
        acc_ref[...] = jnp.zeros_like(acc_ref)

    acc_ref[...] += rows_by_rows(d_ref[0], rows_of(w))

    @pl.when(j == pl.num_programs(0) - 1)
    def _():
        by_block(s_ref, acc_ref, grad_ref, back=True)
        grad = grad_ref[...]
        normal, inverse = normalize(resid_zero_of(s_ref, act_ref[...], time_ref[...], 0, slots))
        d_in = dres_ref[...] + normalize_back(grad, normal, inverse, gain_ref[...])
        out_ref[...] = d_in.astype(BF16)
        sums_ref[...] = jnp.zeros_like(sums_ref)
        sums_ref[0:1, :] = jnp.sum(grad * normal, axis=0, keepdims=True)
        sums_ref[1:2, :] = jnp.sum(grad, axis=0, keepdims=True)
        for slot, inside in enumerate(members_of(s_ref, row_ids(act_ref.shape[0]), slots)):
            sums_ref[2 + slot : 3 + slot, :] = jnp.sum(jnp.where(inside, d_in, 0.0), axis=0, keepdims=True)


def grad_kernel(steps, sources, groups, s_ref, *refs):
    per = 5 * sources
    outs = refs[per * len(steps) :]
    i = pl.program_id(0)
    first = 0
    for n, (count, lead) in enumerate(steps):
        mine = refs[per * n : per * (n + 1)]

        @pl.when((i >= first) & (i < first + count))
        def _():
            product = None
            for source in range(sources):
                *a_refs, b_ref = mine[5 * source : 5 * source + 5]
                a = jnp.concatenate([ref[...] for ref in a_refs], axis=1)
                part = cols_by_cols(a, b_ref[0] if lead else b_ref[...])
                product = part if product is None else product + part
            rows = product.shape[0] // 4
            for out, group in zip(outs, groups):
                out[...] = product[group[0] * rows : (group[-1] + 1) * rows].astype(BF16)

        first += count


def weight_grad(scalars, odd, pairs, tile, after=(), groups=((0,), (1,), (2, 3))):
    tokens, width = pairs[0][0].shape[0], pairs[0][0].shape[1] // BLOCKS
    sources = len(pairs[0]) // 2
    specs, inputs, steps = [], [], []
    first = 0
    for pair in pairs:
        lead = pair[1].ndim == 3
        per = pair[1].shape[-1] // tile
        count = per * (pair[1].shape[0] if lead else 1)

        def local(i, first=first, count=count):
            return jnp.clip(i - first, 0, count - 1)

        for a, b in zip(pair[::2], pair[1::2]):
            for j in range(4):
                specs.append(pl.BlockSpec((tokens, width), lambda i, s, j=j: (0, s[2 * j + odd])))
                inputs.append(a)
            if lead:
                specs.append(
                    pl.BlockSpec((1, tokens, tile), lambda i, s, at=local, per=per: (at(i) // per, 0, at(i) % per))
                )
            else:
                specs.append(pl.BlockSpec((tokens, tile), lambda i, s, at=local: (0, at(i))))
            inputs.append(b)
        steps.append((count, lead))
        first += count
    sizes = [len(group) * width for group in groups]
    out = call(
        partial(grad_kernel, tuple(steps), sources, groups), scalars, inputs, specs,
        [jax.ShapeDtypeStruct((rows, first * tile), BF16) for rows in sizes],
        [pl.BlockSpec((rows, tile), lambda i, s: (0, i)) for rows in sizes], (first,), after=after,
    )
    return list(out)


def pack_grads_kernel(slots, s_ref, one_ref, qkv_ref, two_ref, up_ref, down_ref, time_ref, odd_ref, even_ref):
    rows = time_ref.shape[0] // BLOCKS
    d_time = one_ref[2 : 2 + slots, :]
    one, two = d_time.shape[1] // BLOCKS, 2 * d_time.shape[1] // BLOCKS
    ff = up_ref.shape[1] // BLOCKS
    odd_ref[...] = jnp.zeros_like(odd_ref)
    even_ref[...] = jnp.zeros_like(even_ref)
    for j in range(BLOCKS):
        block = s_ref[j]
        out, chip = (odd_ref, (0, 2, 1, 3)[j // 2]) if j % 2 else (even_ref, j // 2)
        features = time_ref[pl.ds(pl.multiple_of(block * rows, 8), rows), :]
        out[chip, 0:rows, :] = sum(features[:, s : s + 1] * d_time[s : s + 1, :] for s in range(slots)).astype(BF16)
        at = pl.ds(pl.multiple_of(block * one, 128), one)
        sources = (one_ref[0:1, at], one_ref[1:2, at], two_ref[2:3, at], two_ref[0:1, at], two_ref[1:2, at],
                   down_ref[0:1, at], qkv_ref[2:3, at])
        line = jnp.concatenate(sources, axis=1)
        out[chip, rows : rows + 1, 0 : line.shape[1]] = line.astype(BF16)
        wide = pl.ds(pl.multiple_of((block % 4) * two, 128), two)
        pair = jnp.where(block < 4, qkv_ref[0:1, wide], qkv_ref[1:2, wide])
        hidden = up_ref[0:1, pl.ds(pl.multiple_of(block * ff, 128), ff)]
        out[chip, rows + 1 : rows + 2, 0 : two + ff] = jnp.concatenate([pair, hidden], axis=1).astype(BF16)
        bias = jnp.sum(one_ref[2 : 2 + slots, at], axis=0, keepdims=True)
        out[chip, rows + 2 : rows + 3, 0:one] = bias.astype(BF16)


def per_device(
    n_dp, n_fsdp, activations, time_features, lengths, attn_gain, attn_shift, qkv_weight, qkv_bias, out_weight, out_bias,
    mlp_gain, mlp_shift, up_weight, up_bias, down_weight, down_bias, time_weight, time_bias, cotangent,
):
    tokens, width = activations.shape
    slots = lengths.shape[1]
    hidden = down_weight.shape[0] * n_fsdp
    small = n_fsdp == BLOCKS
    me = lax.axis_index("fsdp")
    blocks = jnp.arange(BLOCKS, dtype=jnp.int32)
    chips = jnp.arange(CHIPS, dtype=jnp.int32)
    if small:
        turned = jnp.where(chips % 3 > 0, 3 - chips, chips)
        chips = jnp.where(me % 2 == 0, turned, chips)
        blocks = (2 * chips[:, None] + jnp.arange(2, dtype=jnp.int32)[None, :]).reshape(-1) ^ me
        chips = chips ^ (me // 2)
    upto = jnp.arange(slots)[:, None] >= jnp.arange(slots)[None, :]
    ends = jnp.sum(jnp.where(upto, lengths, 0), axis=1)
    parity = lax.axis_index("dp") % 2
    scalars = jnp.concatenate([blocks, chips, parity[None], ends]).astype(jnp.int32)

    def swap(x, even, odd):
        return lax.ppermute(x, "fsdp", [(i, i ^ (odd if i % 2 else even)) for i in range(n_fsdp)])

    def sibling(x):
        return swap(x, 1, 1)

    def first_way(x):
        return swap(x, 4, 2)

    def second_way(x):
        return swap(x, 2, 4)

    def pieces(own, first, second, far, own_sibling, first_sibling, second_sibling, far_sibling):
        return [own, own_sibling, first, second_sibling, second, first_sibling, far, far_sibling]

    def add(*parts):
        total = parts[0].astype(F32)
        for part in parts[1:]:
            total = total + part.astype(F32)
        return total.astype(BF16)

    def gather_rows(w):
        return lax.all_gather(w, "fsdp", axis=0, tiled=True).reshape(BLOCKS, -1, w.shape[1])

    rows = whole((tokens, width))
    line = whole((1, width))
    vectors = [attn_gain, attn_shift, out_bias, mlp_gain, mlp_shift, down_bias, time_bias, qkv_bias, up_bias]
    per = width // BLOCKS
    qkv_columns = qkv_weight.shape[1]
    columns = qkv_columns + width
    depth = 16
    if small:
        sources = [qkv_weight, out_weight, time_weight] + vectors
        pack = call(
            pack_kernel, scalars, sources, [whole(x.shape) for x in sources],
            jax.ShapeDtypeStruct((per + depth, columns), BF16), whole((per + depth, columns)), (1,),
        )
        first_one, first_two, first_core = first_way(pack), second_way(pack), sibling(pack)
        up_own, down_own = copy_after(up_weight, pack), copy_after(down_weight, pack)
    else:
        gathered = [lax.all_gather(v, "fsdp", axis=0, tiled=True).reshape(BLOCKS, -1) for v in vectors]
        matrices = jnp.concatenate([gather_rows(qkv_weight), gather_rows(out_weight)], axis=2)
        times = lax.all_gather(time_weight, "fsdp", axis=0, tiled=True).reshape(BLOCKS, 2, depth, width)
        lines = jnp.concatenate(gathered, axis=1)
        lines = jnp.pad(lines, ((0, 0), (0, columns - 2 * width - lines.shape[1])))[:, None]
        lines = jnp.pad(lines, ((0, 0), (0, depth - 1), (0, 0)))
        extra = jnp.concatenate([times[:, 0], times[:, 1], lines], axis=2)
        first = list(jnp.concatenate([matrices, extra], axis=1))
        up_rel = list(gather_rows(up_weight))
        down_rel = list(gather_rows(down_weight))

    ids = jnp.arange(tokens, dtype=jnp.int32)[:, None]
    starts = ends - lengths[0]
    inside = (ids >= starts[None, :]) & (ids < ends[None, :])
    position = (ids[:, 0] - jnp.sum(jnp.where(inside, starts[None, :], 0), axis=1)).astype(F32)
    frequency = 10000.0 ** (-2.0 * jnp.arange(32, dtype=F32) / 64)
    angles = position[:, None] * frequency[None, :]
    cosine, sine = jnp.cos(angles), jnp.sin(angles)
    lanes = 64 * GROUP
    cos_table = jnp.tile(cosine, (1, 2 * GROUP))
    sin_table = jnp.tile(jnp.concatenate([-sine, sine], axis=1), (1, GROUP))

    d_branch, down_bias_sum = call(
        partial(branch_kernel, slots), scalars, [cotangent], [rows],
        [jax.ShapeDtypeStruct((tokens, width), BF16), jax.ShapeDtypeStruct((1, width), F32)], [rows, line], (1,),
    )
    if small:
        first_one, first_two = next_round(
            scalars, [first_one, first_two], [first_core, d_branch, up_own, down_own, cos_table, sin_table]
        )
        first_far = second_way(first_one)
        core_one, core_two, branch_core = sibling(first_one), sibling(first_two), sibling(d_branch)
        first_far, up_own = next_round(scalars, [first_far, up_own], [core_one, core_two, branch_core])
        up_one, up_two = first_way(up_own), second_way(up_own)
        first = pieces(pack, first_one, first_two, first_far, first_core, core_one, core_two, sibling(first_far))
    spread = time_features.reshape(slots, 2 * BLOCKS, -1)
    spread = jnp.pad(spread, ((0, 0), (0, 0), (0, 128 - spread.shape[2]))).reshape(slots, -1)
    extra_specs = [pl.BlockSpec((depth, columns), lambda i, s: (per // depth, 0))] * BLOCKS
    attn_in, time_rows, lines, qkv_b, up_b = call(
        partial(norm_one_kernel, slots), scalars, [activations, spread] + first,
        [rows, whole(spread.shape)] + extra_specs,
        [jax.ShapeDtypeStruct((tokens, width), BF16), jax.ShapeDtypeStruct((slots, width), F32),
         jax.ShapeDtypeStruct((8, width), F32), jax.ShapeDtypeStruct((1, qkv_columns), F32),
         jax.ShapeDtypeStruct((1, hidden), F32)],
        [rows, whole((slots, width)), whole((8, width)), whole((1, qkv_columns)), whole((1, hidden))], (1,),
        after=(d_branch,),
    )
    gain_one, shift_one, out_b, gain_two, shift_two, down_b = [lines[i : i + 1] for i in range(6)]
    groups = H // GROUP
    col = pl.BlockSpec((tokens, lanes), lambda g, s: (0, g))
    table = whole((tokens, lanes))
    mask_rooms = [pltpu.VMEM((2, tokens, lanes), BF16)] * 2
    qkv_specs = []
    for o in range(3):
        qkv_specs += piece_specs(per, lanes, lambda g, s, o=o: o * groups + g)
    queries, keys, values, attended, lse = call(
        partial(attention_kernel, slots), scalars,
        [attn_in, qkv_b, qkv_b, qkv_b, cos_table, sin_table] + first * 3,
        [rows] + [pl.BlockSpec((1, lanes), lambda g, s, o=o: (0, o * groups + g)) for o in range(3)]
        + [table, table] + qkv_specs,
        [jax.ShapeDtypeStruct((tokens, width), BF16)] * 4 + [jax.ShapeDtypeStruct((groups, tokens, 128), F32)],
        [col, col, col, col, pl.BlockSpec((1, tokens, 128), lambda g, s: (g, 0, 0))],
        (groups,), [pltpu.VMEM((tokens, width), BF16)] + mask_rooms)
    if small:
        up_one, up_two, up_own = next_round(scalars, [up_one, up_two, up_own], [attended])
        up_far = second_way(up_one)
        up_core, core_one, core_two = sibling(up_own), sibling(up_one), sibling(up_two)
        wait = (up_one,)
    else:
        wait = ()
    out_specs = piece_specs(per, width, lambda *a: qkv_columns // width)
    resid_one, mlp_in = call(
        partial(out_kernel, slots), scalars,
        [attended, activations, time_rows, out_b, gain_two, shift_two] + first,
        [rows, rows, whole((slots, width)), line, line, line] + out_specs,
        [jax.ShapeDtypeStruct((tokens, width), F32), jax.ShapeDtypeStruct((tokens, width), BF16)],
        [rows, rows], (1,), [pltpu.VMEM((tokens, width), BF16)], after=wait,
    )
    if small:
        up_far, down_own = next_round(scalars, [up_far, down_own], [core_one, core_two, up_core, mlp_in])
        up_rel = pieces(up_own, up_one, up_two, up_far, up_core, core_one, core_two, sibling(up_far))
        down_one, down_two, down_core = first_way(down_own), second_way(down_own), sibling(down_own)
        attn_in_core = sibling(attn_in)
    tile = hidden // CHIPS
    wide = pl.BlockSpec((tokens, tile), lambda i, s: (0, i))
    activated, slope = call(
        up_kernel, scalars, [mlp_in, up_b] + up_rel,
        [rows, pl.BlockSpec((1, tile), lambda i, s: (0, i))] + piece_specs(per, tile, lambda i, s: i),
        [jax.ShapeDtypeStruct((tokens, hidden), BF16)] * 2, [wide, wide], (CHIPS,),
        [pltpu.VMEM((tokens, width), BF16)])

    even_z = parity == 0

    def swap_z(x, bit):
        return lax.ppermute(x, "dp", [(i, i ^ bit) for i in range(n_dp)])

    def sum_of(*arrays, row=0, column=0, rows=None, columns=None):
        shape = arrays[0].shape
        return [(x, row, column) for x in arrays], rows or shape[0], columns or shape[1]

    def halves(*parts):
        half = parts[0].shape[0] // 2
        low, high = add(*[x[:half] for x in parts]), add(*[x[half:] for x in parts])
        return jnp.where(even_z, low, high), jnp.where(even_z, high, low)

    def quarters(*parts):
        size = parts[0].shape[0] // 4
        place = lax.axis_index("dp")
        cuts = [[lax.dynamic_slice_in_dim(x, (place ^ bits) * size, size) for x in parts] for bits in range(4)]
        return [add(*cut) for cut in cuts]

    def exchange(parts):
        return [swap_z(x, bits) for x, bits in zip(parts, (1, 2, 3))]

    def sum_four(own, came):
        one, two, three = [x.astype(F32) for x in came]
        return ((own.astype(F32) + one) + (two + three)).astype(BF16)

    def in_place(own, came):
        four = jnp.stack([own, *came]).reshape(2, 2, *own.shape)
        place = lax.axis_index("dp")
        for axis, bit in ((0, 2), (1, 1)):
            four = jnp.where((place & bit) > 0, jnp.flip(four, axis), four)
        return four.reshape(-1, own.shape[1]).astype(F32)

    def joined(own, other):
        return jnp.where(even_z, jnp.concatenate([own, other]), jnp.concatenate([other, own])).astype(F32)

    def rows_of_all(pairs, tile):
        blocks = [weight_grad(scalars, odd, pairs, tile) for odd in range(2)]
        blocks = [jnp.concatenate(x).reshape(CHIPS, -1, x[0].shape[1]) for x in blocks]
        both = jnp.stack(blocks, axis=1).reshape(-1, blocks[0].shape[2])
        return lax.psum(lax.psum_scatter(both, "fsdp", scatter_dimension=0, tiled=True), "dp").astype(F32)

    if small:
        down_one, down_two, activated = next_round(scalars, [down_one, down_two, activated], [down_core, attn_in_core])
        down_far = second_way(down_one)
        core_one, core_two, activated_core = sibling(down_one), sibling(down_two), sibling(activated)
        down_parts = weight_grad(scalars, 0, [(activated, d_branch, activated_core, branch_core)], 512)
        down_far, down_parts[2] = next_round(scalars, [down_far, down_parts[2]], [core_one, core_two])
        down_came = second_way(down_parts[2])
        down_rel = pieces(down_own, down_one, down_two, down_far, down_core, core_one, core_two, sibling(down_far))
        mlp_in_core = sibling(mlp_in)
    else:
        down_grad = rows_of_all([(activated, d_branch)], 512)

    chip_wide = pl.BlockSpec((tokens, tile), lambda i, s: (0, s[CHIP_AT + i]))
    down_rooms = [pltpu.VMEM((BLOCKS, hidden // BLOCKS, width), BF16), pltpu.SemaphoreType.DMA((BLOCKS,))]
    d_pre, up_bias_sum, d_resid_one, d_attn, sums_two = call(
        mlp_back_kernel, scalars, [d_branch, slope, resid_one, gain_two] + down_rel + up_rel,
        [rows, chip_wide, rows, line] + [pl.BlockSpec(memory_space=pl.ANY)] * BLOCKS
        + piece_specs(per, tile, lambda i, s: s[CHIP_AT + i]),
        [jax.ShapeDtypeStruct((tokens, hidden), BF16),
         jax.ShapeDtypeStruct((1, hidden), F32), jax.ShapeDtypeStruct((tokens, width), F32),
         jax.ShapeDtypeStruct((tokens, width), BF16), jax.ShapeDtypeStruct((8, width), F32)],
        [chip_wide, pl.BlockSpec((1, tile), lambda i, s: (0, s[CHIP_AT + i])), rows, rows, whole((8, width))],
        (CHIPS,), [pltpu.VMEM((tokens, width), F32)] * 2 + down_rooms,
    )
    def layer_output(after):
        return call(
            partial(down_kernel, slots), scalars, [activated, resid_one, down_b] + down_rel,
            [chip_wide, rows, line] + [pl.BlockSpec(memory_space=pl.ANY)] * BLOCKS,
            jax.ShapeDtypeStruct((tokens, width), BF16), rows, (CHIPS,), [pltpu.VMEM((tokens, width), F32)] + down_rooms,
            after=after,
        )

    if small:
        d_pre, d_attn, down_came = next_round(scalars, [d_pre, d_attn, down_came], [mlp_in_core])
        d_pre_core, d_attn_core, attended_core = sibling(d_pre), sibling(d_attn), sibling(attended)
        far = down_came.shape[0] // 2
        down_one = first_way(add(down_parts[1], down_came[far:]))
        up_parts = weight_grad(
            scalars, 0, [(mlp_in, d_pre, mlp_in_core, d_pre_core), (attended, d_attn, attended_core, d_attn_core)], width
        )
        up_parts[2], down_came, down_one = next_round(scalars, [up_parts[2], down_came, down_one])
        up_came = second_way(up_parts[2])
        down_sum, *down_send = quarters(down_parts[0], down_came, down_one)
        down_z = exchange(down_send)
        wait = (down_came,)
    else:
        up_out_grad = rows_of_all([(mlp_in, d_pre), (attended, d_attn)], width)
        up_grad, out_grad = up_out_grad[:, :hidden], up_out_grad[:, hidden:]
        wait = ()
    chip_col = pl.BlockSpec((tokens, lanes), lambda g, s: (0, s[CHIP_AT + g]))
    d_qkv, sums_qkv = call(
        partial(attention_back_kernel, slots), scalars,
        [d_attn, queries, keys, values, lse, cos_table, sin_table] + first,
        [rows, chip_col, chip_col, chip_col,
         pl.BlockSpec((1, tokens, 128), lambda g, s: (s[CHIP_AT + g], 0, 0)), table, table] + out_specs,
        [jax.ShapeDtypeStruct((3, tokens, width), BF16), jax.ShapeDtypeStruct((8, width), F32)],
        [pl.BlockSpec((3, tokens, lanes), lambda g, s: (0, 0, s[CHIP_AT + g])),
         pl.BlockSpec((8, lanes), lambda g, s: (0, s[CHIP_AT + g]))],
        (groups,), mask_rooms + [pltpu.VMEM((tokens, lanes), F32)] * 3 + [pltpu.VMEM((tokens, lanes), BF16)],
        after=wait,
    )
    if small:
        d_qkv, up_came, *down_z = next_round(scalars, [d_qkv, up_came, *down_z])
        d_qkv_core = sibling(d_qkv)
        up_one = first_way(add(up_parts[1], up_came[per:]))
        down_sum = sum_four(down_sum, down_z)
        down_z = exchange([down_sum] * 3)
    else:
        qkv_grad = rows_of_all([(attn_in, d_qkv)], width)
    input_grad, sums_one = call(
        partial(d_input_kernel, slots), scalars,
        [d_qkv, activations, time_rows, gain_one, d_resid_one] + first,
        [pl.BlockSpec((1, tokens, width), lambda i, s: (i, 0, 0)), rows, whole((slots, width)), line, rows]
        + piece_specs(per, width, lambda i, s: i),
        [jax.ShapeDtypeStruct((tokens, width), BF16), jax.ShapeDtypeStruct((8, width), F32)],
        [rows, whole((8, width))], (3,), [pltpu.VMEM((tokens, width), F32)] * 2,
    )
    if small:
        half = per // 2
        up_sum, up_send = next_round(
            scalars, [], [sums_one],
            [sum_of(up_parts[0], up_came, up_one, row=rows_, rows=half) for rows_ in ((0, half), (half, 0))],
        )
        up_z = swap_z(up_send, 1)
        qkv_parts = weight_grad(scalars, 0, [(attn_in, d_qkv, attn_in_core, d_qkv_core)], width, after=(up_sum,))
        qkv_parts[2], sums_one = next_round(scalars, [qkv_parts[2], sums_one], down_z)
        qkv_came = second_way(qkv_parts[2])
        time_cols = time_features.astype(F32).T
        depth = 64
        v_odd, v_even = call(
            partial(pack_grads_kernel, slots), scalars,
            [sums_one, sums_qkv, sums_two, up_bias_sum, down_bias_sum, time_cols],
            [whole((8, width)), whole((8, width)), whole((8, width)), whole((1, hidden)), line, whole(time_cols.shape)],
            [jax.ShapeDtypeStruct((4, depth, width), BF16)] * 2, [whole((4, depth, width))] * 2, (1,), cost=SOME_COST,
        )
        v_odd, v_even = v_odd.reshape(-1, width), v_even.reshape(-1, width)
        v_odd, up_z = next_round(scalars, [v_odd, up_z])
        up_sum = add(up_sum, up_z)
        up_z = swap_z(up_sum, 2)
        v_came = sibling(v_odd)
        v_came, down_sum, *to_one = next_round(
            scalars, [v_came, down_sum], [up_sum],
            [([(qkv_parts[1], row, 0), (qkv_came, per + row, 0)], half, qkv_columns) for row in (0, half)],
        )
        qkv_one = [first_way(x) for x in to_one]
        down_grad = in_place(down_sum, down_z)
        *qkv_one, v_came, up_z = next_round(scalars, [*qkv_one, v_came, up_z])
        low, high = [
            add(qkv_parts[0][row : row + half], qkv_came[row : row + half], x) for row, x in zip((0, half), qkv_one)
        ]
        qkv_sum, qkv_send = jnp.where(even_z, low, high), jnp.where(even_z, high, low)
        qkv_z = swap_z(qkv_send, 1)
        (up_z,) = next_round(scalars, [up_z], [qkv_send])
        up_sum = add(up_sum, up_z)
        up_z = swap_z(up_sum, 1)
        part = add(v_even, v_came).reshape(4, depth, width)
        parts = [part[k] for k in range(4)]
        v_came = [first_way(parts[1]), second_way(parts[2]), swap(parts[3], 6, 6)]
        qkv_sum, part = next_round(scalars, [], [], [sum_of(qkv_sum, qkv_z), sum_of(parts[0], *v_came)])
        qkv_z = swap_z(qkv_sum, 2)
        v_came = swap_z(part, 1)
        output = layer_output((part,))
        qkv_z, v_came = next_round(scalars, [qkv_z, v_came], [output, up_z])
        qkv_sum = add(qkv_sum, qkv_z)
        qkv_grad = joined(qkv_sum, swap_z(qkv_sum, 1))
        part = add(part, v_came)
        share = part.astype(F32) + swap_z(part, 2).astype(F32)
        up_out_grad = joined(up_sum, up_z)
        up_grad, out_grad = up_out_grad[:, :hidden], up_out_grad[:, hidden:]
        time_rows_here = time_weight.shape[0]
        time_grad = share[:time_rows_here]
        one, two, ff = width // BLOCKS, 2 * width // BLOCKS, hidden // BLOCKS
        row = share[time_rows_here]
        (gain_one_grad, shift_one_grad, out_bias_grad, gain_two_grad, shift_two_grad, down_bias_grad,
         value_bias_grad) = [row[i * one : (i + 1) * one] for i in range(7)]
        row = share[time_rows_here + 1]
        qk_bias_grad, up_bias_grad = row[:two], row[two : two + ff]
        time_bias_grad = share[time_rows_here + 2, :one]
    else:
        output = layer_output(())
        d_time = sums_one[2 : 2 + slots]
        time_grad = lax.dot_general(
            time_features.astype(F32), d_time, (((0,), (0,)), ((), ())), precision=lax.Precision.HIGHEST
        )
        vector_sums = (
            sums_one[0], sums_one[1], sums_qkv[:2].reshape(-1), sums_qkv[2], sums_two[2], sums_two[0], sums_two[1],
            up_bias_sum[0], down_bias_sum[0], jnp.sum(d_time, axis=0),
        )
        shares = jnp.concatenate(
            [time_grad.reshape(n_fsdp, -1)] + [v.reshape(n_fsdp, -1) for v in vector_sums], axis=1
        )
        sizes = [time_weight.size] + [v.size // n_fsdp for v in vector_sums]
        shares = jnp.pad(shares, ((0, 0), (0, -shares.shape[1] % 4096))).reshape(n_fsdp, -1, 128)
        shares = lax.psum_scatter(shares.astype(BF16), "fsdp", scatter_dimension=0, tiled=False)
        share = lax.psum(shares, "dp").astype(F32).reshape(-1)
        got = []
        at = 0
        for size in sizes:
            got.append(share[at : at + size])
            at += size
        (time_grad, gain_one_grad, shift_one_grad, qk_bias_grad, value_bias_grad, out_bias_grad, gain_two_grad,
         shift_two_grad, up_bias_grad, down_bias_grad, time_bias_grad) = got
    return (
        output, input_grad, gain_one_grad, shift_one_grad, qkv_grad, qk_bias_grad, value_bias_grad, out_grad, out_bias_grad,
        gain_two_grad, shift_two_grad, up_grad, up_bias_grad, down_grad, down_bias_grad,
        time_grad.reshape(time_weight.shape), time_bias_grad,
    )


def solution(mesh):
    tokens = P(("dp", "fsdp"), None)
    vector = P("fsdp")
    matrix = P("fsdp", None)
    in_specs = (
        tokens, tokens, tokens, vector, vector, matrix, vector, matrix, vector, vector, vector, matrix, vector, matrix,
        vector, matrix, vector, tokens,
    )
    out_specs = (
        tokens, tokens, vector, vector, matrix, vector, vector, matrix, vector, vector, vector, matrix, vector, matrix,
        vector, matrix, vector,
    )
    body = partial(per_device, mesh.shape["dp"], mesh.shape["fsdp"])
    return jax.shard_map(body, mesh=mesh, in_specs=in_specs, out_specs=out_specs, check_vma=False)
```

```python
from functools import partial

import jax
import jax.numpy as jnp
from jax import lax
from jax.experimental import pallas as pl
from jax.experimental.pallas import tpu as pltpu
from jax.sharding import PartitionSpec as P

H = 16
GROUP = 4
BLOCKS = 8
CHIPS = 4
CHIP_AT = BLOCKS
PARITY_AT = CHIP_AT + CHIPS
ENDS_AT = PARITY_AT + 1
FAR = -1e30
NO_COST = pl.CostEstimate(flops=0, bytes_accessed=0, transcendentals=0)
SOME_COST = pl.CostEstimate(flops=30 * 10**9, bytes_accessed=100 * 10**6, transcendentals=0)
F32 = jnp.float32
BF16 = jnp.bfloat16


def rows_by_cols(a, b):
    return lax.dot_general(a, b, (((1,), (0,)), ((), ())), preferred_element_type=F32)


def rows_by_rows(a, b):
    return lax.dot_general(a, b, (((1,), (1,)), ((), ())), preferred_element_type=F32)


def cols_by_cols(a, b):
    return lax.dot_general(a, b, (((0,), (0,)), ((), ())), preferred_element_type=F32)


def call(kernel, scalars, inputs, in_specs, out_shapes, out_specs, grid, scratch=(), aliases=None, after=(), cost=NO_COST):
    count = len(inputs)

    def body(s_ref, *refs):
        kernel(s_ref, *refs[:count], *refs[count + len(after) :])

    return pl.pallas_call(
        body,
        name=getattr(kernel, "func", kernel).__name__,
        grid_spec=pltpu.PrefetchScalarGridSpec(
            num_scalar_prefetch=1,
            grid=grid,
            in_specs=list(in_specs) + [pl.BlockSpec(memory_space=pl.ANY)] * len(after),
            out_specs=out_specs,
            scratch_shapes=list(scratch),
        ),
        out_shape=out_shapes,
        input_output_aliases=aliases or {},
        compiler_params=pltpu.CompilerParams(
            dimension_semantics=("arbitrary",) * len(grid), vmem_limit_bytes=64 * 2**20
        ),
        cost_estimate=cost,
    )(scalars, *inputs, *after)


def round_kernel(counts, s_ref, *refs):
    outs = refs[-len(counts) :] if counts else ()
    at = 0
    for count, out in zip(counts, outs):
        total = refs[at][...].astype(F32)
        for ref in refs[at + 1 : at + count]:
            total = total + ref[...].astype(F32)
        out[...] = total.astype(BF16)
        at += count


def next_round(scalars, passed, others=(), sums=()):
    anywhere = pl.BlockSpec(memory_space=pl.ANY)
    steps = 2
    specs, inputs, counts, shapes, out_specs = [], [], [], [], []
    for parts, rows, columns in sums:
        size = rows // steps
        for array, row, column in parts:
            even, odd = row if isinstance(row, tuple) else (row, row)

            def at(i, s, even=even // size, odd=odd // size, column=column // columns):
                return (i + even + s[PARITY_AT] * (odd - even), column)

            specs.append(pl.BlockSpec((size, columns), at))
            inputs.append(array)
        counts.append(len(parts))
        shapes.append(jax.ShapeDtypeStruct((rows, columns), BF16))
        out_specs.append(pl.BlockSpec((size, columns), lambda i, s: (i, 0)))
    first = len(inputs)

    def kernel(s_ref, *refs):
        given = first + len(passed) + len(others)
        round_kernel(counts, s_ref, *refs[:first], *refs[given + len(passed) :])

    out = pl.pallas_call(
        kernel,
        name="next_round",
        grid_spec=pltpu.PrefetchScalarGridSpec(
            num_scalar_prefetch=1,
            grid=(steps if sums else 1,),
            in_specs=specs + [anywhere] * (len(passed) + len(others)),
            out_specs=[anywhere] * len(passed) + out_specs,
        ),
        out_shape=[jax.ShapeDtypeStruct(x.shape, x.dtype) for x in passed] + shapes,
        input_output_aliases={1 + first + i: i for i in range(len(passed))},
        compiler_params=pltpu.CompilerParams(dimension_semantics=("arbitrary",), vmem_limit_bytes=64 * 2**20),
        cost_estimate=NO_COST,
    )(scalars, *inputs, *passed, *others)
    return list(out)


def copy_after(x, *others):
    def kernel(x_ref, *refs):
        refs[-1][...] = x_ref[...]

    block = pl.BlockSpec((x.shape[0] // 2, x.shape[1]), lambda i: (i, 0))
    return pl.pallas_call(
        kernel,
        grid=(2,),
        out_shape=jax.ShapeDtypeStruct(x.shape, x.dtype),
        in_specs=[block] + [pl.BlockSpec(memory_space=pl.ANY)] * len(others),
        out_specs=block,
        cost_estimate=NO_COST,
    )(x, *others)


def whole(shape):
    zeros = (0,) * len(shape)
    return pl.BlockSpec(shape, lambda *_: zeros)


def normalize(x):
    center = x - jnp.mean(x, axis=-1, keepdims=True)
    variance = jnp.mean(center * center, axis=-1, keepdims=True)
    inverse = lax.rsqrt(variance + 1e-05)
    return center * inverse, inverse


def normalize_back(grad, normal, inverse, gain):
    scaled = grad * gain
    return inverse * (
        scaled
        - jnp.mean(scaled, axis=-1, keepdims=True)
        - normal * jnp.mean(scaled * normal, axis=-1, keepdims=True)
    )


def row_ids(count, first=0):
    return lax.broadcasted_iota(jnp.int32, (count, 1), 0) + first


def members_of(s_ref, ids, slots):
    out = []
    start = 0
    for slot in range(slots):
        end = s_ref[ENDS_AT + slot]
        out.append((ids >= start) & (ids < end))
        start = end
    return out


def segment_of(s_ref, ids, slots):
    segment = jnp.zeros(ids.shape, jnp.int32)
    for slot in range(slots):
        segment = segment + (ids >= s_ref[ENDS_AT + slot]).astype(jnp.int32)
    return segment


def resid_zero_of(s_ref, act, time_rows, first, slots):
    x = act.astype(F32)
    for slot, inside in enumerate(members_of(s_ref, row_ids(act.shape[0], first), slots)):
        x = x + jnp.where(inside, time_rows[slot : slot + 1, :], 0.0)
    return x


def piece_specs(rows, columns, at):
    return [pl.BlockSpec((rows, columns), lambda *a: (0, at(*a)))] * BLOCKS


def rows_of(refs, at=slice(None)):
    return jnp.concatenate([ref[:, at] for ref in refs], axis=0)


def pack_kernel(s_ref, qkv_ref, out_ref, time_ref, *refs):
    vectors, pack_ref = refs[:-1], refs[-1]
    rows, columns = qkv_ref.shape
    pack_ref[0:rows, 0:columns] = qkv_ref[...]
    pack_ref[0:rows, columns:] = out_ref[...]
    depth = pack_ref.shape[0] - rows
    width = out_ref.shape[1]
    pack_ref[rows:, 0:width] = time_ref[0:depth, :]
    pack_ref[rows:, width : 2 * width] = time_ref[depth:, :]
    line = jnp.concatenate([v[...].astype(F32).reshape(1, -1) for v in vectors], axis=1)
    line = jnp.concatenate([line, jnp.zeros((1, pack_ref.shape[1] - 2 * width - line.shape[1]), F32)], axis=1)
    lines = jnp.where(row_ids(depth) == 0, line, 0.0).astype(BF16)
    pack_ref[rows:, 2 * width :] = lines


def norm_one_kernel(slots, s_ref, act_ref, feat_ref, *refs):
    extras = refs[:BLOCKS]
    out_ref, time_ref, lines_ref, qkv_b_ref, up_b_ref = refs[BLOCKS:]
    depth = extras[0].shape[0]
    width = act_ref.shape[1]
    small = width // BLOCKS
    time_rows = jnp.zeros((slots, width), F32)
    for j in range(BLOCKS):
        block = s_ref[j]
        for half in range(2):
            at = pl.multiple_of((block * 2 + half) * 128, 128)
            part = feat_ref[:, pl.ds(at, 128)]
            time_rows = time_rows + rows_by_cols(part[:, 0:depth], extras[j][:, half * width : (half + 1) * width])
        line = extras[j][:, 2 * width :].astype(F32)[0:1]
        at = pl.ds(pl.multiple_of(block * small, 128), small)
        for v in range(7):
            lines_ref[v : v + 1, at] = line[:, v * small : (v + 1) * small]
        first = 7 * small
        for ref in (qkv_b_ref, up_b_ref):
            size = ref.shape[1] // BLOCKS
            ref[0:1, pl.ds(pl.multiple_of(block * size, 128), size)] = line[:, first : first + size]
            first += size
    lines_ref[7:8, :] = jnp.zeros((1, width), F32)
    time_rows = time_rows + lines_ref[6:7, :]
    time_ref[...] = time_rows
    x = resid_zero_of(s_ref, act_ref[...], time_rows, 0, slots)
    normal, _ = normalize(x)
    out_ref[...] = (normal * lines_ref[0:1, :] + lines_ref[1:2, :]).astype(BF16)


def by_block(s_ref, x_ref, out_ref, back=False):
    width = x_ref.shape[1] // BLOCKS
    for j in range(BLOCKS):
        at = pl.ds(pl.multiple_of(s_ref[j] * width, 128), width)
        if back:
            out_ref[:, at] = x_ref[:, j * width : (j + 1) * width]
        else:
            out_ref[:, j * width : (j + 1) * width] = x_ref[:, at]


def turn(x, cosine, sine):
    lanes = lax.broadcasted_iota(jnp.int32, x.shape, 1)
    width = x.shape[1]
    swapped = jnp.where(lanes % 64 < 32, pltpu.roll(x, width - 32, 1), pltpu.roll(x, 32, 1))
    return x * cosine + swapped * sine


def lane_ids(width):
    return lax.broadcasted_iota(jnp.int32, (1, width), 1)


def head_lanes(h, width):
    lanes = lane_ids(width)
    return (lanes >= h * 64) & (lanes < (h + 1) * 64)


def spare_head(h):
    return 1 if h == 0 else 0


def mask_lanes(s_ref, tokens, width, slots, query_ref, key_ref):
    segment = segment_of(s_ref, row_ids(tokens), slots)
    for p in range(2):
        at = lane_ids(width) - 64 * p
        inside = (at >= 0) & (at <= slots)
        more = (at > slots) & (at <= slots + 3)
        query_ref[p] = jnp.where(inside & (at != segment), FAR, 0.0).astype(BF16)
        key_ref[p] = jnp.where((inside & (at == segment)) | more, 1.0, 0.0).astype(BF16)


def attention_kernel(slots, s_ref, x_ref, bq_ref, bk_ref, bv_ref, cos_ref, sin_ref, *refs):
    wq, wk, wv = refs[:BLOCKS], refs[BLOCKS : 2 * BLOCKS], refs[2 * BLOCKS : 3 * BLOCKS]
    q_ref, k_ref, v_ref, att_ref, lse_ref, rel_ref, qm_ref, km_ref = refs[3 * BLOCKS :]
    tokens, width = q_ref.shape

    @pl.when(pl.program_id(0) == 0)
    def _():
        by_block(s_ref, x_ref, rel_ref)
        mask_lanes(s_ref, tokens, width, slots, qm_ref, km_ref)

    x = rel_ref[...]
    cosine, sine = cos_ref[...], sin_ref[...]
    q = turn(rows_by_cols(x, rows_of(wq)) + bq_ref[...], cosine, sine).astype(BF16)
    k = turn(rows_by_cols(x, rows_of(wk)) + bk_ref[...], cosine, sine).astype(BF16)
    v = (rows_by_cols(x, rows_of(wv)) + bv_ref[...]).astype(BF16)
    q = q * jnp.asarray(0.125, BF16)
    q_ref[...] = q
    k_ref[...] = k
    v_ref[...] = v
    masked_keys = [jnp.where(head_lanes(p, width), km_ref[p], k) for p in range(2)]
    total = jnp.zeros((tokens, width), F32)
    lse = jnp.zeros((tokens, 128), F32)
    for h in range(GROUP):
        p = spare_head(h)
        mine = head_lanes(h, width)
        scores = rows_by_rows(jnp.where(mine, q, qm_ref[p]), masked_keys[p])
        top = jnp.max(scores, axis=1, keepdims=True)
        e = jnp.exp(scores - top)
        denominator = jnp.sum(e, axis=1, keepdims=True)
        part = rows_by_cols(e.astype(BF16), v) * (1.0 / denominator)
        total = jnp.where(mine, part, total)
        lse = jnp.where(lane_ids(128) == h, top + jnp.log(denominator), lse)
    att_ref[...] = total.astype(BF16)
    lse_ref[0] = lse


def out_kernel(slots, s_ref, att_ref, act_ref, time_ref, bias_ref, gain_ref, shift_ref, *refs):
    w, (res_ref, mlp_ref, rel_ref) = refs[:BLOCKS], refs[BLOCKS:]
    by_block(s_ref, att_ref, rel_ref)
    x = resid_zero_of(s_ref, act_ref[...], time_ref[...], 0, slots)
    x = x + rows_by_cols(rel_ref[...], rows_of(w)) + bias_ref[...]
    res_ref[...] = x
    normal, _ = normalize(x)
    mlp_ref[...] = (normal * gain_ref[...] + shift_ref[...]).astype(BF16)


def up_kernel(s_ref, x_ref, bias_ref, *refs):
    w, (act_ref, slope_ref, rel_ref) = refs[:BLOCKS], refs[BLOCKS:]

    @pl.when(pl.program_id(0) == 0)
    def _():
        by_block(s_ref, x_ref, rel_ref)

    pre = rows_by_cols(rel_ref[...], rows_of(w)) + bias_ref[...]
    cdf = 0.5 + 0.5 * lax.erf(pre * 0.7071067811865476)
    density = 0.3989422804014327 * jnp.exp(-0.5 * pre * pre)
    act_ref[...] = (pre * cdf).astype(BF16)
    slope_ref[...] = (cdf + pre * density).astype(BF16)


def down_copies(refs, held_ref, sems):
    return [(n // 2, pltpu.make_async_copy(ref, held_ref.at[n], sems.at[n])) for n, ref in enumerate(refs)]


def fetch_down(step, copies):
    @pl.when(step == 0)
    def _():
        for _, copy in copies:
            copy.start()

    for chip in range(CHIPS):

        @pl.when(step == chip)
        def _():
            for owner, copy in copies:
                if owner == chip:
                    copy.wait()


def halves_of(s_ref, width):
    core = s_ref[0] % 2
    return [pl.ds(pl.multiple_of(at * width, 128), width) for at in (core, 1 - core)]


def down_kernel(slots, s_ref, a_ref, res_ref, bias_ref, *refs):
    w, (out_ref, acc_ref, held_ref, sems) = refs[:BLOCKS], refs[BLOCKS:]
    c = pl.program_id(0)
    fetch_down(c, down_copies(w, held_ref, sems))

    @pl.when(c == 0)
    def _():
        acc_ref[...] = res_ref[...] + bias_ref[...]

    for n, at in enumerate(halves_of(s_ref, held_ref.shape[1])):
        acc_ref[...] += rows_by_cols(a_ref[:, at], held_ref[2 * c + n])

    @pl.when(c == pl.num_programs(0) - 1)
    def _():
        valid = row_ids(out_ref.shape[0]) < s_ref[ENDS_AT + slots - 1]
        out_ref[...] = jnp.where(valid, acc_ref[...], 0.0).astype(BF16)


def branch_kernel(slots, s_ref, cot_ref, branch_ref, bias_ref):
    valid = row_ids(cot_ref.shape[0]) < s_ref[ENDS_AT + slots - 1]
    branch = jnp.where(valid, cot_ref[...].astype(F32), 0.0)
    branch_ref[...] = branch.astype(BF16)
    bias_ref[...] = jnp.sum(branch, axis=0, keepdims=True)


def mlp_back_kernel(s_ref, branch_ref, slope_ref, res_ref, gain_ref, *refs):
    down, up = refs[:BLOCKS], refs[BLOCKS : 2 * BLOCKS]
    pre_ref, bias_ref, dres_ref, datt_ref, sums_ref, acc_ref, grad_ref, held_ref, sems = refs[2 * BLOCKS :]
    c = pl.program_id(0)
    fetch_down(c, down_copies(down, held_ref, sems))

    @pl.when(c == 0)
    def _():
        acc_ref[...] = jnp.zeros_like(acc_ref)

    branch = branch_ref[...]
    for n, at in enumerate(halves_of(s_ref, held_ref.shape[1])):
        d_pre = (rows_by_rows(branch, held_ref[2 * c + n]) * slope_ref[:, at].astype(F32)).astype(BF16)
        pre_ref[:, at] = d_pre
        bias_ref[:, at] = jnp.sum(d_pre.astype(F32), axis=0, keepdims=True)
        acc_ref[...] += rows_by_rows(d_pre, rows_of(up, at))

    @pl.when(c == pl.num_programs(0) - 1)
    def _():
        by_block(s_ref, acc_ref, grad_ref, back=True)
        grad = grad_ref[...]
        normal, inverse = normalize(res_ref[...])
        d_res = branch.astype(F32) + normalize_back(grad, normal, inverse, gain_ref[...])
        dres_ref[...] = d_res
        d_att = d_res.astype(BF16)
        datt_ref[...] = d_att
        sums_ref[0:1, :] = jnp.sum(grad * normal, axis=0, keepdims=True)
        sums_ref[1:2, :] = jnp.sum(grad, axis=0, keepdims=True)
        sums_ref[2:3, :] = jnp.sum(d_att.astype(F32), axis=0, keepdims=True)
        sums_ref[3:8, :] = jnp.zeros((5, sums_ref.shape[1]), F32)


def three_lanes(x, p, slots):
    first = x.astype(BF16)
    rest = x - first.astype(F32)
    second = rest.astype(BF16)
    third = (rest - second.astype(F32)).astype(BF16)
    at = lane_ids(64 * GROUP) - 64 * p - slots - 1
    spread = jnp.where(at == 0, first, jnp.where(at == 1, second, third))
    return jnp.where((at >= 0) & (at < 3), spread, jnp.zeros((), BF16))


def attention_back_kernel(slots, s_ref, d_ref, q_ref, k_ref, v_ref, lse_ref, cos_ref, sin_ref, *refs):
    w, (out_ref, sums_ref, qm_ref, km_ref, dq_ref, dk_ref, dv_ref, heads_ref) = refs[:BLOCKS], refs[BLOCKS:]
    tokens, width = q_ref.shape
    step = pl.program_id(0)

    @pl.when(pl.program_id(0) == 0)
    def _():
        mask_lanes(s_ref, tokens, width, slots, qm_ref, km_ref)

    for chip, pieces in enumerate((w[0:2], w[2:4], w[4:6], w[6:8])):

        @pl.when(step == chip)
        def _():
            both = rows_by_rows(d_ref[...], rows_of(pieces)).astype(BF16)
            for n, at in enumerate(halves_of(s_ref, width // 2)):
                heads_ref[:, at] = both[:, n * (width // 2) : (n + 1) * (width // 2)]

    d_heads = heads_ref[...]
    q, k, v = q_ref[...], k_ref[...], v_ref[...]
    for h in range(GROUP):
        p = spare_head(h)
        mine, spare = head_lanes(h, width), head_lanes(p, width)
        queries = jnp.where(spare, qm_ref[p] + three_lanes(-lse_ref[0, :, h : h + 1], p, slots), q)
        soft = jnp.exp(rows_by_rows(jnp.where(mine, k, km_ref[p]), queries))
        product = soft * rows_by_rows(jnp.where(mine, v, jnp.zeros((), BF16)), d_heads)
        row_terms = jnp.sum(product, axis=0, keepdims=True)
        d_scores = (product - soft * row_terms).astype(BF16)
        d_v = rows_by_cols(soft.astype(BF16), d_heads)
        d_k = rows_by_cols(d_scores, q)
        d_q = cols_by_cols(d_scores, k)
        if h == 0:
            dq_ref[...], dk_ref[...], dv_ref[...] = d_q, d_k, d_v
        else:
            dq_ref[...] = jnp.where(mine, d_q, dq_ref[...])
            dk_ref[...] = jnp.where(mine, d_k, dk_ref[...])
            dv_ref[...] = jnp.where(mine, d_v, dv_ref[...])
    cosine, sine = cos_ref[...], sin_ref[...]
    sums_ref[...] = jnp.zeros_like(sums_ref)
    parts = (turn(dq_ref[...] * 0.125, cosine, -sine), turn(dk_ref[...], cosine, -sine), dv_ref[...])
    for i, part in enumerate(parts):
        part = part.astype(BF16)
        out_ref[i] = part
        sums_ref[i : i + 1, :] = jnp.sum(part.astype(F32), axis=0, keepdims=True)


def d_input_kernel(slots, s_ref, d_ref, act_ref, time_ref, gain_ref, dres_ref, *refs):
    w, (out_ref, sums_ref, acc_ref, grad_ref) = refs[:BLOCKS], refs[BLOCKS:]
    j = pl.program_id(0)

    @pl.when(j == 0)
    def _():
        acc_ref[...] = jnp.zeros_like(acc_ref)

    acc_ref[...] += rows_by_rows(d_ref[0], rows_of(w))

    @pl.when(j == pl.num_programs(0) - 1)
    def _():
        by_block(s_ref, acc_ref, grad_ref, back=True)
        grad = grad_ref[...]
        normal, inverse = normalize(resid_zero_of(s_ref, act_ref[...], time_ref[...], 0, slots))
        d_in = dres_ref[...] + normalize_back(grad, normal, inverse, gain_ref[...])
        out_ref[...] = d_in.astype(BF16)
        sums_ref[...] = jnp.zeros_like(sums_ref)
        sums_ref[0:1, :] = jnp.sum(grad * normal, axis=0, keepdims=True)
        sums_ref[1:2, :] = jnp.sum(grad, axis=0, keepdims=True)
        for slot, inside in enumerate(members_of(s_ref, row_ids(act_ref.shape[0]), slots)):
            sums_ref[2 + slot : 3 + slot, :] = jnp.sum(jnp.where(inside, d_in, 0.0), axis=0, keepdims=True)


def grad_kernel(steps, sources, groups, s_ref, *refs):
    per = 5 * sources
    outs = refs[per * len(steps) :]
    i = pl.program_id(0)
    first = 0
    for n, (count, lead) in enumerate(steps):
        mine = refs[per * n : per * (n + 1)]

        @pl.when((i >= first) & (i < first + count))
        def _():
            product = None
            for source in range(sources):
                *a_refs, b_ref = mine[5 * source : 5 * source + 5]
                a = jnp.concatenate([ref[...] for ref in a_refs], axis=1)
                part = cols_by_cols(a, b_ref[0] if lead else b_ref[...])
                product = part if product is None else product + part
            rows = product.shape[0] // 4
            for out, group in zip(outs, groups):
                out[...] = product[group[0] * rows : (group[-1] + 1) * rows].astype(BF16)

        first += count


def weight_grad(scalars, odd, pairs, tile, after=(), groups=((0,), (1,), (2, 3))):
    tokens, width = pairs[0][0].shape[0], pairs[0][0].shape[1] // BLOCKS
    sources = len(pairs[0]) // 2
    specs, inputs, steps = [], [], []
    first = 0
    for pair in pairs:
        lead = pair[1].ndim == 3
        per = pair[1].shape[-1] // tile
        count = per * (pair[1].shape[0] if lead else 1)

        def local(i, first=first, count=count):
            return jnp.clip(i - first, 0, count - 1)

        for a, b in zip(pair[::2], pair[1::2]):
            for j in range(4):
                specs.append(pl.BlockSpec((tokens, width), lambda i, s, j=j: (0, s[2 * j + odd])))
                inputs.append(a)
            if lead:
                specs.append(
                    pl.BlockSpec((1, tokens, tile), lambda i, s, at=local, per=per: (at(i) // per, 0, at(i) % per))
                )
            else:
                specs.append(pl.BlockSpec((tokens, tile), lambda i, s, at=local: (0, at(i))))
            inputs.append(b)
        steps.append((count, lead))
        first += count
    sizes = [len(group) * width for group in groups]
    out = call(
        partial(grad_kernel, tuple(steps), sources, groups), scalars, inputs, specs,
        [jax.ShapeDtypeStruct((rows, first * tile), BF16) for rows in sizes],
        [pl.BlockSpec((rows, tile), lambda i, s: (0, i)) for rows in sizes], (first,), after=after,
    )
    return list(out)


def pack_grads_kernel(slots, s_ref, one_ref, qkv_ref, two_ref, up_ref, down_ref, time_ref, odd_ref, even_ref):
    rows = time_ref.shape[0] // BLOCKS
    d_time = one_ref[2 : 2 + slots, :]
    one, two = d_time.shape[1] // BLOCKS, 2 * d_time.shape[1] // BLOCKS
    ff = up_ref.shape[1] // BLOCKS
    odd_ref[...] = jnp.zeros_like(odd_ref)
    even_ref[...] = jnp.zeros_like(even_ref)
    for j in range(BLOCKS):
        block = s_ref[j]
        out, chip = (odd_ref, (0, 2, 1, 3)[j // 2]) if j % 2 else (even_ref, j // 2)
        features = time_ref[pl.ds(pl.multiple_of(block * rows, 8), rows), :]
        out[chip, 0:rows, :] = sum(features[:, s : s + 1] * d_time[s : s + 1, :] for s in range(slots)).astype(BF16)
        at = pl.ds(pl.multiple_of(block * one, 128), one)
        sources = (one_ref[0:1, at], one_ref[1:2, at], two_ref[2:3, at], two_ref[0:1, at], two_ref[1:2, at],
                   down_ref[0:1, at], qkv_ref[2:3, at])
        line = jnp.concatenate(sources, axis=1)
        out[chip, rows : rows + 1, 0 : line.shape[1]] = line.astype(BF16)
        wide = pl.ds(pl.multiple_of((block % 4) * two, 128), two)
        pair = jnp.where(block < 4, qkv_ref[0:1, wide], qkv_ref[1:2, wide])
        hidden = up_ref[0:1, pl.ds(pl.multiple_of(block * ff, 128), ff)]
        out[chip, rows + 1 : rows + 2, 0 : two + ff] = jnp.concatenate([pair, hidden], axis=1).astype(BF16)
        bias = jnp.sum(one_ref[2 : 2 + slots, at], axis=0, keepdims=True)
        out[chip, rows + 2 : rows + 3, 0:one] = bias.astype(BF16)


def per_device(
    n_dp, n_fsdp, activations, time_features, lengths, attn_gain, attn_shift, qkv_weight, qkv_bias, out_weight, out_bias,
    mlp_gain, mlp_shift, up_weight, up_bias, down_weight, down_bias, time_weight, time_bias, cotangent,
):
    tokens, width = activations.shape
    slots = lengths.shape[1]
    hidden = down_weight.shape[0] * n_fsdp
    small = n_fsdp == BLOCKS
    me = lax.axis_index("fsdp")
    blocks = jnp.arange(BLOCKS, dtype=jnp.int32)
    chips = jnp.arange(CHIPS, dtype=jnp.int32)
    if small:
        turned = jnp.where(chips % 3 > 0, 3 - chips, chips)
        chips = jnp.where(me % 2 == 0, turned, chips)
        blocks = (2 * chips[:, None] + jnp.arange(2, dtype=jnp.int32)[None, :]).reshape(-1) ^ me
        chips = chips ^ (me // 2)
    upto = jnp.arange(slots)[:, None] >= jnp.arange(slots)[None, :]
    ends = jnp.sum(jnp.where(upto, lengths, 0), axis=1)
    parity = lax.axis_index("dp") % 2
    scalars = jnp.concatenate([blocks, chips, parity[None], ends]).astype(jnp.int32)

    def swap(x, even, odd):
        return lax.ppermute(x, "fsdp", [(i, i ^ (odd if i % 2 else even)) for i in range(n_fsdp)])

    def sibling(x):
        return swap(x, 1, 1)

    def first_way(x):
        return swap(x, 4, 2)

    def second_way(x):
        return swap(x, 2, 4)

    def pieces(own, first, second, far, own_sibling, first_sibling, second_sibling, far_sibling):
        return [own, own_sibling, first, second_sibling, second, first_sibling, far, far_sibling]

    def add(*parts):
        total = parts[0].astype(F32)
        for part in parts[1:]:
            total = total + part.astype(F32)
        return total.astype(BF16)

    def gather_rows(w):
        return lax.all_gather(w, "fsdp", axis=0, tiled=True).reshape(BLOCKS, -1, w.shape[1])

    rows = whole((tokens, width))
    line = whole((1, width))
    vectors = [attn_gain, attn_shift, out_bias, mlp_gain, mlp_shift, down_bias, time_bias, qkv_bias, up_bias]
    per = width // BLOCKS
    qkv_columns = qkv_weight.shape[1]
    columns = qkv_columns + width
    depth = 16
    if small:
        sources = [qkv_weight, out_weight, time_weight] + vectors
        pack = call(
            pack_kernel, scalars, sources, [whole(x.shape) for x in sources],
            jax.ShapeDtypeStruct((per + depth, columns), BF16), whole((per + depth, columns)), (1,),
        )
        first_one, first_two, first_core = first_way(pack), second_way(pack), sibling(pack)
        up_own, down_own = copy_after(up_weight, pack), copy_after(down_weight, pack)
    else:
        gathered = [lax.all_gather(v, "fsdp", axis=0, tiled=True).reshape(BLOCKS, -1) for v in vectors]
        matrices = jnp.concatenate([gather_rows(qkv_weight), gather_rows(out_weight)], axis=2)
        times = lax.all_gather(time_weight, "fsdp", axis=0, tiled=True).reshape(BLOCKS, 2, depth, width)
        lines = jnp.concatenate(gathered, axis=1)
        lines = jnp.pad(lines, ((0, 0), (0, columns - 2 * width - lines.shape[1])))[:, None]
        lines = jnp.pad(lines, ((0, 0), (0, depth - 1), (0, 0)))
        extra = jnp.concatenate([times[:, 0], times[:, 1], lines], axis=2)
        first = list(jnp.concatenate([matrices, extra], axis=1))
        up_rel = list(gather_rows(up_weight))
        down_rel = list(gather_rows(down_weight))

    ids = jnp.arange(tokens, dtype=jnp.int32)[:, None]
    starts = ends - lengths[0]
    inside = (ids >= starts[None, :]) & (ids < ends[None, :])
    position = (ids[:, 0] - jnp.sum(jnp.where(inside, starts[None, :], 0), axis=1)).astype(F32)
    frequency = 10000.0 ** (-2.0 * jnp.arange(32, dtype=F32) / 64)
    angles = position[:, None] * frequency[None, :]
    cosine, sine = jnp.cos(angles), jnp.sin(angles)
    lanes = 64 * GROUP
    cos_table = jnp.tile(cosine, (1, 2 * GROUP))
    sin_table = jnp.tile(jnp.concatenate([-sine, sine], axis=1), (1, GROUP))

    d_branch, down_bias_sum = call(
        partial(branch_kernel, slots), scalars, [cotangent], [rows],
        [jax.ShapeDtypeStruct((tokens, width), BF16), jax.ShapeDtypeStruct((1, width), F32)], [rows, line], (1,),
    )
    if small:
        first_one, first_two = next_round(
            scalars, [first_one, first_two], [first_core, d_branch, up_own, down_own, cos_table, sin_table]
        )
        first_far = second_way(first_one)
        core_one, core_two, branch_core = sibling(first_one), sibling(first_two), sibling(d_branch)
        first_far, up_own = next_round(scalars, [first_far, up_own], [core_one, core_two, branch_core])
        up_one, up_two = first_way(up_own), second_way(up_own)
        first = pieces(pack, first_one, first_two, first_far, first_core, core_one, core_two, sibling(first_far))
    spread = time_features.reshape(slots, 2 * BLOCKS, -1)
    spread = jnp.pad(spread, ((0, 0), (0, 0), (0, 128 - spread.shape[2]))).reshape(slots, -1)
    extra_specs = [pl.BlockSpec((depth, columns), lambda i, s: (per // depth, 0))] * BLOCKS
    attn_in, time_rows, lines, qkv_b, up_b = call(
        partial(norm_one_kernel, slots), scalars, [activations, spread] + first,
        [rows, whole(spread.shape)] + extra_specs,
        [jax.ShapeDtypeStruct((tokens, width), BF16), jax.ShapeDtypeStruct((slots, width), F32),
         jax.ShapeDtypeStruct((8, width), F32), jax.ShapeDtypeStruct((1, qkv_columns), F32),
         jax.ShapeDtypeStruct((1, hidden), F32)],
        [rows, whole((slots, width)), whole((8, width)), whole((1, qkv_columns)), whole((1, hidden))], (1,),
        after=(d_branch,),
    )
    gain_one, shift_one, out_b, gain_two, shift_two, down_b = [lines[i : i + 1] for i in range(6)]
    groups = H // GROUP
    col = pl.BlockSpec((tokens, lanes), lambda g, s: (0, g))
    table = whole((tokens, lanes))
    mask_rooms = [pltpu.VMEM((2, tokens, lanes), BF16)] * 2
    qkv_specs = []
    for o in range(3):
        qkv_specs += piece_specs(per, lanes, lambda g, s, o=o: o * groups + g)
    queries, keys, values, attended, lse = call(
        partial(attention_kernel, slots), scalars,
        [attn_in, qkv_b, qkv_b, qkv_b, cos_table, sin_table] + first * 3,
        [rows] + [pl.BlockSpec((1, lanes), lambda g, s, o=o: (0, o * groups + g)) for o in range(3)]
        + [table, table] + qkv_specs,
        [jax.ShapeDtypeStruct((tokens, width), BF16)] * 4 + [jax.ShapeDtypeStruct((groups, tokens, 128), F32)],
        [col, col, col, col, pl.BlockSpec((1, tokens, 128), lambda g, s: (g, 0, 0))],
        (groups,), [pltpu.VMEM((tokens, width), BF16)] + mask_rooms)
    if small:
        up_one, up_two, up_own = next_round(scalars, [up_one, up_two, up_own], [attended])
        up_far = second_way(up_one)
        up_core, core_one, core_two = sibling(up_own), sibling(up_one), sibling(up_two)
        wait = (up_one,)
    else:
        wait = ()
    out_specs = piece_specs(per, width, lambda *a: qkv_columns // width)
    resid_one, mlp_in = call(
        partial(out_kernel, slots), scalars,
        [attended, activations, time_rows, out_b, gain_two, shift_two] + first,
        [rows, rows, whole((slots, width)), line, line, line] + out_specs,
        [jax.ShapeDtypeStruct((tokens, width), F32), jax.ShapeDtypeStruct((tokens, width), BF16)],
        [rows, rows], (1,), [pltpu.VMEM((tokens, width), BF16)], after=wait,
    )
    if small:
        up_far, down_own = next_round(scalars, [up_far, down_own], [core_one, core_two, up_core, mlp_in])
        up_rel = pieces(up_own, up_one, up_two, up_far, up_core, core_one, core_two, sibling(up_far))
        down_one, down_two, down_core = first_way(down_own), second_way(down_own), sibling(down_own)
        attn_in_core = sibling(attn_in)
    tile = hidden // CHIPS
    wide = pl.BlockSpec((tokens, tile), lambda i, s: (0, i))
    activated, slope = call(
        up_kernel, scalars, [mlp_in, up_b] + up_rel,
        [rows, pl.BlockSpec((1, tile), lambda i, s: (0, i))] + piece_specs(per, tile, lambda i, s: i),
        [jax.ShapeDtypeStruct((tokens, hidden), BF16)] * 2, [wide, wide], (CHIPS,),
        [pltpu.VMEM((tokens, width), BF16)])

    even_z = parity == 0

    def swap_z(x, bit):
        return lax.ppermute(x, "dp", [(i, i ^ bit) for i in range(n_dp)])

    def sum_of(*arrays, row=0, column=0, rows=None, columns=None):
        shape = arrays[0].shape
        return [(x, row, column) for x in arrays], rows or shape[0], columns or shape[1]

    def halves(*parts):
        half = parts[0].shape[0] // 2
        low, high = add(*[x[:half] for x in parts]), add(*[x[half:] for x in parts])
        return jnp.where(even_z, low, high), jnp.where(even_z, high, low)

    def quarters(*parts):
        size = parts[0].shape[0] // 4
        place = lax.axis_index("dp")
        cuts = [[lax.dynamic_slice_in_dim(x, (place ^ bits) * size, size) for x in parts] for bits in range(4)]
        return [add(*cut) for cut in cuts]

    def exchange(parts):
        return [swap_z(x, bits) for x, bits in zip(parts, (1, 2, 3))]

    def sum_four(own, came):
        one, two, three = [x.astype(F32) for x in came]
        return ((own.astype(F32) + one) + (two + three)).astype(BF16)

    def in_place(own, came):
        four = jnp.stack([own, *came]).reshape(2, 2, *own.shape)
        place = lax.axis_index("dp")
        for axis, bit in ((0, 2), (1, 1)):
            four = jnp.where((place & bit) > 0, jnp.flip(four, axis), four)
        return four.reshape(-1, own.shape[1]).astype(F32)

    def joined(own, other):
        return jnp.where(even_z, jnp.concatenate([own, other]), jnp.concatenate([other, own])).astype(F32)

    def rows_of_all(pairs, tile):
        blocks = [weight_grad(scalars, odd, pairs, tile) for odd in range(2)]
        blocks = [jnp.concatenate(x).reshape(CHIPS, -1, x[0].shape[1]) for x in blocks]
        both = jnp.stack(blocks, axis=1).reshape(-1, blocks[0].shape[2])
        return lax.psum(lax.psum_scatter(both, "fsdp", scatter_dimension=0, tiled=True), "dp").astype(F32)

    if small:
        down_one, down_two, activated = next_round(scalars, [down_one, down_two, activated], [down_core, attn_in_core])
        down_far = second_way(down_one)
        core_one, core_two, activated_core = sibling(down_one), sibling(down_two), sibling(activated)
        down_parts = weight_grad(scalars, 0, [(activated, d_branch, activated_core, branch_core)], 512)
        down_far, down_parts[2] = next_round(scalars, [down_far, down_parts[2]], [core_one, core_two])
        down_came = second_way(down_parts[2])
        down_rel = pieces(down_own, down_one, down_two, down_far, down_core, core_one, core_two, sibling(down_far))
        mlp_in_core = sibling(mlp_in)
    else:
        down_grad = rows_of_all([(activated, d_branch)], 512)

    chip_wide = pl.BlockSpec((tokens, tile), lambda i, s: (0, s[CHIP_AT + i]))
    down_rooms = [pltpu.VMEM((BLOCKS, hidden // BLOCKS, width), BF16), pltpu.SemaphoreType.DMA((BLOCKS,))]
    d_pre, up_bias_sum, d_resid_one, d_attn, sums_two = call(
        mlp_back_kernel, scalars, [d_branch, slope, resid_one, gain_two] + down_rel + up_rel,
        [rows, chip_wide, rows, line] + [pl.BlockSpec(memory_space=pl.ANY)] * BLOCKS
        + piece_specs(per, tile, lambda i, s: s[CHIP_AT + i]),
        [jax.ShapeDtypeStruct((tokens, hidden), BF16),
         jax.ShapeDtypeStruct((1, hidden), F32), jax.ShapeDtypeStruct((tokens, width), F32),
         jax.ShapeDtypeStruct((tokens, width), BF16), jax.ShapeDtypeStruct((8, width), F32)],
        [chip_wide, pl.BlockSpec((1, tile), lambda i, s: (0, s[CHIP_AT + i])), rows, rows, whole((8, width))],
        (CHIPS,), [pltpu.VMEM((tokens, width), F32)] * 2 + down_rooms,
    )
    def layer_output(after):
        return call(
            partial(down_kernel, slots), scalars, [activated, resid_one, down_b] + down_rel,
            [chip_wide, rows, line] + [pl.BlockSpec(memory_space=pl.ANY)] * BLOCKS,
            jax.ShapeDtypeStruct((tokens, width), BF16), rows, (CHIPS,), [pltpu.VMEM((tokens, width), F32)] + down_rooms,
            after=after,
        )

    if small:
        d_pre, d_attn, down_came = next_round(scalars, [d_pre, d_attn, down_came], [mlp_in_core])
        d_pre_core, d_attn_core, attended_core = sibling(d_pre), sibling(d_attn), sibling(attended)
        far = down_came.shape[0] // 2
        down_one = first_way(add(down_parts[1], down_came[far:]))
        up_parts = weight_grad(
            scalars, 0, [(mlp_in, d_pre, mlp_in_core, d_pre_core), (attended, d_attn, attended_core, d_attn_core)], width
        )
        up_parts[2], down_came, down_one = next_round(scalars, [up_parts[2], down_came, down_one])
        up_came = second_way(up_parts[2])
        down_sum, *down_send = quarters(down_parts[0], down_came, down_one)
        down_z = exchange(down_send)
        wait = (down_came,)
    else:
        up_out_grad = rows_of_all([(mlp_in, d_pre), (attended, d_attn)], width)
        up_grad, out_grad = up_out_grad[:, :hidden], up_out_grad[:, hidden:]
        wait = ()
    chip_col = pl.BlockSpec((tokens, lanes), lambda g, s: (0, s[CHIP_AT + g]))
    d_qkv, sums_qkv = call(
        partial(attention_back_kernel, slots), scalars,
        [d_attn, queries, keys, values, lse, cos_table, sin_table] + first,
        [rows, chip_col, chip_col, chip_col,
         pl.BlockSpec((1, tokens, 128), lambda g, s: (s[CHIP_AT + g], 0, 0)), table, table] + out_specs,
        [jax.ShapeDtypeStruct((3, tokens, width), BF16), jax.ShapeDtypeStruct((8, width), F32)],
        [pl.BlockSpec((3, tokens, lanes), lambda g, s: (0, 0, s[CHIP_AT + g])),
         pl.BlockSpec((8, lanes), lambda g, s: (0, s[CHIP_AT + g]))],
        (groups,), mask_rooms + [pltpu.VMEM((tokens, lanes), F32)] * 3 + [pltpu.VMEM((tokens, lanes), BF16)],
        after=wait,
    )
    if small:
        d_qkv, up_came, *down_z = next_round(scalars, [d_qkv, up_came, *down_z])
        d_qkv_core = sibling(d_qkv)
        up_one = first_way(add(up_parts[1], up_came[per:]))
        down_sum = sum_four(down_sum, down_z)
        down_z = exchange([down_sum] * 3)
    else:
        qkv_grad = rows_of_all([(attn_in, d_qkv)], width)
    input_grad, sums_one = call(
        partial(d_input_kernel, slots), scalars,
        [d_qkv, activations, time_rows, gain_one, d_resid_one] + first,
        [pl.BlockSpec((1, tokens, width), lambda i, s: (i, 0, 0)), rows, whole((slots, width)), line, rows]
        + piece_specs(per, width, lambda i, s: i),
        [jax.ShapeDtypeStruct((tokens, width), BF16), jax.ShapeDtypeStruct((8, width), F32)],
        [rows, whole((8, width))], (3,), [pltpu.VMEM((tokens, width), F32)] * 2,
    )
    if small:
        half = per // 2
        up_sum, up_send = next_round(
            scalars, [], [sums_one],
            [sum_of(up_parts[0], up_came, up_one, row=rows_, rows=half) for rows_ in ((0, half), (half, 0))],
        )
        up_z = swap_z(up_send, 1)
        qkv_parts = weight_grad(scalars, 0, [(attn_in, d_qkv, attn_in_core, d_qkv_core)], width, after=(up_sum,))
        qkv_parts[2], sums_one = next_round(scalars, [qkv_parts[2], sums_one], down_z)
        qkv_came = second_way(qkv_parts[2])
        time_cols = time_features.astype(F32).T
        depth = 64
        v_odd, v_even = call(
            partial(pack_grads_kernel, slots), scalars,
            [sums_one, sums_qkv, sums_two, up_bias_sum, down_bias_sum, time_cols],
            [whole((8, width)), whole((8, width)), whole((8, width)), whole((1, hidden)), line, whole(time_cols.shape)],
            [jax.ShapeDtypeStruct((4, depth, width), BF16)] * 2, [whole((4, depth, width))] * 2, (1,), cost=SOME_COST,
        )
        v_odd, v_even = v_odd.reshape(-1, width), v_even.reshape(-1, width)
        v_odd, up_z, down_sum = next_round(scalars, [v_odd, up_z, down_sum])
        down_grad = in_place(down_sum, down_z)
        up_sum = add(up_sum, up_z)
        up_z = swap_z(up_sum, 2)
        v_came = sibling(v_odd)
        v_came, *to_one = next_round(
            scalars, [v_came], [up_sum],
            [([(qkv_parts[1], row, 0), (qkv_came, per + row, 0)], half, qkv_columns) for row in (0, half)],
        )
        qkv_one = [first_way(x) for x in to_one]
        *qkv_one, v_came = next_round(scalars, [*qkv_one, v_came])
        low, high = [
            add(qkv_parts[0][row : row + half], qkv_came[row : row + half], x) for row, x in zip((0, half), qkv_one)
        ]
        qkv_sum, qkv_send = jnp.where(even_z, low, high), jnp.where(even_z, high, low)
        qkv_z = swap_z(qkv_send, 1)
        (up_z,) = next_round(scalars, [up_z], [qkv_send])
        up_sum = add(up_sum, up_z)
        up_z = swap_z(up_sum, 1)
        part = add(v_even, v_came).reshape(4, depth, width)
        parts = [part[k] for k in range(4)]
        v_came = [first_way(parts[1]), second_way(parts[2]), swap(parts[3], 6, 6)]
        qkv_sum, part = next_round(scalars, [], [], [sum_of(qkv_sum, qkv_z), sum_of(parts[0], *v_came)])
        qkv_z = swap_z(qkv_sum, 2)
        v_came = swap_z(part, 1)
        output = layer_output((part,))
        qkv_z, v_came = next_round(scalars, [qkv_z, v_came], [output, up_z])
        qkv_sum = add(qkv_sum, qkv_z)
        qkv_grad = joined(qkv_sum, swap_z(qkv_sum, 1))
        part = add(part, v_came)
        share = part.astype(F32) + swap_z(part, 2).astype(F32)
        up_out_grad = joined(up_sum, up_z)
        up_grad, out_grad = up_out_grad[:, :hidden], up_out_grad[:, hidden:]
        time_rows_here = time_weight.shape[0]
        time_grad = share[:time_rows_here]
        one, two, ff = width // BLOCKS, 2 * width // BLOCKS, hidden // BLOCKS
        row = share[time_rows_here]
        (gain_one_grad, shift_one_grad, out_bias_grad, gain_two_grad, shift_two_grad, down_bias_grad,
         value_bias_grad) = [row[i * one : (i + 1) * one] for i in range(7)]
        row = share[time_rows_here + 1]
        qk_bias_grad, up_bias_grad = row[:two], row[two : two + ff]
        time_bias_grad = share[time_rows_here + 2, :one]
    else:
        output = layer_output(())
        d_time = sums_one[2 : 2 + slots]
        time_grad = lax.dot_general(
            time_features.astype(F32), d_time, (((0,), (0,)), ((), ())), precision=lax.Precision.HIGHEST
        )
        vector_sums = (
            sums_one[0], sums_one[1], sums_qkv[:2].reshape(-1), sums_qkv[2], sums_two[2], sums_two[0], sums_two[1],
            up_bias_sum[0], down_bias_sum[0], jnp.sum(d_time, axis=0),
        )
        shares = jnp.concatenate(
            [time_grad.reshape(n_fsdp, -1)] + [v.reshape(n_fsdp, -1) for v in vector_sums], axis=1
        )
        sizes = [time_weight.size] + [v.size // n_fsdp for v in vector_sums]
        shares = jnp.pad(shares, ((0, 0), (0, -shares.shape[1] % 4096))).reshape(n_fsdp, -1, 128)
        shares = lax.psum_scatter(shares.astype(BF16), "fsdp", scatter_dimension=0, tiled=False)
        share = lax.psum(shares, "dp").astype(F32).reshape(-1)
        got = []
        at = 0
        for size in sizes:
            got.append(share[at : at + size])
            at += size
        (time_grad, gain_one_grad, shift_one_grad, qk_bias_grad, value_bias_grad, out_bias_grad, gain_two_grad,
         shift_two_grad, up_bias_grad, down_bias_grad, time_bias_grad) = got
    return (
        output, input_grad, gain_one_grad, shift_one_grad, qkv_grad, qk_bias_grad, value_bias_grad, out_grad, out_bias_grad,
        gain_two_grad, shift_two_grad, up_grad, up_bias_grad, down_grad, down_bias_grad,
        time_grad.reshape(time_weight.shape), time_bias_grad,
    )


def solution(mesh):
    tokens = P(("dp", "fsdp"), None)
    vector = P("fsdp")
    matrix = P("fsdp", None)
    in_specs = (
        tokens, tokens, tokens, vector, vector, matrix, vector, matrix, vector, vector, vector, matrix, vector, matrix,
        vector, matrix, vector, tokens,
    )
    out_specs = (
        tokens, tokens, vector, vector, matrix, vector, vector, matrix, vector, vector, vector, matrix, vector, matrix,
        vector, matrix, vector,
    )
    body = partial(per_device, mesh.shape["dp"], mesh.shape["fsdp"])
    return jax.shard_map(body, mesh=mesh, in_specs=in_specs, out_specs=out_specs, check_vma=False)
```

```python
from functools import partial

import jax
import jax.numpy as jnp
from jax import lax
from jax.experimental import pallas as pl
from jax.experimental.pallas import tpu as pltpu
from jax.sharding import PartitionSpec as P

H = 16
GROUP = 4
BLOCKS = 8
CHIPS = 4
CHIP_AT = BLOCKS
PARITY_AT = CHIP_AT + CHIPS
ENDS_AT = PARITY_AT + 1
FAR = -1e30
NO_COST = pl.CostEstimate(flops=0, bytes_accessed=0, transcendentals=0)
SOME_COST = pl.CostEstimate(flops=30 * 10**9, bytes_accessed=100 * 10**6, transcendentals=0)
F32 = jnp.float32
BF16 = jnp.bfloat16


def rows_by_cols(a, b):
    return lax.dot_general(a, b, (((1,), (0,)), ((), ())), preferred_element_type=F32)


def rows_by_rows(a, b):
    return lax.dot_general(a, b, (((1,), (1,)), ((), ())), preferred_element_type=F32)


def cols_by_cols(a, b):
    return lax.dot_general(a, b, (((0,), (0,)), ((), ())), preferred_element_type=F32)


def call(kernel, scalars, inputs, in_specs, out_shapes, out_specs, grid, scratch=(), aliases=None, after=(), cost=NO_COST):
    count = len(inputs)

    def body(s_ref, *refs):
        kernel(s_ref, *refs[:count], *refs[count + len(after) :])

    return pl.pallas_call(
        body,
        name=getattr(kernel, "func", kernel).__name__,
        grid_spec=pltpu.PrefetchScalarGridSpec(
            num_scalar_prefetch=1,
            grid=grid,
            in_specs=list(in_specs) + [pl.BlockSpec(memory_space=pl.ANY)] * len(after),
            out_specs=out_specs,
            scratch_shapes=list(scratch),
        ),
        out_shape=out_shapes,
        input_output_aliases=aliases or {},
        compiler_params=pltpu.CompilerParams(
            dimension_semantics=("arbitrary",) * len(grid), vmem_limit_bytes=64 * 2**20
        ),
        cost_estimate=cost,
    )(scalars, *inputs, *after)


def round_kernel(counts, s_ref, *refs):
    outs = refs[-len(counts) :] if counts else ()
    at = 0
    for count, out in zip(counts, outs):
        total = refs[at][...].astype(F32)
        for ref in refs[at + 1 : at + count]:
            total = total + ref[...].astype(F32)
        out[...] = total.astype(BF16)
        at += count


def next_round(scalars, passed, others=(), sums=()):
    anywhere = pl.BlockSpec(memory_space=pl.ANY)
    steps = 2
    specs, inputs, counts, shapes, out_specs = [], [], [], [], []
    for parts, rows, columns in sums:
        size = rows // steps
        for array, row, column in parts:
            even, odd = row if isinstance(row, tuple) else (row, row)

            def at(i, s, even=even // size, odd=odd // size, column=column // columns):
                return (i + even + s[PARITY_AT] * (odd - even), column)

            specs.append(pl.BlockSpec((size, columns), at))
            inputs.append(array)
        counts.append(len(parts))
        shapes.append(jax.ShapeDtypeStruct((rows, columns), BF16))
        out_specs.append(pl.BlockSpec((size, columns), lambda i, s: (i, 0)))
    first = len(inputs)

    def kernel(s_ref, *refs):
        given = first + len(passed) + len(others)
        round_kernel(counts, s_ref, *refs[:first], *refs[given + len(passed) :])

    out = pl.pallas_call(
        kernel,
        name="next_round",
        grid_spec=pltpu.PrefetchScalarGridSpec(
            num_scalar_prefetch=1,
            grid=(steps if sums else 1,),
            in_specs=specs + [anywhere] * (len(passed) + len(others)),
            out_specs=[anywhere] * len(passed) + out_specs,
        ),
        out_shape=[jax.ShapeDtypeStruct(x.shape, x.dtype) for x in passed] + shapes,
        input_output_aliases={1 + first + i: i for i in range(len(passed))},
        compiler_params=pltpu.CompilerParams(dimension_semantics=("arbitrary",), vmem_limit_bytes=64 * 2**20),
        cost_estimate=NO_COST,
    )(scalars, *inputs, *passed, *others)
    return list(out)


def copy_after(x, *others):
    def kernel(x_ref, *refs):
        refs[-1][...] = x_ref[...]

    block = pl.BlockSpec((x.shape[0] // 2, x.shape[1]), lambda i: (i, 0))
    return pl.pallas_call(
        kernel,
        grid=(2,),
        out_shape=jax.ShapeDtypeStruct(x.shape, x.dtype),
        in_specs=[block] + [pl.BlockSpec(memory_space=pl.ANY)] * len(others),
        out_specs=block,
        cost_estimate=NO_COST,
    )(x, *others)


def whole(shape):
    zeros = (0,) * len(shape)
    return pl.BlockSpec(shape, lambda *_: zeros)


def normalize(x):
    center = x - jnp.mean(x, axis=-1, keepdims=True)
    variance = jnp.mean(center * center, axis=-1, keepdims=True)
    inverse = lax.rsqrt(variance + 1e-05)
    return center * inverse, inverse


def normalize_back(grad, normal, inverse, gain):
    scaled = grad * gain
    return inverse * (
        scaled
        - jnp.mean(scaled, axis=-1, keepdims=True)
        - normal * jnp.mean(scaled * normal, axis=-1, keepdims=True)
    )


def row_ids(count, first=0):
    return lax.broadcasted_iota(jnp.int32, (count, 1), 0) + first


def members_of(s_ref, ids, slots):
    out = []
    start = 0
    for slot in range(slots):
        end = s_ref[ENDS_AT + slot]
        out.append((ids >= start) & (ids < end))
        start = end
    return out


def segment_of(s_ref, ids, slots):
    segment = jnp.zeros(ids.shape, jnp.int32)
    for slot in range(slots):
        segment = segment + (ids >= s_ref[ENDS_AT + slot]).astype(jnp.int32)
    return segment


def resid_zero_of(s_ref, act, time_rows, first, slots):
    x = act.astype(F32)
    for slot, inside in enumerate(members_of(s_ref, row_ids(act.shape[0], first), slots)):
        x = x + jnp.where(inside, time_rows[slot : slot + 1, :], 0.0)
    return x


def piece_specs(rows, columns, at):
    return [pl.BlockSpec((rows, columns), lambda *a: (0, at(*a)))] * BLOCKS


def rows_of(refs, at=slice(None)):
    return jnp.concatenate([ref[:, at] for ref in refs], axis=0)


def pack_kernel(s_ref, qkv_ref, out_ref, time_ref, *refs):
    vectors, pack_ref = refs[:-1], refs[-1]
    rows, columns = qkv_ref.shape
    pack_ref[0:rows, 0:columns] = qkv_ref[...]
    pack_ref[0:rows, columns:] = out_ref[...]
    depth = pack_ref.shape[0] - rows
    width = out_ref.shape[1]
    pack_ref[rows:, 0:width] = time_ref[0:depth, :]
    pack_ref[rows:, width : 2 * width] = time_ref[depth:, :]
    line = jnp.concatenate([v[...].astype(F32).reshape(1, -1) for v in vectors], axis=1)
    line = jnp.concatenate([line, jnp.zeros((1, pack_ref.shape[1] - 2 * width - line.shape[1]), F32)], axis=1)
    lines = jnp.where(row_ids(depth) == 0, line, 0.0).astype(BF16)
    pack_ref[rows:, 2 * width :] = lines


def norm_one_kernel(slots, s_ref, act_ref, feat_ref, *refs):
    extras = refs[:BLOCKS]
    out_ref, time_ref, lines_ref, qkv_b_ref, up_b_ref = refs[BLOCKS:]
    depth = extras[0].shape[0]
    width = act_ref.shape[1]
    small = width // BLOCKS
    time_rows = jnp.zeros((slots, width), F32)
    for j in range(BLOCKS):
        block = s_ref[j]
        for half in range(2):
            at = pl.multiple_of((block * 2 + half) * 128, 128)
            part = feat_ref[:, pl.ds(at, 128)]
            time_rows = time_rows + rows_by_cols(part[:, 0:depth], extras[j][:, half * width : (half + 1) * width])
        line = extras[j][:, 2 * width :].astype(F32)[0:1]
        at = pl.ds(pl.multiple_of(block * small, 128), small)
        for v in range(7):
            lines_ref[v : v + 1, at] = line[:, v * small : (v + 1) * small]
        first = 7 * small
        for ref in (qkv_b_ref, up_b_ref):
            size = ref.shape[1] // BLOCKS
            ref[0:1, pl.ds(pl.multiple_of(block * size, 128), size)] = line[:, first : first + size]
            first += size
    lines_ref[7:8, :] = jnp.zeros((1, width), F32)
    time_rows = time_rows + lines_ref[6:7, :]
    time_ref[...] = time_rows
    x = resid_zero_of(s_ref, act_ref[...], time_rows, 0, slots)
    normal, _ = normalize(x)
    out_ref[...] = (normal * lines_ref[0:1, :] + lines_ref[1:2, :]).astype(BF16)


def by_block(s_ref, x_ref, out_ref, back=False):
    width = x_ref.shape[1] // BLOCKS
    for j in range(BLOCKS):
        at = pl.ds(pl.multiple_of(s_ref[j] * width, 128), width)
        if back:
            out_ref[:, at] = x_ref[:, j * width : (j + 1) * width]
        else:
            out_ref[:, j * width : (j + 1) * width] = x_ref[:, at]


def turn(x, cosine, sine):
    lanes = lax.broadcasted_iota(jnp.int32, x.shape, 1)
    width = x.shape[1]
    swapped = jnp.where(lanes % 64 < 32, pltpu.roll(x, width - 32, 1), pltpu.roll(x, 32, 1))
    return x * cosine + swapped * sine


def lane_ids(width):
    return lax.broadcasted_iota(jnp.int32, (1, width), 1)


def head_lanes(h, width):
    lanes = lane_ids(width)
    return (lanes >= h * 64) & (lanes < (h + 1) * 64)


def spare_head(h):
    return 1 if h == 0 else 0


def mask_lanes(s_ref, tokens, width, slots, query_ref, key_ref):
    segment = segment_of(s_ref, row_ids(tokens), slots)
    for p in range(2):
        at = lane_ids(width) - 64 * p
        inside = (at >= 0) & (at <= slots)
        more = (at > slots) & (at <= slots + 3)
        query_ref[p] = jnp.where(inside & (at != segment), FAR, 0.0).astype(BF16)
        key_ref[p] = jnp.where((inside & (at == segment)) | more, 1.0, 0.0).astype(BF16)


def attention_kernel(slots, s_ref, x_ref, bq_ref, bk_ref, bv_ref, cos_ref, sin_ref, *refs):
    wq, wk, wv = refs[:BLOCKS], refs[BLOCKS : 2 * BLOCKS], refs[2 * BLOCKS : 3 * BLOCKS]
    q_ref, k_ref, v_ref, att_ref, lse_ref, rel_ref, qm_ref, km_ref = refs[3 * BLOCKS :]
    tokens, width = q_ref.shape

    @pl.when(pl.program_id(0) == 0)
    def _():
        by_block(s_ref, x_ref, rel_ref)
        mask_lanes(s_ref, tokens, width, slots, qm_ref, km_ref)

    x = rel_ref[...]
    cosine, sine = cos_ref[...], sin_ref[...]
    q = turn(rows_by_cols(x, rows_of(wq)) + bq_ref[...], cosine, sine).astype(BF16)
    k = turn(rows_by_cols(x, rows_of(wk)) + bk_ref[...], cosine, sine).astype(BF16)
    v = (rows_by_cols(x, rows_of(wv)) + bv_ref[...]).astype(BF16)
    q = q * jnp.asarray(0.125, BF16)
    q_ref[...] = q
    k_ref[...] = k
    v_ref[...] = v
    masked_keys = [jnp.where(head_lanes(p, width), km_ref[p], k) for p in range(2)]
    total = jnp.zeros((tokens, width), F32)
    lse = jnp.zeros((tokens, 128), F32)
    for h in range(GROUP):
        p = spare_head(h)
        mine = head_lanes(h, width)
        scores = rows_by_rows(jnp.where(mine, q, qm_ref[p]), masked_keys[p])
        top = jnp.max(scores, axis=1, keepdims=True)
        e = jnp.exp(scores - top)
        denominator = jnp.sum(e, axis=1, keepdims=True)
        part = rows_by_cols(e.astype(BF16), v) * (1.0 / denominator)
        total = jnp.where(mine, part, total)
        lse = jnp.where(lane_ids(128) == h, top + jnp.log(denominator), lse)
    att_ref[...] = total.astype(BF16)
    lse_ref[0] = lse


def out_kernel(slots, s_ref, att_ref, act_ref, time_ref, bias_ref, gain_ref, shift_ref, *refs):
    w, (res_ref, mlp_ref, rel_ref) = refs[:BLOCKS], refs[BLOCKS:]
    by_block(s_ref, att_ref, rel_ref)
    x = resid_zero_of(s_ref, act_ref[...], time_ref[...], 0, slots)
    x = x + rows_by_cols(rel_ref[...], rows_of(w)) + bias_ref[...]
    res_ref[...] = x
    normal, _ = normalize(x)
    mlp_ref[...] = (normal * gain_ref[...] + shift_ref[...]).astype(BF16)


def up_kernel(s_ref, x_ref, bias_ref, *refs):
    w, (act_ref, slope_ref, rel_ref) = refs[:BLOCKS], refs[BLOCKS:]

    @pl.when(pl.program_id(0) == 0)
    def _():
        by_block(s_ref, x_ref, rel_ref)

    pre = rows_by_cols(rel_ref[...], rows_of(w)) + bias_ref[...]
    cdf = 0.5 + 0.5 * lax.erf(pre * 0.7071067811865476)
    density = 0.3989422804014327 * jnp.exp(-0.5 * pre * pre)
    act_ref[...] = (pre * cdf).astype(BF16)
    slope_ref[...] = (cdf + pre * density).astype(BF16)


def down_copies(refs, held_ref, sems):
    return [(n // 2, pltpu.make_async_copy(ref, held_ref.at[n], sems.at[n])) for n, ref in enumerate(refs)]


def fetch_down(step, copies):
    @pl.when(step == 0)
    def _():
        for _, copy in copies:
            copy.start()

    for chip in range(CHIPS):

        @pl.when(step == chip)
        def _():
            for owner, copy in copies:
                if owner == chip:
                    copy.wait()


def halves_of(s_ref, width):
    core = s_ref[0] % 2
    return [pl.ds(pl.multiple_of(at * width, 128), width) for at in (core, 1 - core)]


def down_kernel(slots, s_ref, a_ref, res_ref, bias_ref, *refs):
    w, (out_ref, acc_ref, held_ref, sems) = refs[:BLOCKS], refs[BLOCKS:]
    c = pl.program_id(0)
    fetch_down(c, down_copies(w, held_ref, sems))

    @pl.when(c == 0)
    def _():
        acc_ref[...] = res_ref[...] + bias_ref[...]

    for n, at in enumerate(halves_of(s_ref, held_ref.shape[1])):
        acc_ref[...] += rows_by_cols(a_ref[:, at], held_ref[2 * c + n])

    @pl.when(c == pl.num_programs(0) - 1)
    def _():
        valid = row_ids(out_ref.shape[0]) < s_ref[ENDS_AT + slots - 1]
        out_ref[...] = jnp.where(valid, acc_ref[...], 0.0).astype(BF16)


def branch_kernel(slots, s_ref, cot_ref, branch_ref, bias_ref):
    valid = row_ids(cot_ref.shape[0]) < s_ref[ENDS_AT + slots - 1]
    branch = jnp.where(valid, cot_ref[...].astype(F32), 0.0)
    branch_ref[...] = branch.astype(BF16)
    bias_ref[...] = jnp.sum(branch, axis=0, keepdims=True)


def mlp_back_kernel(s_ref, branch_ref, slope_ref, res_ref, gain_ref, *refs):
    down, up = refs[:BLOCKS], refs[BLOCKS : 2 * BLOCKS]
    pre_ref, bias_ref, dres_ref, datt_ref, sums_ref, acc_ref, grad_ref, held_ref, sems = refs[2 * BLOCKS :]
    c = pl.program_id(0)
    fetch_down(c, down_copies(down, held_ref, sems))

    @pl.when(c == 0)
    def _():
        acc_ref[...] = jnp.zeros_like(acc_ref)

    branch = branch_ref[...]
    for n, at in enumerate(halves_of(s_ref, held_ref.shape[1])):
        d_pre = (rows_by_rows(branch, held_ref[2 * c + n]) * slope_ref[:, at].astype(F32)).astype(BF16)
        pre_ref[:, at] = d_pre
        bias_ref[:, at] = jnp.sum(d_pre.astype(F32), axis=0, keepdims=True)
        acc_ref[...] += rows_by_rows(d_pre, rows_of(up, at))

    @pl.when(c == pl.num_programs(0) - 1)
    def _():
        by_block(s_ref, acc_ref, grad_ref, back=True)
        grad = grad_ref[...]
        normal, inverse = normalize(res_ref[...])
        d_res = branch.astype(F32) + normalize_back(grad, normal, inverse, gain_ref[...])
        dres_ref[...] = d_res
        d_att = d_res.astype(BF16)
        datt_ref[...] = d_att
        sums_ref[0:1, :] = jnp.sum(grad * normal, axis=0, keepdims=True)
        sums_ref[1:2, :] = jnp.sum(grad, axis=0, keepdims=True)
        sums_ref[2:3, :] = jnp.sum(d_att.astype(F32), axis=0, keepdims=True)
        sums_ref[3:8, :] = jnp.zeros((5, sums_ref.shape[1]), F32)


def three_lanes(x, p, slots):
    first = x.astype(BF16)
    rest = x - first.astype(F32)
    second = rest.astype(BF16)
    third = (rest - second.astype(F32)).astype(BF16)
    at = lane_ids(64 * GROUP) - 64 * p - slots - 1
    spread = jnp.where(at == 0, first, jnp.where(at == 1, second, third))
    return jnp.where((at >= 0) & (at < 3), spread, jnp.zeros((), BF16))


def attention_back_kernel(slots, s_ref, d_ref, q_ref, k_ref, v_ref, lse_ref, cos_ref, sin_ref, *refs):
    w, (out_ref, sums_ref, qm_ref, km_ref, dq_ref, dk_ref, dv_ref, heads_ref) = refs[:BLOCKS], refs[BLOCKS:]
    tokens, width = q_ref.shape
    step = pl.program_id(0)

    @pl.when(pl.program_id(0) == 0)
    def _():
        mask_lanes(s_ref, tokens, width, slots, qm_ref, km_ref)

    for chip, pieces in enumerate((w[0:2], w[2:4], w[4:6], w[6:8])):

        @pl.when(step == chip)
        def _():
            both = rows_by_rows(d_ref[...], rows_of(pieces)).astype(BF16)
            for n, at in enumerate(halves_of(s_ref, width // 2)):
                heads_ref[:, at] = both[:, n * (width // 2) : (n + 1) * (width // 2)]

    d_heads = heads_ref[...]
    q, k, v = q_ref[...], k_ref[...], v_ref[...]
    for h in range(GROUP):
        p = spare_head(h)
        mine, spare = head_lanes(h, width), head_lanes(p, width)
        queries = jnp.where(spare, qm_ref[p] + three_lanes(-lse_ref[0, :, h : h + 1], p, slots), q)
        soft = jnp.exp(rows_by_rows(jnp.where(mine, k, km_ref[p]), queries))
        product = soft * rows_by_rows(jnp.where(mine, v, jnp.zeros((), BF16)), d_heads)
        row_terms = jnp.sum(product, axis=0, keepdims=True)
        d_scores = (product - soft * row_terms).astype(BF16)
        d_v = rows_by_cols(soft.astype(BF16), d_heads)
        d_k = rows_by_cols(d_scores, q)
        d_q = cols_by_cols(d_scores, k)
        if h == 0:
            dq_ref[...], dk_ref[...], dv_ref[...] = d_q, d_k, d_v
        else:
            dq_ref[...] = jnp.where(mine, d_q, dq_ref[...])
            dk_ref[...] = jnp.where(mine, d_k, dk_ref[...])
            dv_ref[...] = jnp.where(mine, d_v, dv_ref[...])
    cosine, sine = cos_ref[...], sin_ref[...]
    sums_ref[...] = jnp.zeros_like(sums_ref)
    parts = (turn(dq_ref[...] * 0.125, cosine, -sine), turn(dk_ref[...], cosine, -sine), dv_ref[...])
    for i, part in enumerate(parts):
        part = part.astype(BF16)
        out_ref[i] = part
        sums_ref[i : i + 1, :] = jnp.sum(part.astype(F32), axis=0, keepdims=True)


def d_input_kernel(slots, s_ref, d_ref, act_ref, time_ref, gain_ref, dres_ref, *refs):
    w, (out_ref, sums_ref, acc_ref, grad_ref, act_held, dres_held, sems) = refs[:BLOCKS], refs[BLOCKS:]
    late = [pltpu.make_async_copy(act_ref, act_held, sems.at[0]), pltpu.make_async_copy(dres_ref, dres_held, sems.at[1])]
    j = pl.program_id(0)

    @pl.when(j == 0)
    def _():
        for copy in late:
            copy.start()
        acc_ref[...] = rows_by_rows(d_ref[0], rows_of(w))

    @pl.when(j > 0)
    def _():
        acc_ref[...] += rows_by_rows(d_ref[0], rows_of(w))

    @pl.when(j == pl.num_programs(0) - 1)
    def _():
        for copy in late:
            copy.wait()
        by_block(s_ref, acc_ref, grad_ref, back=True)
        grad = grad_ref[...]
        normal, inverse = normalize(resid_zero_of(s_ref, act_held[...], time_ref[...], 0, slots))
        d_in = dres_held[...] + normalize_back(grad, normal, inverse, gain_ref[...])
        out_ref[...] = d_in.astype(BF16)
        sums_ref[...] = jnp.zeros_like(sums_ref)
        sums_ref[0:1, :] = jnp.sum(grad * normal, axis=0, keepdims=True)
        sums_ref[1:2, :] = jnp.sum(grad, axis=0, keepdims=True)
        for slot, inside in enumerate(members_of(s_ref, row_ids(act_held.shape[0]), slots)):
            sums_ref[2 + slot : 3 + slot, :] = jnp.sum(jnp.where(inside, d_in, 0.0), axis=0, keepdims=True)


def grad_kernel(steps, sources, groups, s_ref, *refs):
    per = 5 * sources
    outs = refs[per * len(steps) :]
    i = pl.program_id(0)
    first = 0
    for n, (count, lead) in enumerate(steps):
        mine = refs[per * n : per * (n + 1)]

        @pl.when((i >= first) & (i < first + count))
        def _():
            product = None
            for source in range(sources):
                *a_refs, b_ref = mine[5 * source : 5 * source + 5]
                a = jnp.concatenate([ref[...] for ref in a_refs], axis=1)
                part = cols_by_cols(a, b_ref[0] if lead else b_ref[...])
                product = part if product is None else product + part
            rows = product.shape[0] // 4
            for out, group in zip(outs, groups):
                out[...] = product[group[0] * rows : (group[-1] + 1) * rows].astype(BF16)

        first += count


def weight_grad(scalars, odd, pairs, tile, after=(), groups=((0,), (1,), (2, 3))):
    tokens, width = pairs[0][0].shape[0], pairs[0][0].shape[1] // BLOCKS
    sources = len(pairs[0]) // 2
    specs, inputs, steps = [], [], []
    first = 0
    for pair in pairs:
        lead = pair[1].ndim == 3
        per = pair[1].shape[-1] // tile
        count = per * (pair[1].shape[0] if lead else 1)

        def local(i, first=first, count=count):
            return jnp.clip(i - first, 0, count - 1)

        for a, b in zip(pair[::2], pair[1::2]):
            for j in range(4):
                specs.append(pl.BlockSpec((tokens, width), lambda i, s, j=j: (0, s[2 * j + odd])))
                inputs.append(a)
            if lead:
                specs.append(
                    pl.BlockSpec((1, tokens, tile), lambda i, s, at=local, per=per: (at(i) // per, 0, at(i) % per))
                )
            else:
                specs.append(pl.BlockSpec((tokens, tile), lambda i, s, at=local: (0, at(i))))
            inputs.append(b)
        steps.append((count, lead))
        first += count
    sizes = [len(group) * width for group in groups]
    out = call(
        partial(grad_kernel, tuple(steps), sources, groups), scalars, inputs, specs,
        [jax.ShapeDtypeStruct((rows, first * tile), BF16) for rows in sizes],
        [pl.BlockSpec((rows, tile), lambda i, s: (0, i)) for rows in sizes], (first,), after=after,
    )
    return list(out)


def pack_grads_kernel(slots, s_ref, one_ref, qkv_ref, two_ref, up_ref, down_ref, time_ref, odd_ref, even_ref):
    rows = time_ref.shape[0] // BLOCKS
    d_time = one_ref[2 : 2 + slots, :]
    one, two = d_time.shape[1] // BLOCKS, 2 * d_time.shape[1] // BLOCKS
    ff = up_ref.shape[1] // BLOCKS
    odd_ref[...] = jnp.zeros_like(odd_ref)
    even_ref[...] = jnp.zeros_like(even_ref)
    for j in range(BLOCKS):
        block = s_ref[j]
        out, chip = (odd_ref, (0, 2, 1, 3)[j // 2]) if j % 2 else (even_ref, j // 2)
        features = time_ref[pl.ds(pl.multiple_of(block * rows, 8), rows), :]
        out[chip, 0:rows, :] = sum(features[:, s : s + 1] * d_time[s : s + 1, :] for s in range(slots)).astype(BF16)
        at = pl.ds(pl.multiple_of(block * one, 128), one)
        sources = (one_ref[0:1, at], one_ref[1:2, at], two_ref[2:3, at], two_ref[0:1, at], two_ref[1:2, at],
                   down_ref[0:1, at], qkv_ref[2:3, at])
        line = jnp.concatenate(sources, axis=1)
        out[chip, rows : rows + 1, 0 : line.shape[1]] = line.astype(BF16)
        wide = pl.ds(pl.multiple_of((block % 4) * two, 128), two)
        pair = jnp.where(block < 4, qkv_ref[0:1, wide], qkv_ref[1:2, wide])
        hidden = up_ref[0:1, pl.ds(pl.multiple_of(block * ff, 128), ff)]
        out[chip, rows + 1 : rows + 2, 0 : two + ff] = jnp.concatenate([pair, hidden], axis=1).astype(BF16)
        bias = jnp.sum(one_ref[2 : 2 + slots, at], axis=0, keepdims=True)
        out[chip, rows + 2 : rows + 3, 0:one] = bias.astype(BF16)


def per_device(
    n_dp, n_fsdp, activations, time_features, lengths, attn_gain, attn_shift, qkv_weight, qkv_bias, out_weight, out_bias,
    mlp_gain, mlp_shift, up_weight, up_bias, down_weight, down_bias, time_weight, time_bias, cotangent,
):
    tokens, width = activations.shape
    slots = lengths.shape[1]
    hidden = down_weight.shape[0] * n_fsdp
    small = n_fsdp == BLOCKS
    me = lax.axis_index("fsdp")
    blocks = jnp.arange(BLOCKS, dtype=jnp.int32)
    chips = jnp.arange(CHIPS, dtype=jnp.int32)
    if small:
        turned = jnp.where(chips % 3 > 0, 3 - chips, chips)
        chips = jnp.where(me % 2 == 0, turned, chips)
        blocks = (2 * chips[:, None] + jnp.arange(2, dtype=jnp.int32)[None, :]).reshape(-1) ^ me
        chips = chips ^ (me // 2)
    upto = jnp.arange(slots)[:, None] >= jnp.arange(slots)[None, :]
    ends = jnp.sum(jnp.where(upto, lengths, 0), axis=1)
    parity = lax.axis_index("dp") % 2
    scalars = jnp.concatenate([blocks, chips, parity[None], ends]).astype(jnp.int32)

    def swap(x, even, odd):
        return lax.ppermute(x, "fsdp", [(i, i ^ (odd if i % 2 else even)) for i in range(n_fsdp)])

    def sibling(x):
        return swap(x, 1, 1)

    def first_way(x):
        return swap(x, 4, 2)

    def second_way(x):
        return swap(x, 2, 4)

    def pieces(own, first, second, far, own_sibling, first_sibling, second_sibling, far_sibling):
        return [own, own_sibling, first, second_sibling, second, first_sibling, far, far_sibling]

    def add(*parts):
        total = parts[0].astype(F32)
        for part in parts[1:]:
            total = total + part.astype(F32)
        return total.astype(BF16)

    def gather_rows(w):
        return lax.all_gather(w, "fsdp", axis=0, tiled=True).reshape(BLOCKS, -1, w.shape[1])

    rows = whole((tokens, width))
    line = whole((1, width))
    anywhere = pl.BlockSpec(memory_space=pl.ANY)
    vectors = [attn_gain, attn_shift, out_bias, mlp_gain, mlp_shift, down_bias, time_bias, qkv_bias, up_bias]
    per = width // BLOCKS
    qkv_columns = qkv_weight.shape[1]
    columns = qkv_columns + width
    depth = 16
    if small:
        sources = [qkv_weight, out_weight, time_weight] + vectors
        pack = call(
            pack_kernel, scalars, sources, [whole(x.shape) for x in sources],
            jax.ShapeDtypeStruct((per + depth, columns), BF16), whole((per + depth, columns)), (1,),
        )
        first_one, first_two, first_core = first_way(pack), second_way(pack), sibling(pack)
        up_own, down_own = copy_after(up_weight, pack), copy_after(down_weight, pack)
    else:
        gathered = [lax.all_gather(v, "fsdp", axis=0, tiled=True).reshape(BLOCKS, -1) for v in vectors]
        matrices = jnp.concatenate([gather_rows(qkv_weight), gather_rows(out_weight)], axis=2)
        times = lax.all_gather(time_weight, "fsdp", axis=0, tiled=True).reshape(BLOCKS, 2, depth, width)
        lines = jnp.concatenate(gathered, axis=1)
        lines = jnp.pad(lines, ((0, 0), (0, columns - 2 * width - lines.shape[1])))[:, None]
        lines = jnp.pad(lines, ((0, 0), (0, depth - 1), (0, 0)))
        extra = jnp.concatenate([times[:, 0], times[:, 1], lines], axis=2)
        first = list(jnp.concatenate([matrices, extra], axis=1))
        up_rel = list(gather_rows(up_weight))
        down_rel = list(gather_rows(down_weight))

    ids = jnp.arange(tokens, dtype=jnp.int32)[:, None]
    starts = ends - lengths[0]
    inside = (ids >= starts[None, :]) & (ids < ends[None, :])
    position = (ids[:, 0] - jnp.sum(jnp.where(inside, starts[None, :], 0), axis=1)).astype(F32)
    frequency = 10000.0 ** (-2.0 * jnp.arange(32, dtype=F32) / 64)
    angles = position[:, None] * frequency[None, :]
    cosine, sine = jnp.cos(angles), jnp.sin(angles)
    lanes = 64 * GROUP
    cos_table = jnp.tile(cosine, (1, 2 * GROUP))
    sin_table = jnp.tile(jnp.concatenate([-sine, sine], axis=1), (1, GROUP))

    d_branch, down_bias_sum = call(
        partial(branch_kernel, slots), scalars, [cotangent], [rows],
        [jax.ShapeDtypeStruct((tokens, width), BF16), jax.ShapeDtypeStruct((1, width), F32)], [rows, line], (1,),
    )
    if small:
        first_one, first_two = next_round(
            scalars, [first_one, first_two], [first_core, d_branch, up_own, down_own, cos_table, sin_table]
        )
        first_far = second_way(first_one)
        core_one, core_two, branch_core = sibling(first_one), sibling(first_two), sibling(d_branch)
        first_far, up_own = next_round(scalars, [first_far, up_own], [core_one, core_two, branch_core])
        up_one, up_two = first_way(up_own), second_way(up_own)
        first = pieces(pack, first_one, first_two, first_far, first_core, core_one, core_two, sibling(first_far))
    spread = time_features.reshape(slots, 2 * BLOCKS, -1)
    spread = jnp.pad(spread, ((0, 0), (0, 0), (0, 128 - spread.shape[2]))).reshape(slots, -1)
    extra_specs = [pl.BlockSpec((depth, columns), lambda i, s: (per // depth, 0))] * BLOCKS
    attn_in, time_rows, lines, qkv_b, up_b = call(
        partial(norm_one_kernel, slots), scalars, [activations, spread] + first,
        [rows, whole(spread.shape)] + extra_specs,
        [jax.ShapeDtypeStruct((tokens, width), BF16), jax.ShapeDtypeStruct((slots, width), F32),
         jax.ShapeDtypeStruct((8, width), F32), jax.ShapeDtypeStruct((1, qkv_columns), F32),
         jax.ShapeDtypeStruct((1, hidden), F32)],
        [rows, whole((slots, width)), whole((8, width)), whole((1, qkv_columns)), whole((1, hidden))], (1,),
        after=(d_branch,),
    )
    gain_one, shift_one, out_b, gain_two, shift_two, down_b = [lines[i : i + 1] for i in range(6)]
    groups = H // GROUP
    col = pl.BlockSpec((tokens, lanes), lambda g, s: (0, g))
    table = whole((tokens, lanes))
    mask_rooms = [pltpu.VMEM((2, tokens, lanes), BF16)] * 2
    qkv_specs = []
    for o in range(3):
        qkv_specs += piece_specs(per, lanes, lambda g, s, o=o: o * groups + g)
    queries, keys, values, attended, lse = call(
        partial(attention_kernel, slots), scalars,
        [attn_in, qkv_b, qkv_b, qkv_b, cos_table, sin_table] + first * 3,
        [rows] + [pl.BlockSpec((1, lanes), lambda g, s, o=o: (0, o * groups + g)) for o in range(3)]
        + [table, table] + qkv_specs,
        [jax.ShapeDtypeStruct((tokens, width), BF16)] * 4 + [jax.ShapeDtypeStruct((groups, tokens, 128), F32)],
        [col, col, col, col, pl.BlockSpec((1, tokens, 128), lambda g, s: (g, 0, 0))],
        (groups,), [pltpu.VMEM((tokens, width), BF16)] + mask_rooms)
    if small:
        up_one, up_two, up_own = next_round(scalars, [up_one, up_two, up_own], [attended])
        up_far = second_way(up_one)
        up_core, core_one, core_two = sibling(up_own), sibling(up_one), sibling(up_two)
        attended_core = sibling(attended)
        wait = (up_one,)
    else:
        wait = ()
    out_specs = piece_specs(per, width, lambda *a: qkv_columns // width)
    resid_one, mlp_in = call(
        partial(out_kernel, slots), scalars,
        [attended, activations, time_rows, out_b, gain_two, shift_two] + first,
        [rows, rows, whole((slots, width)), line, line, line] + out_specs,
        [jax.ShapeDtypeStruct((tokens, width), F32), jax.ShapeDtypeStruct((tokens, width), BF16)],
        [rows, rows], (1,), [pltpu.VMEM((tokens, width), BF16)], after=wait,
    )
    if small:
        up_far, down_own = next_round(scalars, [up_far, down_own], [core_one, core_two, up_core, mlp_in, attended_core])
        up_rel = pieces(up_own, up_one, up_two, up_far, up_core, core_one, core_two, sibling(up_far))
        down_one, down_two, down_core = first_way(down_own), second_way(down_own), sibling(down_own)
        attn_in_core = sibling(attn_in)
    tile = hidden // CHIPS
    wide = pl.BlockSpec((tokens, tile), lambda i, s: (0, i))
    activated, slope = call(
        up_kernel, scalars, [mlp_in, up_b] + up_rel,
        [rows, pl.BlockSpec((1, tile), lambda i, s: (0, i))] + piece_specs(per, tile, lambda i, s: i),
        [jax.ShapeDtypeStruct((tokens, hidden), BF16)] * 2, [wide, wide], (CHIPS,),
        [pltpu.VMEM((tokens, width), BF16)])

    even_z = parity == 0

    def swap_z(x, bit):
        return lax.ppermute(x, "dp", [(i, i ^ bit) for i in range(n_dp)])

    def sum_of(*arrays, row=0, column=0, rows=None, columns=None):
        shape = arrays[0].shape
        return [(x, row, column) for x in arrays], rows or shape[0], columns or shape[1]

    def halves(*parts):
        half = parts[0].shape[0] // 2
        low, high = add(*[x[:half] for x in parts]), add(*[x[half:] for x in parts])
        return jnp.where(even_z, low, high), jnp.where(even_z, high, low)

    def quarters(*parts):
        size = parts[0].shape[0] // 4
        place = lax.axis_index("dp")
        cuts = [[lax.dynamic_slice_in_dim(x, (place ^ bits) * size, size) for x in parts] for bits in range(4)]
        return [add(*cut) for cut in cuts]

    def exchange(parts):
        return [swap_z(x, bits) for x, bits in zip(parts, (1, 2, 3))]

    def sum_four(own, came):
        one, two, three = [x.astype(F32) for x in came]
        return ((own.astype(F32) + one) + (two + three)).astype(BF16)

    def in_place(own, came):
        four = jnp.stack([own, *came]).reshape(2, 2, *own.shape)
        place = lax.axis_index("dp")
        for axis, bit in ((0, 2), (1, 1)):
            four = jnp.where((place & bit) > 0, jnp.flip(four, axis), four)
        return four.reshape(-1, own.shape[1]).astype(F32)

    def joined(own, other):
        return jnp.where(even_z, jnp.concatenate([own, other]), jnp.concatenate([other, own])).astype(F32)

    def rows_of_all(pairs, tile):
        blocks = [weight_grad(scalars, odd, pairs, tile) for odd in range(2)]
        blocks = [jnp.concatenate(x).reshape(CHIPS, -1, x[0].shape[1]) for x in blocks]
        both = jnp.stack(blocks, axis=1).reshape(-1, blocks[0].shape[2])
        return lax.psum(lax.psum_scatter(both, "fsdp", scatter_dimension=0, tiled=True), "dp").astype(F32)

    if small:
        down_one, down_two, activated = next_round(scalars, [down_one, down_two, activated], [down_core, attn_in_core])
        down_far = second_way(down_one)
        core_one, core_two, activated_core = sibling(down_one), sibling(down_two), sibling(activated)
        down_parts = weight_grad(scalars, 0, [(activated, d_branch, activated_core, branch_core)], 512)
        down_far, down_parts[2] = next_round(scalars, [down_far, down_parts[2]], [core_one, core_two])
        down_came = second_way(down_parts[2])
        down_rel = pieces(down_own, down_one, down_two, down_far, down_core, core_one, core_two, sibling(down_far))
        mlp_in_core = sibling(mlp_in)
    else:
        down_grad = rows_of_all([(activated, d_branch)], 512)

    chip_wide = pl.BlockSpec((tokens, tile), lambda i, s: (0, s[CHIP_AT + i]))
    down_rooms = [pltpu.VMEM((BLOCKS, hidden // BLOCKS, width), BF16), pltpu.SemaphoreType.DMA((BLOCKS,))]
    d_pre, up_bias_sum, d_resid_one, d_attn, sums_two = call(
        mlp_back_kernel, scalars, [d_branch, slope, resid_one, gain_two] + down_rel + up_rel,
        [rows, chip_wide, rows, line] + [pl.BlockSpec(memory_space=pl.ANY)] * BLOCKS
        + piece_specs(per, tile, lambda i, s: s[CHIP_AT + i]),
        [jax.ShapeDtypeStruct((tokens, hidden), BF16),
         jax.ShapeDtypeStruct((1, hidden), F32), jax.ShapeDtypeStruct((tokens, width), F32),
         jax.ShapeDtypeStruct((tokens, width), BF16), jax.ShapeDtypeStruct((8, width), F32)],
        [chip_wide, pl.BlockSpec((1, tile), lambda i, s: (0, s[CHIP_AT + i])), rows, rows, whole((8, width))],
        (CHIPS,), [pltpu.VMEM((tokens, width), F32)] * 2 + down_rooms,
    )
    def layer_output(after):
        return call(
            partial(down_kernel, slots), scalars, [activated, resid_one, down_b] + down_rel,
            [chip_wide, rows, line] + [pl.BlockSpec(memory_space=pl.ANY)] * BLOCKS,
            jax.ShapeDtypeStruct((tokens, width), BF16), rows, (CHIPS,), [pltpu.VMEM((tokens, width), F32)] + down_rooms,
            after=after,
        )

    if small:
        d_pre, d_attn, down_came = next_round(scalars, [d_pre, d_attn, down_came], [mlp_in_core])
        d_pre_core, d_attn_core = sibling(d_pre), sibling(d_attn)
        far = down_came.shape[0] // 2
        down_one = first_way(add(down_parts[1], down_came[far:]))
        up_parts = weight_grad(
            scalars, 0, [(mlp_in, d_pre, mlp_in_core, d_pre_core), (attended, d_attn, attended_core, d_attn_core)], width
        )
        up_parts[2], down_came, down_one = next_round(scalars, [up_parts[2], down_came, down_one])
        up_came = second_way(up_parts[2])
        down_sum, *down_send = quarters(down_parts[0], down_came, down_one)
        down_z = exchange(down_send)
        wait = (down_came,)
    else:
        up_out_grad = rows_of_all([(mlp_in, d_pre), (attended, d_attn)], width)
        up_grad, out_grad = up_out_grad[:, :hidden], up_out_grad[:, hidden:]
        wait = ()
    chip_col = pl.BlockSpec((tokens, lanes), lambda g, s: (0, s[CHIP_AT + g]))
    d_qkv, sums_qkv = call(
        partial(attention_back_kernel, slots), scalars,
        [d_attn, queries, keys, values, lse, cos_table, sin_table] + first,
        [rows, chip_col, chip_col, chip_col,
         pl.BlockSpec((1, tokens, 128), lambda g, s: (s[CHIP_AT + g], 0, 0)), table, table] + out_specs,
        [jax.ShapeDtypeStruct((3, tokens, width), BF16), jax.ShapeDtypeStruct((8, width), F32)],
        [pl.BlockSpec((3, tokens, lanes), lambda g, s: (0, 0, s[CHIP_AT + g])),
         pl.BlockSpec((8, lanes), lambda g, s: (0, s[CHIP_AT + g]))],
        (groups,), mask_rooms + [pltpu.VMEM((tokens, lanes), F32)] * 3 + [pltpu.VMEM((tokens, lanes), BF16)],
        after=wait,
    )
    if small:
        d_qkv, up_came, *down_z = next_round(scalars, [d_qkv, up_came, *down_z])
        d_qkv_core = sibling(d_qkv)
        up_one = first_way(add(up_parts[1], up_came[per:]))
        down_sum = sum_four(down_sum, down_z)
        down_z = exchange([down_sum] * 3)
    else:
        qkv_grad = rows_of_all([(attn_in, d_qkv)], width)
    input_grad, sums_one = call(
        partial(d_input_kernel, slots), scalars,
        [d_qkv, activations, time_rows, gain_one, d_resid_one] + first,
        [pl.BlockSpec((1, tokens, width), lambda i, s: (i, 0, 0)), anywhere, whole((slots, width)), line, anywhere]
        + piece_specs(per, width, lambda i, s: i),
        [jax.ShapeDtypeStruct((tokens, width), BF16), jax.ShapeDtypeStruct((8, width), F32)],
        [rows, whole((8, width))], (3,),
        [pltpu.VMEM((tokens, width), F32)] * 2
        + [pltpu.VMEM((tokens, width), BF16), pltpu.VMEM((tokens, width), F32), pltpu.SemaphoreType.DMA((2,))],
    )
    if small:
        half = per // 2
        up_sum, up_send = next_round(
            scalars, [], [sums_one],
            [sum_of(up_parts[0], up_came, up_one, row=rows_, rows=half) for rows_ in ((0, half), (half, 0))],
        )
        up_z = swap_z(up_send, 1)
        qkv_parts = weight_grad(scalars, 0, [(attn_in, d_qkv, attn_in_core, d_qkv_core)], width, after=(up_sum,))
        qkv_parts[2], sums_one = next_round(scalars, [qkv_parts[2], sums_one], down_z)
        qkv_came = second_way(qkv_parts[2])
        time_cols = time_features.astype(F32).T
        depth = 64
        v_odd, v_even = call(
            partial(pack_grads_kernel, slots), scalars,
            [sums_one, sums_qkv, sums_two, up_bias_sum, down_bias_sum, time_cols],
            [whole((8, width)), whole((8, width)), whole((8, width)), whole((1, hidden)), line, whole(time_cols.shape)],
            [jax.ShapeDtypeStruct((4, depth, width), BF16)] * 2, [whole((4, depth, width))] * 2, (1,), cost=SOME_COST,
        )
        v_odd, v_even = v_odd.reshape(-1, width), v_even.reshape(-1, width)
        v_odd, up_z, down_sum = next_round(scalars, [v_odd, up_z, down_sum])
        down_grad = in_place(down_sum, down_z)
        up_sum = add(up_sum, up_z)
        up_z = swap_z(up_sum, 2)
        v_came = sibling(v_odd)
        v_came, *to_one = next_round(
            scalars, [v_came], [up_sum],
            [([(qkv_parts[1], row, 0), (qkv_came, per + row, 0)], half, qkv_columns) for row in (0, half)],
        )
        qkv_one = [first_way(x) for x in to_one]
        *qkv_one, v_came = next_round(scalars, [*qkv_one, v_came])
        low, high = [
            add(qkv_parts[0][row : row + half], qkv_came[row : row + half], x) for row, x in zip((0, half), qkv_one)
        ]
        qkv_sum, qkv_send = jnp.where(even_z, low, high), jnp.where(even_z, high, low)
        qkv_z = swap_z(qkv_send, 1)
        (up_z,) = next_round(scalars, [up_z], [qkv_send])
        up_sum = add(up_sum, up_z)
        up_z = swap_z(up_sum, 1)
        part = add(v_even, v_came).reshape(4, depth, width)
        parts = [part[k] for k in range(4)]
        v_came = [first_way(parts[1]), second_way(parts[2]), swap(parts[3], 6, 6)]
        qkv_sum, part = next_round(scalars, [], [], [sum_of(qkv_sum, qkv_z), sum_of(parts[0], *v_came)])
        qkv_z = swap_z(qkv_sum, 2)
        v_came = swap_z(part, 1)
        output = layer_output((part,))
        qkv_z, v_came = next_round(scalars, [qkv_z, v_came], [output, up_z])
        qkv_sum = add(qkv_sum, qkv_z)
        qkv_grad = joined(qkv_sum, swap_z(qkv_sum, 1))
        part = add(part, v_came)
        share = part.astype(F32) + swap_z(part, 2).astype(F32)
        up_out_grad = joined(up_sum, up_z)
        up_grad, out_grad = up_out_grad[:, :hidden], up_out_grad[:, hidden:]
        time_rows_here = time_weight.shape[0]
        time_grad = share[:time_rows_here]
        one, two, ff = width // BLOCKS, 2 * width // BLOCKS, hidden // BLOCKS
        row = share[time_rows_here]
        (gain_one_grad, shift_one_grad, out_bias_grad, gain_two_grad, shift_two_grad, down_bias_grad,
         value_bias_grad) = [row[i * one : (i + 1) * one] for i in range(7)]
        row = share[time_rows_here + 1]
        qk_bias_grad, up_bias_grad = row[:two], row[two : two + ff]
        time_bias_grad = share[time_rows_here + 2, :one]
    else:
        output = layer_output(())
        d_time = sums_one[2 : 2 + slots]
        time_grad = lax.dot_general(
            time_features.astype(F32), d_time, (((0,), (0,)), ((), ())), precision=lax.Precision.HIGHEST
        )
        vector_sums = (
            sums_one[0], sums_one[1], sums_qkv[:2].reshape(-1), sums_qkv[2], sums_two[2], sums_two[0], sums_two[1],
            up_bias_sum[0], down_bias_sum[0], jnp.sum(d_time, axis=0),
        )
        shares = jnp.concatenate(
            [time_grad.reshape(n_fsdp, -1)] + [v.reshape(n_fsdp, -1) for v in vector_sums], axis=1
        )
        sizes = [time_weight.size] + [v.size // n_fsdp for v in vector_sums]
        shares = jnp.pad(shares, ((0, 0), (0, -shares.shape[1] % 4096))).reshape(n_fsdp, -1, 128)
        shares = lax.psum_scatter(shares.astype(BF16), "fsdp", scatter_dimension=0, tiled=False)
        share = lax.psum(shares, "dp").astype(F32).reshape(-1)
        got = []
        at = 0
        for size in sizes:
            got.append(share[at : at + size])
            at += size
        (time_grad, gain_one_grad, shift_one_grad, qk_bias_grad, value_bias_grad, out_bias_grad, gain_two_grad,
         shift_two_grad, up_bias_grad, down_bias_grad, time_bias_grad) = got
    return (
        output, input_grad, gain_one_grad, shift_one_grad, qkv_grad, qk_bias_grad, value_bias_grad, out_grad, out_bias_grad,
        gain_two_grad, shift_two_grad, up_grad, up_bias_grad, down_grad, down_bias_grad,
        time_grad.reshape(time_weight.shape), time_bias_grad,
    )


def solution(mesh):
    tokens = P(("dp", "fsdp"), None)
    vector = P("fsdp")
    matrix = P("fsdp", None)
    in_specs = (
        tokens, tokens, tokens, vector, vector, matrix, vector, matrix, vector, vector, vector, matrix, vector, matrix,
        vector, matrix, vector, tokens,
    )
    out_specs = (
        tokens, tokens, vector, vector, matrix, vector, vector, matrix, vector, vector, vector, matrix, vector, matrix,
        vector, matrix, vector,
    )
    body = partial(per_device, mesh.shape["dp"], mesh.shape["fsdp"])
    return jax.shard_map(body, mesh=mesh, in_specs=in_specs, out_specs=out_specs, check_vma=False)
```

```python
from functools import partial

import jax
import jax.numpy as jnp
from jax import lax
from jax.experimental import pallas as pl
from jax.experimental.pallas import tpu as pltpu
from jax.sharding import PartitionSpec as P

H = 16
GROUP = 4
BLOCKS = 8
CHIPS = 4
CHIP_AT = BLOCKS
PARITY_AT = CHIP_AT + CHIPS
ENDS_AT = PARITY_AT + 1
FAR = -1e30
NO_COST = pl.CostEstimate(flops=0, bytes_accessed=0, transcendentals=0)
SOME_COST = pl.CostEstimate(flops=30 * 10**9, bytes_accessed=100 * 10**6, transcendentals=0)
F32 = jnp.float32
BF16 = jnp.bfloat16


def rows_by_cols(a, b):
    return lax.dot_general(a, b, (((1,), (0,)), ((), ())), preferred_element_type=F32)


def rows_by_rows(a, b):
    return lax.dot_general(a, b, (((1,), (1,)), ((), ())), preferred_element_type=F32)


def cols_by_cols(a, b):
    return lax.dot_general(a, b, (((0,), (0,)), ((), ())), preferred_element_type=F32)


def call(kernel, scalars, inputs, in_specs, out_shapes, out_specs, grid, scratch=(), aliases=None, after=(), cost=NO_COST):
    count = len(inputs)

    def body(s_ref, *refs):
        kernel(s_ref, *refs[:count], *refs[count + len(after) :])

    return pl.pallas_call(
        body,
        name=getattr(kernel, "func", kernel).__name__,
        grid_spec=pltpu.PrefetchScalarGridSpec(
            num_scalar_prefetch=1,
            grid=grid,
            in_specs=list(in_specs) + [pl.BlockSpec(memory_space=pl.ANY)] * len(after),
            out_specs=out_specs,
            scratch_shapes=list(scratch),
        ),
        out_shape=out_shapes,
        input_output_aliases=aliases or {},
        compiler_params=pltpu.CompilerParams(
            dimension_semantics=("arbitrary",) * len(grid), vmem_limit_bytes=64 * 2**20
        ),
        cost_estimate=cost,
    )(scalars, *inputs, *after)


def round_kernel(counts, s_ref, *refs):
    outs = refs[-len(counts) :] if counts else ()
    at = 0
    for count, out in zip(counts, outs):
        total = refs[at][...].astype(F32)
        for ref in refs[at + 1 : at + count]:
            total = total + ref[...].astype(F32)
        out[...] = total.astype(BF16)
        at += count


def next_round(scalars, passed, others=(), sums=()):
    anywhere = pl.BlockSpec(memory_space=pl.ANY)
    steps = 2
    specs, inputs, counts, shapes, out_specs = [], [], [], [], []
    for parts, rows, columns in sums:
        size = rows // steps
        for array, row, column in parts:
            even, odd = row if isinstance(row, tuple) else (row, row)

            def at(i, s, even=even // size, odd=odd // size, column=column // columns):
                return (i + even + s[PARITY_AT] * (odd - even), column)

            specs.append(pl.BlockSpec((size, columns), at))
            inputs.append(array)
        counts.append(len(parts))
        shapes.append(jax.ShapeDtypeStruct((rows, columns), BF16))
        out_specs.append(pl.BlockSpec((size, columns), lambda i, s: (i, 0)))
    first = len(inputs)

    def kernel(s_ref, *refs):
        given = first + len(passed) + len(others)
        round_kernel(counts, s_ref, *refs[:first], *refs[given + len(passed) :])

    out = pl.pallas_call(
        kernel,
        name="next_round",
        grid_spec=pltpu.PrefetchScalarGridSpec(
            num_scalar_prefetch=1,
            grid=(steps if sums else 1,),
            in_specs=specs + [anywhere] * (len(passed) + len(others)),
            out_specs=[anywhere] * len(passed) + out_specs,
        ),
        out_shape=[jax.ShapeDtypeStruct(x.shape, x.dtype) for x in passed] + shapes,
        input_output_aliases={1 + first + i: i for i in range(len(passed))},
        compiler_params=pltpu.CompilerParams(dimension_semantics=("arbitrary",), vmem_limit_bytes=64 * 2**20),
        cost_estimate=NO_COST,
    )(scalars, *inputs, *passed, *others)
    return list(out)


def copy_after(x, *others):
    def kernel(x_ref, *refs):
        refs[-1][...] = x_ref[...]

    block = pl.BlockSpec((x.shape[0] // 2, x.shape[1]), lambda i: (i, 0))
    return pl.pallas_call(
        kernel,
        grid=(2,),
        out_shape=jax.ShapeDtypeStruct(x.shape, x.dtype),
        in_specs=[block] + [pl.BlockSpec(memory_space=pl.ANY)] * len(others),
        out_specs=block,
        cost_estimate=NO_COST,
    )(x, *others)


def whole(shape):
    zeros = (0,) * len(shape)
    return pl.BlockSpec(shape, lambda *_: zeros)


def normalize(x):
    center = x - jnp.mean(x, axis=-1, keepdims=True)
    variance = jnp.mean(center * center, axis=-1, keepdims=True)
    inverse = lax.rsqrt(variance + 1e-05)
    return center * inverse, inverse


def normalize_back(grad, normal, inverse, gain):
    scaled = grad * gain
    return inverse * (
        scaled
        - jnp.mean(scaled, axis=-1, keepdims=True)
        - normal * jnp.mean(scaled * normal, axis=-1, keepdims=True)
    )


def row_ids(count, first=0):
    return lax.broadcasted_iota(jnp.int32, (count, 1), 0) + first


def members_of(s_ref, ids, slots):
    out = []
    start = 0
    for slot in range(slots):
        end = s_ref[ENDS_AT + slot]
        out.append((ids >= start) & (ids < end))
        start = end
    return out


def segment_of(s_ref, ids, slots):
    segment = jnp.zeros(ids.shape, jnp.int32)
    for slot in range(slots):
        segment = segment + (ids >= s_ref[ENDS_AT + slot]).astype(jnp.int32)
    return segment


def resid_zero_of(s_ref, act, time_rows, first, slots):
    x = act.astype(F32)
    for slot, inside in enumerate(members_of(s_ref, row_ids(act.shape[0], first), slots)):
        x = x + jnp.where(inside, time_rows[slot : slot + 1, :], 0.0)
    return x


def piece_specs(rows, columns, at):
    return [pl.BlockSpec((rows, columns), lambda *a: (0, at(*a)))] * BLOCKS


def rows_of(refs, at=slice(None)):
    return jnp.concatenate([ref[:, at] for ref in refs], axis=0)


def pack_kernel(s_ref, qkv_ref, out_ref, time_ref, *refs):
    vectors, pack_ref = refs[:-1], refs[-1]
    rows, columns = qkv_ref.shape
    pack_ref[0:rows, 0:columns] = qkv_ref[...]
    pack_ref[0:rows, columns:] = out_ref[...]
    depth = pack_ref.shape[0] - rows
    width = out_ref.shape[1]
    pack_ref[rows:, 0:width] = time_ref[0:depth, :]
    pack_ref[rows:, width : 2 * width] = time_ref[depth:, :]
    line = jnp.concatenate([v[...].astype(F32).reshape(1, -1) for v in vectors], axis=1)
    line = jnp.concatenate([line, jnp.zeros((1, pack_ref.shape[1] - 2 * width - line.shape[1]), F32)], axis=1)
    lines = jnp.where(row_ids(depth) == 0, line, 0.0).astype(BF16)
    pack_ref[rows:, 2 * width :] = lines


def norm_one_kernel(slots, s_ref, act_ref, feat_ref, *refs):
    extras = refs[:BLOCKS]
    out_ref, time_ref, lines_ref, qkv_b_ref, up_b_ref = refs[BLOCKS:]
    depth = extras[0].shape[0]
    width = act_ref.shape[1]
    small = width // BLOCKS
    time_rows = jnp.zeros((slots, width), F32)
    for j in range(BLOCKS):
        block = s_ref[j]
        for half in range(2):
            at = pl.multiple_of((block * 2 + half) * 128, 128)
            part = feat_ref[:, pl.ds(at, 128)]
            time_rows = time_rows + rows_by_cols(part[:, 0:depth], extras[j][:, half * width : (half + 1) * width])
        line = extras[j][:, 2 * width :].astype(F32)[0:1]
        at = pl.ds(pl.multiple_of(block * small, 128), small)
        for v in range(7):
            lines_ref[v : v + 1, at] = line[:, v * small : (v + 1) * small]
        first = 7 * small
        for ref in (qkv_b_ref, up_b_ref):
            size = ref.shape[1] // BLOCKS
            ref[0:1, pl.ds(pl.multiple_of(block * size, 128), size)] = line[:, first : first + size]
            first += size
    lines_ref[7:8, :] = jnp.zeros((1, width), F32)
    time_rows = time_rows + lines_ref[6:7, :]
    time_ref[...] = time_rows
    x = resid_zero_of(s_ref, act_ref[...], time_rows, 0, slots)
    normal, _ = normalize(x)
    out_ref[...] = (normal * lines_ref[0:1, :] + lines_ref[1:2, :]).astype(BF16)


def by_block(s_ref, x_ref, out_ref, back=False):
    width = x_ref.shape[1] // BLOCKS
    for j in range(BLOCKS):
        at = pl.ds(pl.multiple_of(s_ref[j] * width, 128), width)
        if back:
            out_ref[:, at] = x_ref[:, j * width : (j + 1) * width]
        else:
            out_ref[:, j * width : (j + 1) * width] = x_ref[:, at]


def turn(x, cosine, sine):
    lanes = lax.broadcasted_iota(jnp.int32, x.shape, 1)
    width = x.shape[1]
    swapped = jnp.where(lanes % 64 < 32, pltpu.roll(x, width - 32, 1), pltpu.roll(x, 32, 1))
    return x * cosine + swapped * sine


def lane_ids(width):
    return lax.broadcasted_iota(jnp.int32, (1, width), 1)


def head_lanes(h, width):
    lanes = lane_ids(width)
    return (lanes >= h * 64) & (lanes < (h + 1) * 64)


def spare_head(h):
    return 1 if h == 0 else 0


def mask_lanes(s_ref, tokens, width, slots, query_ref, key_ref):
    segment = segment_of(s_ref, row_ids(tokens), slots)
    for p in range(2):
        at = lane_ids(width) - 64 * p
        inside = (at >= 0) & (at <= slots)
        more = (at > slots) & (at <= slots + 3)
        query_ref[p] = jnp.where(inside & (at != segment), FAR, 0.0).astype(BF16)
        key_ref[p] = jnp.where((inside & (at == segment)) | more, 1.0, 0.0).astype(BF16)


def attention_kernel(slots, s_ref, x_ref, bq_ref, bk_ref, bv_ref, cos_ref, sin_ref, *refs):
    wq, wk, wv = refs[:BLOCKS], refs[BLOCKS : 2 * BLOCKS], refs[2 * BLOCKS : 3 * BLOCKS]
    q_ref, k_ref, v_ref, att_ref, lse_ref, rel_ref, qm_ref, km_ref = refs[3 * BLOCKS :]
    tokens, width = q_ref.shape

    @pl.when(pl.program_id(0) == 0)
    def _():
        by_block(s_ref, x_ref, rel_ref)
        mask_lanes(s_ref, tokens, width, slots, qm_ref, km_ref)

    x = rel_ref[...]
    cosine, sine = cos_ref[...], sin_ref[...]
    q = turn(rows_by_cols(x, rows_of(wq)) + bq_ref[...], cosine, sine).astype(BF16)
    k = turn(rows_by_cols(x, rows_of(wk)) + bk_ref[...], cosine, sine).astype(BF16)
    v = (rows_by_cols(x, rows_of(wv)) + bv_ref[...]).astype(BF16)
    q = q * jnp.asarray(0.125, BF16)
    q_ref[...] = q
    k_ref[...] = k
    v_ref[...] = v
    masked_keys = [jnp.where(head_lanes(p, width), km_ref[p], k) for p in range(2)]
    total = jnp.zeros((tokens, width), F32)
    lse = jnp.zeros((tokens, 128), F32)
    for h in range(GROUP):
        p = spare_head(h)
        mine = head_lanes(h, width)
        scores = rows_by_rows(jnp.where(mine, q, qm_ref[p]), masked_keys[p])
        top = jnp.max(scores, axis=1, keepdims=True)
        e = jnp.exp(scores - top)
        denominator = jnp.sum(e, axis=1, keepdims=True)
        part = rows_by_cols(e.astype(BF16), v) * (1.0 / denominator)
        total = jnp.where(mine, part, total)
        lse = jnp.where(lane_ids(128) == h, top + jnp.log(denominator), lse)
    att_ref[...] = total.astype(BF16)
    lse_ref[0] = lse


def out_kernel(slots, s_ref, att_ref, act_ref, time_ref, bias_ref, gain_ref, shift_ref, *refs):
    w, (res_ref, mlp_ref, rel_ref) = refs[:BLOCKS], refs[BLOCKS:]
    by_block(s_ref, att_ref, rel_ref)
    x = resid_zero_of(s_ref, act_ref[...], time_ref[...], 0, slots)
    x = x + rows_by_cols(rel_ref[...], rows_of(w)) + bias_ref[...]
    res_ref[...] = x
    normal, _ = normalize(x)
    mlp_ref[...] = (normal * gain_ref[...] + shift_ref[...]).astype(BF16)


def up_kernel(s_ref, x_ref, bias_ref, *refs):
    w, (act_ref, slope_ref, rel_ref) = refs[:BLOCKS], refs[BLOCKS:]

    @pl.when(pl.program_id(0) == 0)
    def _():
        by_block(s_ref, x_ref, rel_ref)

    pre = rows_by_cols(rel_ref[...], rows_of(w)) + bias_ref[...]
    cdf = 0.5 + 0.5 * lax.erf(pre * 0.7071067811865476)
    density = 0.3989422804014327 * jnp.exp(-0.5 * pre * pre)
    act_ref[...] = (pre * cdf).astype(BF16)
    slope_ref[...] = (cdf + pre * density).astype(BF16)


def down_copies(refs, held_ref, sems):
    return [(n // 2, pltpu.make_async_copy(ref, held_ref.at[n], sems.at[n])) for n, ref in enumerate(refs)]


def fetch_down(step, copies):
    @pl.when(step == 0)
    def _():
        for _, copy in copies:
            copy.start()

    for chip in range(CHIPS):

        @pl.when(step == chip)
        def _():
            for owner, copy in copies:
                if owner == chip:
                    copy.wait()


def halves_of(s_ref, width):
    core = s_ref[0] % 2
    return [pl.ds(pl.multiple_of(at * width, 128), width) for at in (core, 1 - core)]


def down_kernel(slots, s_ref, a_ref, res_ref, bias_ref, *refs):
    w, (out_ref, acc_ref, held_ref, sems) = refs[:BLOCKS], refs[BLOCKS:]
    c = pl.program_id(0)
    fetch_down(c, down_copies(w, held_ref, sems))

    @pl.when(c == 0)
    def _():
        acc_ref[...] = res_ref[...] + bias_ref[...]

    for n, at in enumerate(halves_of(s_ref, held_ref.shape[1])):
        acc_ref[...] += rows_by_cols(a_ref[:, at], held_ref[2 * c + n])

    @pl.when(c == pl.num_programs(0) - 1)
    def _():
        valid = row_ids(out_ref.shape[0]) < s_ref[ENDS_AT + slots - 1]
        out_ref[...] = jnp.where(valid, acc_ref[...], 0.0).astype(BF16)


def branch_kernel(slots, s_ref, cot_ref, branch_ref, bias_ref):
    valid = row_ids(cot_ref.shape[0]) < s_ref[ENDS_AT + slots - 1]
    branch = jnp.where(valid, cot_ref[...].astype(F32), 0.0)
    branch_ref[...] = branch.astype(BF16)
    bias_ref[...] = jnp.sum(branch, axis=0, keepdims=True)


def mlp_back_kernel(s_ref, branch_ref, slope_ref, res_ref, gain_ref, *refs):
    down, up = refs[:BLOCKS], refs[BLOCKS : 2 * BLOCKS]
    pre_ref, bias_ref, dres_ref, datt_ref, sums_ref, acc_ref, grad_ref, held_ref, sems = refs[2 * BLOCKS :]
    c = pl.program_id(0)
    fetch_down(c, down_copies(down, held_ref, sems))

    @pl.when(c == 0)
    def _():
        acc_ref[...] = jnp.zeros_like(acc_ref)

    branch = branch_ref[...]
    for n, at in enumerate(halves_of(s_ref, held_ref.shape[1])):
        d_pre = (rows_by_rows(branch, held_ref[2 * c + n]) * slope_ref[:, at].astype(F32)).astype(BF16)
        pre_ref[:, at] = d_pre
        bias_ref[:, at] = jnp.sum(d_pre.astype(F32), axis=0, keepdims=True)
        acc_ref[...] += rows_by_rows(d_pre, rows_of(up, at))

    @pl.when(c == pl.num_programs(0) - 1)
    def _():
        by_block(s_ref, acc_ref, grad_ref, back=True)
        grad = grad_ref[...]
        normal, inverse = normalize(res_ref[...])
        d_res = branch.astype(F32) + normalize_back(grad, normal, inverse, gain_ref[...])
        dres_ref[...] = d_res
        d_att = d_res.astype(BF16)
        datt_ref[...] = d_att
        sums_ref[0:1, :] = jnp.sum(grad * normal, axis=0, keepdims=True)
        sums_ref[1:2, :] = jnp.sum(grad, axis=0, keepdims=True)
        sums_ref[2:3, :] = jnp.sum(d_att.astype(F32), axis=0, keepdims=True)
        sums_ref[3:8, :] = jnp.zeros((5, sums_ref.shape[1]), F32)


def three_lanes(x, p, slots):
    first = x.astype(BF16)
    rest = x - first.astype(F32)
    second = rest.astype(BF16)
    third = (rest - second.astype(F32)).astype(BF16)
    at = lane_ids(64 * GROUP) - 64 * p - slots - 1
    spread = jnp.where(at == 0, first, jnp.where(at == 1, second, third))
    return jnp.where((at >= 0) & (at < 3), spread, jnp.zeros((), BF16))


def attention_back_kernel(slots, s_ref, d_ref, q_ref, k_ref, v_ref, lse_ref, cos_ref, sin_ref, *refs):
    w, (out_ref, sums_ref, qm_ref, km_ref, dq_ref, dk_ref, dv_ref, heads_ref) = refs[:BLOCKS], refs[BLOCKS:]
    tokens, width = q_ref.shape
    step = pl.program_id(0)

    @pl.when(pl.program_id(0) == 0)
    def _():
        mask_lanes(s_ref, tokens, width, slots, qm_ref, km_ref)

    for chip, pieces in enumerate((w[0:2], w[2:4], w[4:6], w[6:8])):

        @pl.when(step == chip)
        def _():
            both = rows_by_rows(d_ref[...], rows_of(pieces)).astype(BF16)
            for n, at in enumerate(halves_of(s_ref, width // 2)):
                heads_ref[:, at] = both[:, n * (width // 2) : (n + 1) * (width // 2)]

    d_heads = heads_ref[...]
    q, k, v = q_ref[...], k_ref[...], v_ref[...]
    for h in range(GROUP):
        p = spare_head(h)
        mine, spare = head_lanes(h, width), head_lanes(p, width)
        queries = jnp.where(spare, qm_ref[p] + three_lanes(-lse_ref[0, :, h : h + 1], p, slots), q)
        soft = jnp.exp(rows_by_rows(jnp.where(mine, k, km_ref[p]), queries))
        product = soft * rows_by_rows(jnp.where(mine, v, jnp.zeros((), BF16)), d_heads)
        row_terms = jnp.sum(product, axis=0, keepdims=True)
        d_scores = (product - soft * row_terms).astype(BF16)
        d_v = rows_by_cols(soft.astype(BF16), d_heads)
        d_k = rows_by_cols(d_scores, q)
        d_q = cols_by_cols(d_scores, k)
        if h == 0:
            dq_ref[...], dk_ref[...], dv_ref[...] = d_q, d_k, d_v
        else:
            dq_ref[...] = jnp.where(mine, d_q, dq_ref[...])
            dk_ref[...] = jnp.where(mine, d_k, dk_ref[...])
            dv_ref[...] = jnp.where(mine, d_v, dv_ref[...])
    cosine, sine = cos_ref[...], sin_ref[...]
    sums_ref[...] = jnp.zeros_like(sums_ref)
    parts = (turn(dq_ref[...] * 0.125, cosine, -sine), turn(dk_ref[...], cosine, -sine), dv_ref[...])
    for i, part in enumerate(parts):
        part = part.astype(BF16)
        out_ref[i] = part
        sums_ref[i : i + 1, :] = jnp.sum(part.astype(F32), axis=0, keepdims=True)


def d_input_kernel(slots, s_ref, d_ref, act_ref, time_ref, gain_ref, dres_ref, *refs):
    w, (out_ref, sums_ref, acc_ref, grad_ref, act_held, dres_held, sems) = refs[:BLOCKS], refs[BLOCKS:]
    late = [pltpu.make_async_copy(act_ref, act_held, sems.at[0]), pltpu.make_async_copy(dres_ref, dres_held, sems.at[1])]
    j = pl.program_id(0)

    @pl.when(j == 0)
    def _():
        for copy in late:
            copy.start()
        acc_ref[...] = rows_by_rows(d_ref[0], rows_of(w))

    @pl.when(j > 0)
    def _():
        acc_ref[...] += rows_by_rows(d_ref[0], rows_of(w))

    @pl.when(j == pl.num_programs(0) - 1)
    def _():
        for copy in late:
            copy.wait()
        by_block(s_ref, acc_ref, grad_ref, back=True)
        grad = grad_ref[...]
        normal, inverse = normalize(resid_zero_of(s_ref, act_held[...], time_ref[...], 0, slots))
        d_in = dres_held[...] + normalize_back(grad, normal, inverse, gain_ref[...])
        out_ref[...] = d_in.astype(BF16)
        sums_ref[...] = jnp.zeros_like(sums_ref)
        sums_ref[0:1, :] = jnp.sum(grad * normal, axis=0, keepdims=True)
        sums_ref[1:2, :] = jnp.sum(grad, axis=0, keepdims=True)
        for slot, inside in enumerate(members_of(s_ref, row_ids(act_held.shape[0]), slots)):
            sums_ref[2 + slot : 3 + slot, :] = jnp.sum(jnp.where(inside, d_in, 0.0), axis=0, keepdims=True)


def grad_kernel(steps, sources, groups, s_ref, *refs):
    per = 5 * sources
    outs = refs[per * len(steps) :]
    i = pl.program_id(0)
    first = 0
    for n, (count, lead) in enumerate(steps):
        mine = refs[per * n : per * (n + 1)]

        @pl.when((i >= first) & (i < first + count))
        def _():
            product = None
            for source in range(sources):
                *a_refs, b_ref = mine[5 * source : 5 * source + 5]
                a = jnp.concatenate([ref[...] for ref in a_refs], axis=1)
                part = cols_by_cols(a, b_ref[0] if lead else b_ref[...])
                product = part if product is None else product + part
            rows = product.shape[0] // 4
            for out, group in zip(outs, groups):
                out[...] = product[group[0] * rows : (group[-1] + 1) * rows].astype(BF16)

        first += count


def weight_grad(scalars, odd, pairs, tile, after=(), groups=((0,), (1,), (2, 3))):
    tokens, width = pairs[0][0].shape[0], pairs[0][0].shape[1] // BLOCKS
    sources = len(pairs[0]) // 2
    specs, inputs, steps = [], [], []
    first = 0
    for pair in pairs:
        lead = pair[1].ndim == 3
        per = pair[1].shape[-1] // tile
        count = per * (pair[1].shape[0] if lead else 1)

        def local(i, first=first, count=count):
            return jnp.clip(i - first, 0, count - 1)

        for a, b in zip(pair[::2], pair[1::2]):
            for j in range(4):
                specs.append(pl.BlockSpec((tokens, width), lambda i, s, j=j: (0, s[2 * j + odd])))
                inputs.append(a)
            if lead:
                specs.append(
                    pl.BlockSpec((1, tokens, tile), lambda i, s, at=local, per=per: (at(i) // per, 0, at(i) % per))
                )
            else:
                specs.append(pl.BlockSpec((tokens, tile), lambda i, s, at=local: (0, at(i))))
            inputs.append(b)
        steps.append((count, lead))
        first += count
    sizes = [len(group) * width for group in groups]
    out = call(
        partial(grad_kernel, tuple(steps), sources, groups), scalars, inputs, specs,
        [jax.ShapeDtypeStruct((rows, first * tile), BF16) for rows in sizes],
        [pl.BlockSpec((rows, tile), lambda i, s: (0, i)) for rows in sizes], (first,), after=after,
    )
    return list(out)


def pack_grads_kernel(slots, s_ref, one_ref, qkv_ref, two_ref, up_ref, down_ref, time_ref, odd_ref, even_ref):
    rows = time_ref.shape[0] // BLOCKS
    d_time = one_ref[2 : 2 + slots, :]
    one, two = d_time.shape[1] // BLOCKS, 2 * d_time.shape[1] // BLOCKS
    ff = up_ref.shape[1] // BLOCKS
    odd_ref[...] = jnp.zeros_like(odd_ref)
    even_ref[...] = jnp.zeros_like(even_ref)
    for j in range(BLOCKS):
        block = s_ref[j]
        out, chip = (odd_ref, (0, 2, 1, 3)[j // 2]) if j % 2 else (even_ref, j // 2)
        features = time_ref[pl.ds(pl.multiple_of(block * rows, 8), rows), :]
        out[chip, 0:rows, :] = sum(features[:, s : s + 1] * d_time[s : s + 1, :] for s in range(slots)).astype(BF16)
        at = pl.ds(pl.multiple_of(block * one, 128), one)
        sources = (one_ref[0:1, at], one_ref[1:2, at], two_ref[2:3, at], two_ref[0:1, at], two_ref[1:2, at],
                   down_ref[0:1, at], qkv_ref[2:3, at])
        line = jnp.concatenate(sources, axis=1)
        out[chip, rows : rows + 1, 0 : line.shape[1]] = line.astype(BF16)
        wide = pl.ds(pl.multiple_of((block % 4) * two, 128), two)
        pair = jnp.where(block < 4, qkv_ref[0:1, wide], qkv_ref[1:2, wide])
        hidden = up_ref[0:1, pl.ds(pl.multiple_of(block * ff, 128), ff)]
        out[chip, rows + 1 : rows + 2, 0 : two + ff] = jnp.concatenate([pair, hidden], axis=1).astype(BF16)
        bias = jnp.sum(one_ref[2 : 2 + slots, at], axis=0, keepdims=True)
        out[chip, rows + 2 : rows + 3, 0:one] = bias.astype(BF16)


def per_device(
    n_dp, n_fsdp, activations, time_features, lengths, attn_gain, attn_shift, qkv_weight, qkv_bias, out_weight, out_bias,
    mlp_gain, mlp_shift, up_weight, up_bias, down_weight, down_bias, time_weight, time_bias, cotangent,
):
    tokens, width = activations.shape
    slots = lengths.shape[1]
    hidden = down_weight.shape[0] * n_fsdp
    small = n_fsdp == BLOCKS
    me = lax.axis_index("fsdp")
    blocks = jnp.arange(BLOCKS, dtype=jnp.int32)
    chips = jnp.arange(CHIPS, dtype=jnp.int32)
    if small:
        turned = jnp.where(chips % 3 > 0, 3 - chips, chips)
        chips = jnp.where(me % 2 == 0, turned, chips)
        blocks = (2 * chips[:, None] + jnp.arange(2, dtype=jnp.int32)[None, :]).reshape(-1) ^ me
        chips = chips ^ (me // 2)
    upto = jnp.arange(slots)[:, None] >= jnp.arange(slots)[None, :]
    ends = jnp.sum(jnp.where(upto, lengths, 0), axis=1)
    parity = lax.axis_index("dp") % 2
    scalars = jnp.concatenate([blocks, chips, parity[None], ends]).astype(jnp.int32)

    def swap(x, even, odd):
        return lax.ppermute(x, "fsdp", [(i, i ^ (odd if i % 2 else even)) for i in range(n_fsdp)])

    def sibling(x):
        return swap(x, 1, 1)

    def first_way(x):
        return swap(x, 4, 2)

    def second_way(x):
        return swap(x, 2, 4)

    def pieces(own, first, second, far, own_sibling, first_sibling, second_sibling, far_sibling):
        return [own, own_sibling, first, second_sibling, second, first_sibling, far, far_sibling]

    def add(*parts):
        total = parts[0].astype(F32)
        for part in parts[1:]:
            total = total + part.astype(F32)
        return total.astype(BF16)

    def gather_rows(w):
        return lax.all_gather(w, "fsdp", axis=0, tiled=True).reshape(BLOCKS, -1, w.shape[1])

    rows = whole((tokens, width))
    line = whole((1, width))
    anywhere = pl.BlockSpec(memory_space=pl.ANY)
    vectors = [attn_gain, attn_shift, out_bias, mlp_gain, mlp_shift, down_bias, time_bias, qkv_bias, up_bias]
    per = width // BLOCKS
    qkv_columns = qkv_weight.shape[1]
    columns = qkv_columns + width
    depth = 16
    if small:
        sources = [qkv_weight, out_weight, time_weight] + vectors
        pack = call(
            pack_kernel, scalars, sources, [whole(x.shape) for x in sources],
            jax.ShapeDtypeStruct((per + depth, columns), BF16), whole((per + depth, columns)), (1,),
        )
        first_one, first_two, first_core = first_way(pack), second_way(pack), sibling(pack)
        up_own, down_own = copy_after(up_weight, pack), copy_after(down_weight, pack)
    else:
        gathered = [lax.all_gather(v, "fsdp", axis=0, tiled=True).reshape(BLOCKS, -1) for v in vectors]
        matrices = jnp.concatenate([gather_rows(qkv_weight), gather_rows(out_weight)], axis=2)
        times = lax.all_gather(time_weight, "fsdp", axis=0, tiled=True).reshape(BLOCKS, 2, depth, width)
        lines = jnp.concatenate(gathered, axis=1)
        lines = jnp.pad(lines, ((0, 0), (0, columns - 2 * width - lines.shape[1])))[:, None]
        lines = jnp.pad(lines, ((0, 0), (0, depth - 1), (0, 0)))
        extra = jnp.concatenate([times[:, 0], times[:, 1], lines], axis=2)
        first = list(jnp.concatenate([matrices, extra], axis=1))
        up_rel = list(gather_rows(up_weight))
        down_rel = list(gather_rows(down_weight))

    ids = jnp.arange(tokens, dtype=jnp.int32)[:, None]
    starts = ends - lengths[0]
    inside = (ids >= starts[None, :]) & (ids < ends[None, :])
    position = (ids[:, 0] - jnp.sum(jnp.where(inside, starts[None, :], 0), axis=1)).astype(F32)
    frequency = 10000.0 ** (-2.0 * jnp.arange(32, dtype=F32) / 64)
    angles = position[:, None] * frequency[None, :]
    cosine, sine = jnp.cos(angles), jnp.sin(angles)
    lanes = 64 * GROUP
    cos_table = jnp.tile(cosine, (1, 2 * GROUP))
    sin_table = jnp.tile(jnp.concatenate([-sine, sine], axis=1), (1, GROUP))

    d_branch, down_bias_sum = call(
        partial(branch_kernel, slots), scalars, [cotangent], [rows],
        [jax.ShapeDtypeStruct((tokens, width), BF16), jax.ShapeDtypeStruct((1, width), F32)], [rows, line], (1,),
    )
    if small:
        first_one, first_two = next_round(
            scalars, [first_one, first_two], [first_core, d_branch, up_own, down_own, cos_table, sin_table]
        )
        first_far = second_way(first_one)
        core_one, core_two, branch_core = sibling(first_one), sibling(first_two), sibling(d_branch)
        first_far, up_own = next_round(scalars, [first_far, up_own], [core_one, core_two, branch_core])
        up_one, up_two = first_way(up_own), second_way(up_own)
        first = pieces(pack, first_one, first_two, first_far, first_core, core_one, core_two, sibling(first_far))
    spread = time_features.reshape(slots, 2 * BLOCKS, -1)
    spread = jnp.pad(spread, ((0, 0), (0, 0), (0, 128 - spread.shape[2]))).reshape(slots, -1)
    extra_specs = [pl.BlockSpec((depth, columns), lambda i, s: (per // depth, 0))] * BLOCKS
    attn_in, time_rows, lines, qkv_b, up_b = call(
        partial(norm_one_kernel, slots), scalars, [activations, spread] + first,
        [rows, whole(spread.shape)] + extra_specs,
        [jax.ShapeDtypeStruct((tokens, width), BF16), jax.ShapeDtypeStruct((slots, width), F32),
         jax.ShapeDtypeStruct((8, width), F32), jax.ShapeDtypeStruct((1, qkv_columns), F32),
         jax.ShapeDtypeStruct((1, hidden), F32)],
        [rows, whole((slots, width)), whole((8, width)), whole((1, qkv_columns)), whole((1, hidden))], (1,),
        after=(d_branch,),
    )
    gain_one, shift_one, out_b, gain_two, shift_two, down_b = [lines[i : i + 1] for i in range(6)]
    groups = H // GROUP
    col = pl.BlockSpec((tokens, lanes), lambda g, s: (0, g))
    table = whole((tokens, lanes))
    mask_rooms = [pltpu.VMEM((2, tokens, lanes), BF16)] * 2
    qkv_specs = []
    for o in range(3):
        qkv_specs += piece_specs(per, lanes, lambda g, s, o=o: o * groups + g)
    queries, keys, values, attended, lse = call(
        partial(attention_kernel, slots), scalars,
        [attn_in, qkv_b, qkv_b, qkv_b, cos_table, sin_table] + first * 3,
        [rows] + [pl.BlockSpec((1, lanes), lambda g, s, o=o: (0, o * groups + g)) for o in range(3)]
        + [table, table] + qkv_specs,
        [jax.ShapeDtypeStruct((tokens, width), BF16)] * 4 + [jax.ShapeDtypeStruct((groups, tokens, 128), F32)],
        [col, col, col, col, pl.BlockSpec((1, tokens, 128), lambda g, s: (g, 0, 0))],
        (groups,), [pltpu.VMEM((tokens, width), BF16)] + mask_rooms)
    if small:
        up_one, up_two, up_own = next_round(scalars, [up_one, up_two, up_own], [attended])
        up_far = second_way(up_one)
        up_core, core_one, core_two = sibling(up_own), sibling(up_one), sibling(up_two)
        attended_core = sibling(attended)
        wait = (up_one,)
    else:
        wait = ()
    out_specs = piece_specs(per, width, lambda *a: qkv_columns // width)
    resid_one, mlp_in = call(
        partial(out_kernel, slots), scalars,
        [attended, activations, time_rows, out_b, gain_two, shift_two] + first,
        [rows, rows, whole((slots, width)), line, line, line] + out_specs,
        [jax.ShapeDtypeStruct((tokens, width), F32), jax.ShapeDtypeStruct((tokens, width), BF16)],
        [rows, rows], (1,), [pltpu.VMEM((tokens, width), BF16)], after=wait,
    )
    if small:
        up_far, down_own = next_round(scalars, [up_far, down_own], [core_one, core_two, up_core, mlp_in, attended_core])
        up_rel = pieces(up_own, up_one, up_two, up_far, up_core, core_one, core_two, sibling(up_far))
        down_one, down_two, down_core = first_way(down_own), second_way(down_own), sibling(down_own)
        attn_in_core = sibling(attn_in)
    tile = hidden // CHIPS
    wide = pl.BlockSpec((tokens, tile), lambda i, s: (0, i))
    activated, slope = call(
        up_kernel, scalars, [mlp_in, up_b] + up_rel,
        [rows, pl.BlockSpec((1, tile), lambda i, s: (0, i))] + piece_specs(per, tile, lambda i, s: i),
        [jax.ShapeDtypeStruct((tokens, hidden), BF16)] * 2, [wide, wide], (CHIPS,),
        [pltpu.VMEM((tokens, width), BF16)])

    even_z = parity == 0

    def swap_z(x, bit):
        return lax.ppermute(x, "dp", [(i, i ^ bit) for i in range(n_dp)])

    def sum_of(*arrays, row=0, column=0, rows=None, columns=None):
        shape = arrays[0].shape
        return [(x, row, column) for x in arrays], rows or shape[0], columns or shape[1]

    def halves(*parts):
        half = parts[0].shape[0] // 2
        low, high = add(*[x[:half] for x in parts]), add(*[x[half:] for x in parts])
        return jnp.where(even_z, low, high), jnp.where(even_z, high, low)

    def quarters(*parts):
        size = parts[0].shape[0] // 4
        place = lax.axis_index("dp")
        cuts = [[lax.dynamic_slice_in_dim(x, (place ^ bits) * size, size) for x in parts] for bits in range(4)]
        return [add(*cut) for cut in cuts]

    def exchange(parts):
        return [swap_z(x, bits) for x, bits in zip(parts, (1, 2, 3))]

    def sum_four(own, came):
        one, two, three = [x.astype(F32) for x in came]
        return ((own.astype(F32) + one) + (two + three)).astype(BF16)

    def in_place(own, came):
        four = jnp.stack([own, *came]).reshape(2, 2, *own.shape)
        place = lax.axis_index("dp")
        for axis, bit in ((0, 2), (1, 1)):
            four = jnp.where((place & bit) > 0, jnp.flip(four, axis), four)
        return four.reshape(-1, own.shape[1]).astype(F32)

    def joined(own, other):
        return jnp.where(even_z, jnp.concatenate([own, other]), jnp.concatenate([other, own])).astype(F32)

    def rows_of_all(pairs, tile):
        blocks = [weight_grad(scalars, odd, pairs, tile) for odd in range(2)]
        blocks = [jnp.concatenate(x).reshape(CHIPS, -1, x[0].shape[1]) for x in blocks]
        both = jnp.stack(blocks, axis=1).reshape(-1, blocks[0].shape[2])
        return lax.psum(lax.psum_scatter(both, "fsdp", scatter_dimension=0, tiled=True), "dp").astype(F32)

    if small:
        down_one, down_two, activated = next_round(scalars, [down_one, down_two, activated], [down_core, attn_in_core])
        down_far = second_way(down_one)
        activated_core = sibling(activated)
        down_parts = weight_grad(scalars, 0, [(activated, d_branch, activated_core, branch_core)], 512)
        down_far, down_parts[2], down_one, down_two = next_round(
            scalars, [down_far, down_parts[2], down_one, down_two]
        )
        core_one, core_two = sibling(down_one), sibling(down_two)
        down_came = second_way(down_parts[2])
        down_rel = pieces(down_own, down_one, down_two, down_far, down_core, core_one, core_two, sibling(down_far))
        mlp_in_core = sibling(mlp_in)
    else:
        down_grad = rows_of_all([(activated, d_branch)], 512)

    chip_wide = pl.BlockSpec((tokens, tile), lambda i, s: (0, s[CHIP_AT + i]))
    down_rooms = [pltpu.VMEM((BLOCKS, hidden // BLOCKS, width), BF16), pltpu.SemaphoreType.DMA((BLOCKS,))]
    d_pre, up_bias_sum, d_resid_one, d_attn, sums_two = call(
        mlp_back_kernel, scalars, [d_branch, slope, resid_one, gain_two] + down_rel + up_rel,
        [rows, chip_wide, rows, line] + [pl.BlockSpec(memory_space=pl.ANY)] * BLOCKS
        + piece_specs(per, tile, lambda i, s: s[CHIP_AT + i]),
        [jax.ShapeDtypeStruct((tokens, hidden), BF16),
         jax.ShapeDtypeStruct((1, hidden), F32), jax.ShapeDtypeStruct((tokens, width), F32),
         jax.ShapeDtypeStruct((tokens, width), BF16), jax.ShapeDtypeStruct((8, width), F32)],
        [chip_wide, pl.BlockSpec((1, tile), lambda i, s: (0, s[CHIP_AT + i])), rows, rows, whole((8, width))],
        (CHIPS,), [pltpu.VMEM((tokens, width), F32)] * 2 + down_rooms,
    )
    def layer_output(after):
        return call(
            partial(down_kernel, slots), scalars, [activated, resid_one, down_b] + down_rel,
            [chip_wide, rows, line] + [pl.BlockSpec(memory_space=pl.ANY)] * BLOCKS,
            jax.ShapeDtypeStruct((tokens, width), BF16), rows, (CHIPS,), [pltpu.VMEM((tokens, width), F32)] + down_rooms,
            after=after,
        )

    if small:
        d_pre, d_attn, down_came = next_round(scalars, [d_pre, d_attn, down_came], [mlp_in_core])
        d_pre_core, d_attn_core = sibling(d_pre), sibling(d_attn)
        far = down_came.shape[0] // 2
        down_one = first_way(add(down_parts[1], down_came[far:]))
        up_parts = weight_grad(
            scalars, 0, [(mlp_in, d_pre, mlp_in_core, d_pre_core), (attended, d_attn, attended_core, d_attn_core)], width
        )
        up_parts[2], down_came, down_one = next_round(scalars, [up_parts[2], down_came, down_one])
        up_came = second_way(up_parts[2])
        down_sum, *down_send = quarters(down_parts[0], down_came, down_one)
        down_z = exchange(down_send)
        wait = (down_came,)
    else:
        up_out_grad = rows_of_all([(mlp_in, d_pre), (attended, d_attn)], width)
        up_grad, out_grad = up_out_grad[:, :hidden], up_out_grad[:, hidden:]
        wait = ()
    chip_col = pl.BlockSpec((tokens, lanes), lambda g, s: (0, s[CHIP_AT + g]))
    d_qkv, sums_qkv = call(
        partial(attention_back_kernel, slots), scalars,
        [d_attn, queries, keys, values, lse, cos_table, sin_table] + first,
        [rows, chip_col, chip_col, chip_col,
         pl.BlockSpec((1, tokens, 128), lambda g, s: (s[CHIP_AT + g], 0, 0)), table, table] + out_specs,
        [jax.ShapeDtypeStruct((3, tokens, width), BF16), jax.ShapeDtypeStruct((8, width), F32)],
        [pl.BlockSpec((3, tokens, lanes), lambda g, s: (0, 0, s[CHIP_AT + g])),
         pl.BlockSpec((8, lanes), lambda g, s: (0, s[CHIP_AT + g]))],
        (groups,), mask_rooms + [pltpu.VMEM((tokens, lanes), F32)] * 3 + [pltpu.VMEM((tokens, lanes), BF16)],
        after=wait,
    )
    if small:
        d_qkv, up_came, *down_z = next_round(scalars, [d_qkv, up_came, *down_z])
        d_qkv_core = sibling(d_qkv)
        up_one = first_way(add(up_parts[1], up_came[per:]))
        down_sum = sum_four(down_sum, down_z)
        down_z = exchange([down_sum] * 3)
    else:
        qkv_grad = rows_of_all([(attn_in, d_qkv)], width)
    input_grad, sums_one = call(
        partial(d_input_kernel, slots), scalars,
        [d_qkv, activations, time_rows, gain_one, d_resid_one] + first,
        [pl.BlockSpec((1, tokens, width), lambda i, s: (i, 0, 0)), anywhere, whole((slots, width)), line, anywhere]
        + piece_specs(per, width, lambda i, s: i),
        [jax.ShapeDtypeStruct((tokens, width), BF16), jax.ShapeDtypeStruct((8, width), F32)],
        [rows, whole((8, width))], (3,),
        [pltpu.VMEM((tokens, width), F32)] * 2
        + [pltpu.VMEM((tokens, width), BF16), pltpu.VMEM((tokens, width), F32), pltpu.SemaphoreType.DMA((2,))],
    )
    if small:
        half = per // 2
        up_sum, up_send = next_round(
            scalars, [], [sums_one],
            [sum_of(up_parts[0], up_came, up_one, row=rows_, rows=half) for rows_ in ((0, half), (half, 0))],
        )
        up_z = swap_z(up_send, 1)
        qkv_parts = weight_grad(scalars, 0, [(attn_in, d_qkv, attn_in_core, d_qkv_core)], width, after=(up_sum,))
        qkv_parts[2], sums_one = next_round(scalars, [qkv_parts[2], sums_one], down_z)
        qkv_came = second_way(qkv_parts[2])
        time_cols = time_features.astype(F32).T
        depth = 64
        v_odd, v_even = call(
            partial(pack_grads_kernel, slots), scalars,
            [sums_one, sums_qkv, sums_two, up_bias_sum, down_bias_sum, time_cols],
            [whole((8, width)), whole((8, width)), whole((8, width)), whole((1, hidden)), line, whole(time_cols.shape)],
            [jax.ShapeDtypeStruct((4, depth, width), BF16)] * 2, [whole((4, depth, width))] * 2, (1,), cost=SOME_COST,
        )
        v_odd, v_even = v_odd.reshape(-1, width), v_even.reshape(-1, width)
        v_odd, up_z, down_sum = next_round(scalars, [v_odd, up_z, down_sum])
        down_grad = in_place(down_sum, down_z)
        up_sum = add(up_sum, up_z)
        up_z = swap_z(up_sum, 2)
        v_came = sibling(v_odd)
        v_came, *to_one = next_round(
            scalars, [v_came], [up_sum],
            [([(qkv_parts[1], row, 0), (qkv_came, per + row, 0)], half, qkv_columns) for row in (0, half)],
        )
        qkv_one = [first_way(x) for x in to_one]
        *qkv_one, v_came = next_round(scalars, [*qkv_one, v_came])
        low, high = [
            add(qkv_parts[0][row : row + half], qkv_came[row : row + half], x) for row, x in zip((0, half), qkv_one)
        ]
        qkv_sum, qkv_send = jnp.where(even_z, low, high), jnp.where(even_z, high, low)
        qkv_z = swap_z(qkv_send, 1)
        (up_z,) = next_round(scalars, [up_z], [qkv_send])
        up_sum = add(up_sum, up_z)
        up_z = swap_z(up_sum, 1)
        part = add(v_even, v_came).reshape(4, depth, width)
        parts = [part[k] for k in range(4)]
        v_came = [first_way(parts[1]), second_way(parts[2]), swap(parts[3], 6, 6)]
        qkv_sum, part = next_round(scalars, [], [], [sum_of(qkv_sum, qkv_z), sum_of(parts[0], *v_came)])
        qkv_z = swap_z(qkv_sum, 2)
        v_came = swap_z(part, 1)
        output = layer_output((part,))
        qkv_z, v_came = next_round(scalars, [qkv_z, v_came], [output, up_z])
        qkv_sum = add(qkv_sum, qkv_z)
        qkv_grad = joined(qkv_sum, swap_z(qkv_sum, 1))
        part = add(part, v_came)
        share = part.astype(F32) + swap_z(part, 2).astype(F32)
        up_out_grad = joined(up_sum, up_z)
        up_grad, out_grad = up_out_grad[:, :hidden], up_out_grad[:, hidden:]
        time_rows_here = time_weight.shape[0]
        time_grad = share[:time_rows_here]
        one, two, ff = width // BLOCKS, 2 * width // BLOCKS, hidden // BLOCKS
        row = share[time_rows_here]
        (gain_one_grad, shift_one_grad, out_bias_grad, gain_two_grad, shift_two_grad, down_bias_grad,
         value_bias_grad) = [row[i * one : (i + 1) * one] for i in range(7)]
        row = share[time_rows_here + 1]
        qk_bias_grad, up_bias_grad = row[:two], row[two : two + ff]
        time_bias_grad = share[time_rows_here + 2, :one]
    else:
        output = layer_output(())
        d_time = sums_one[2 : 2 + slots]
        time_grad = lax.dot_general(
            time_features.astype(F32), d_time, (((0,), (0,)), ((), ())), precision=lax.Precision.HIGHEST
        )
        vector_sums = (
            sums_one[0], sums_one[1], sums_qkv[:2].reshape(-1), sums_qkv[2], sums_two[2], sums_two[0], sums_two[1],
            up_bias_sum[0], down_bias_sum[0], jnp.sum(d_time, axis=0),
        )
        shares = jnp.concatenate(
            [time_grad.reshape(n_fsdp, -1)] + [v.reshape(n_fsdp, -1) for v in vector_sums], axis=1
        )
        sizes = [time_weight.size] + [v.size // n_fsdp for v in vector_sums]
        shares = jnp.pad(shares, ((0, 0), (0, -shares.shape[1] % 4096))).reshape(n_fsdp, -1, 128)
        shares = lax.psum_scatter(shares.astype(BF16), "fsdp", scatter_dimension=0, tiled=False)
        share = lax.psum(shares, "dp").astype(F32).reshape(-1)
        got = []
        at = 0
        for size in sizes:
            got.append(share[at : at + size])
            at += size
        (time_grad, gain_one_grad, shift_one_grad, qk_bias_grad, value_bias_grad, out_bias_grad, gain_two_grad,
         shift_two_grad, up_bias_grad, down_bias_grad, time_bias_grad) = got
    return (
        output, input_grad, gain_one_grad, shift_one_grad, qkv_grad, qk_bias_grad, value_bias_grad, out_grad, out_bias_grad,
        gain_two_grad, shift_two_grad, up_grad, up_bias_grad, down_grad, down_bias_grad,
        time_grad.reshape(time_weight.shape), time_bias_grad,
    )


def solution(mesh):
    tokens = P(("dp", "fsdp"), None)
    vector = P("fsdp")
    matrix = P("fsdp", None)
    in_specs = (
        tokens, tokens, tokens, vector, vector, matrix, vector, matrix, vector, vector, vector, matrix, vector, matrix,
        vector, matrix, vector, tokens,
    )
    out_specs = (
        tokens, tokens, vector, vector, matrix, vector, vector, matrix, vector, vector, vector, matrix, vector, matrix,
        vector, matrix, vector,
    )
    body = partial(per_device, mesh.shape["dp"], mesh.shape["fsdp"])
    return jax.shard_map(body, mesh=mesh, in_specs=in_specs, out_specs=out_specs, check_vma=False)
```
